32 devices in a mesh: groups: 2 (over x), mp: 16 (over z, y, core).
Axes of the slice: x: 2, y: 2, z: 4, core: 2. Of those that a mesh axis runs over, the one named last changes fastest.
Arguments:
- activations: bfloat16 [512, 8192], P(('groups', 'mp')), parts along dimension 0, may hold values from -60 to 60
- gate_weight: bfloat16 [8192, 14336], P(None, 'mp'), may hold values from -0.0625 to 0.0625
- up_weight: bfloat16 [8192, 14336], P(None, 'mp'), may hold values from -0.0625 to 0.0625
- down_weight: bfloat16 [14336, 8192], P('mp'), may hold values from -0.046875 to 0.046875
- norm_gain_vector: bfloat16 [8192], replicated, may hold values from 0.25 to 1.75
- shrink_factors: bfloat16 [16, 8192, 64], P('mp'), may hold values from -0.0625 to 0.0625
- expand_factors: bfloat16 [16, 64, 14336], P(None, None, 'mp'), may hold values from -0.75 to 0.75
- adapter_ranks: int32 [16], replicated, may hold values from 16 to 64, as said below
- adapter_storage_slot: int32 [16], replicated, may hold values from 0 to 15, each once
- segment_start: int32 [64], P('groups'), parts along dimension 0, may hold values from 0 to 255, as said below
- segment_adapter: int32 [64], P('groups'), parts along dimension 0, may hold values from 0 to 15
Outputs:
- block_out: bfloat16 [512, 8192], P(('groups', 'mp')), parts along dimension 0
- normed: bfloat16 [512, 8192], P(('groups', 'mp')), parts along dimension 0
The draws below stay inside these ranges and needn't reach their ends.
There are 2 independent parts, one for each index of `groups`. The reference program is written for one: setup_inputs(seed, part) draws one part's arguments, and reference() takes and returns one part's arrays. A program takes and returns all parts, laid end to end along the dimension named above; an argument that names none is the same for every part. Nothing has to cross between parts.
Inputs may be any that keep to these rules, and one draw needn't show every extreme that they name: `adapter_ranks`: one adapter has rank 64 and one rank 16. `segment_start`: strictly increasing, the first is 0.
All inputs are finite; a program needn't handle non-finite values.
Results may differ from the reference program's by a relative error of at most 0.017.
Values may be sent and summed in bfloat16 or wider, within the bound.
No kernel may reach another device: no remote copies, remote signals or barrier semaphores. Data moves between devices by JAX's collectives and lax.ppermute only.
A program may use at most 128 MiB of HBM per device.

```python
import math
import jax
import jax.numpy as jnp
import numpy as np
from jax import lax

MODEL_WIDTH = 8192
HIDDEN_UNITS = 14336
RANK_LIMIT = 64
RMIN = 16
ROWS = 256
ADAPTER_COUNT = 16
SEGS = 32
N_MP = 16


def draw_activations(key, part):
    key = jax.random.fold_in(key, 3)
    keys = jax.random.split(key, 5)
    row_scale = 0.3 * jnp.exp(jax.random.uniform(keys[0], (ROWS, 1), jnp.float32) * math.log(10.0))
    col_scale = 0.3 * jnp.exp(jax.random.uniform(keys[1], (1, MODEL_WIDTH), jnp.float32) * math.log(10.0))
    base = jnp.clip(jax.random.normal(keys[4], (ROWS, MODEL_WIDTH), jnp.float32), -6.0, 6.0)
    return (base * row_scale * col_scale).astype(jnp.bfloat16)


def draw_adapter_ranks(key, part):
    key = jax.random.fold_in(key, 5)
    keys = jax.random.split(key, 2)
    ranks = jax.random.randint(keys[0], (ADAPTER_COUNT,), RMIN, RANK_LIMIT + 1)
    top = jax.random.randint(keys[1], (), 0, ADAPTER_COUNT)
    index = jnp.arange(ADAPTER_COUNT)
    ranks = jnp.where(index == top, RANK_LIMIT, ranks)
    ranks = jnp.where(index == (top + 1) % ADAPTER_COUNT, RMIN, ranks)
    return ranks.astype(jnp.int32)


def draw_segment_start(key, part):
    key = jax.random.fold_in(key, 7)
    cuts = jax.random.permutation(key, ROWS - 1)[:SEGS - 1] + 1
    starts = jnp.concatenate([jnp.zeros((1,), jnp.int32), jnp.sort(cuts.astype(jnp.int32))])
    return starts.astype(jnp.int32)


def set_ends(result, stream_key, smallest, largest):
    extent = result.shape
    index_at = [jax.random.randint(jax.random.fold_in(stream_key, axis), (), 0, extent[axis]) for axis in range(len(extent))]
    result = result.at[tuple(index_at)].set(smallest)
    longest = extent.index(max(extent))
    index_at[longest] = (index_at[longest] + 1) % extent[longest]
    return result.at[tuple(index_at)].set(largest)


def levels(own_key, dims, pieces, smallest, largest):
    def one(axis_at, shards_of):
        steps = jax.random.uniform(jax.random.fold_in(jax.random.fold_in(own_key, 6), axis_at), (shards_of,), jnp.float32, smallest / len(pieces), largest / len(pieces))
        return jnp.repeat(jnp.exp(steps), dims[axis_at] // shards_of).reshape((-1,) + (1,) * (len(dims) - axis_at - 1))

    loudness = one(*pieces[0])
    for cut in pieces[1:]:
        loudness = loudness * one(*cut)
    return loudness


def rank_table(amount, skew):
    weights = [(1 << 20) // math.isqrt(grade ** skew) + 1 for grade in range(1, amount + 1)]
    deviation = 1 + sum(weights) // (1 << 30)
    return np.cumsum(np.array([max(1, weight // deviation) for weight in weights]))


def ranked(stream_key, shape, count, lean):
    listing = rank_table(count, lean)
    ticket = jax.random.randint(jax.random.fold_in(stream_key, 1), shape, 0, int(listing[count - 1]))
    rank = jnp.searchsorted(jnp.asarray(listing, jnp.int32), ticket, side="right")
    return jax.random.permutation(jax.random.fold_in(stream_key, 2), count)[rank].astype(jnp.int32)


def normal_values(stream_key, dims, width, limit, shards=(), held_as=jnp.bfloat16):
    factor_of = levels(stream_key, dims, shards, -0.22, 0.18) if shards else 1.0
    entries = jax.random.normal(stream_key, dims, jnp.float32) * width * factor_of
    return jnp.minimum(jnp.maximum(entries, -limit), limit).astype(held_as)


def setup_inputs(seed: int = 0, part: int = 0) -> dict:
    splits = jax.random.split(jax.random.key(seed), 12)
    part_splits = jax.random.split(jax.random.fold_in(splits[11], part), 12)
    return {
        "activations": draw_activations(jax.random.fold_in(jax.random.fold_in(splits[11], part), 71), part),
        "gate_weight": normal_values(splits[1], (MODEL_WIDTH, HIDDEN_UNITS), MODEL_WIDTH ** -0.5, 0.0625, ((1, 16),)),
        "up_weight": normal_values(splits[2], (MODEL_WIDTH, HIDDEN_UNITS), MODEL_WIDTH ** -0.5, 0.0625, ((1, 16),)),
        "down_weight": normal_values(splits[3], (HIDDEN_UNITS, MODEL_WIDTH), HIDDEN_UNITS ** -0.5, 0.046875, ((0, 16),)),
        "norm_gain_vector": jnp.clip(1.0 + 0.15 * jax.random.normal(splits[4], (MODEL_WIDTH,), jnp.float32), 0.25, 1.75).astype(jnp.bfloat16),
        "shrink_factors": normal_values(splits[5], (ADAPTER_COUNT, MODEL_WIDTH, RANK_LIMIT), MODEL_WIDTH ** -0.5, 0.0625, ((0, 16),)),
        "expand_factors": normal_values(splits[6], (ADAPTER_COUNT, RANK_LIMIT, HIDDEN_UNITS), RANK_LIMIT ** -0.5, 0.75, ((2, 16),)),
        "adapter_ranks": draw_adapter_ranks(jax.random.fold_in(splits[11], 71), part),
        "adapter_storage_slot": jax.random.permutation(splits[8], ADAPTER_COUNT).astype(jnp.int32),
        "segment_start": draw_segment_start(jax.random.fold_in(jax.random.fold_in(splits[11], part), 71), part),
        "segment_adapter": set_ends(ranked(part_splits[10], (SEGS,), ADAPTER_COUNT, 2), jax.random.fold_in(part_splits[10], 3), 0, ADAPTER_COUNT - 1).astype(jnp.int32),
    }


adapter_alpha = 32.0

def row_tables(segment_start, segment_adapter, adapter_ranks, adapter_storage_slot):
    position = lax.iota(jnp.int32, ROWS)
    segment = lax.optimization_barrier(jnp.sum((segment_start[None, :] <= position[:, None]).astype(jnp.int32), axis=1)) - 1
    seg_hot = (segment[:, None] == lax.iota(jnp.int32, SEGS)[None, :]).astype(jnp.int32)
    row_adapter = lax.optimization_barrier(jnp.sum(seg_hot * segment_adapter[None, :], axis=1)).astype(jnp.int32)
    adapt_hot = (row_adapter[:, None] == lax.iota(jnp.int32, ADAPTER_COUNT)[None, :]).astype(jnp.int32)
    rank_per_row = lax.optimization_barrier(jnp.sum(adapt_hot * adapter_ranks[None, :], axis=1)).astype(jnp.int32)
    row_slot = lax.optimization_barrier(jnp.sum(adapt_hot * adapter_storage_slot[None, :], axis=1)).astype(jnp.int32)
    return (adapt_hot, rank_per_row, row_slot)

def reference(activations, gate_weight, up_weight, down_weight, norm_gain_vector, shrink_factors, expand_factors, adapter_ranks, adapter_storage_slot, segment_start, segment_adapter):
    adapt_hot, rank_per_row, row_slot = row_tables(segment_start, segment_adapter, adapter_ranks, adapter_storage_slot)
    gate = jnp.dot(activations, gate_weight, preferred_element_type=jnp.float32)
    shrink_flattened = jnp.transpose(shrink_factors, (1, 0, 2)).reshape(MODEL_WIDTH, ADAPTER_COUNT * RANK_LIMIT)
    every = jnp.dot(activations, shrink_flattened, preferred_element_type=jnp.float32).reshape(ROWS, ADAPTER_COUNT, RANK_LIMIT)
    slot_hot = (row_slot[:, None] == lax.iota(jnp.int32, ADAPTER_COUNT)[None, :]).astype(jnp.float32)
    shrink = lax.optimization_barrier(jnp.sum(slot_hot[:, :, None] * every, axis=1))
    keep = lax.iota(jnp.int32, RANK_LIMIT)[None, :] < rank_per_row[:, None]
    adapter_scale = adapter_alpha / rank_per_row.astype(jnp.float32)
    coeff = jnp.where(keep, shrink * adapter_scale[:, None], 0.0).astype(jnp.bfloat16)
    spread_rows = (adapt_hot.astype(jnp.bfloat16)[:, :, None] * coeff[:, None, :]).reshape(ROWS, ADAPTER_COUNT * RANK_LIMIT)
    up_output = jnp.dot(activations, up_weight, preferred_element_type=jnp.float32)
    up_output = up_output + jnp.dot(spread_rows, expand_factors.reshape(ADAPTER_COUNT * RANK_LIMIT, HIDDEN_UNITS), preferred_element_type=jnp.float32)
    hidden = (jax.nn.silu(gate) * up_output).astype(jnp.bfloat16)
    hidden_width = HIDDEN_UNITS // N_MP
    hidden_blocks = jnp.transpose(hidden.reshape(ROWS, N_MP, hidden_width), (1, 0, 2))
    down_blocks = down_weight.reshape(N_MP, hidden_width, MODEL_WIDTH)

    def add_block(total, pair):
        term = jnp.dot(pair[0], pair[1], preferred_element_type=jnp.float32).astype(jnp.bfloat16)
        return (total + term.astype(jnp.float32), None)
    total, unused = lax.scan(add_block, jnp.zeros((ROWS, MODEL_WIDTH), jnp.float32), (hidden_blocks, down_blocks))
    stream_sum = activations.astype(jnp.float32) + total
    block_out = stream_sum.astype(jnp.bfloat16)
    scale_rows = lax.rsqrt(lax.optimization_barrier(jnp.mean(stream_sum * stream_sum, axis=1, keepdims=True)) + 1e-05)
    normed = (stream_sum * scale_rows * norm_gain_vector.astype(jnp.float32)[None, :]).astype(jnp.bfloat16)
    return (block_out, normed)
```

```python
import jax
import jax.numpy as jnp
from jax import lax
from jax.sharding import PartitionSpec as P

adapter_alpha = 32.0
AXIS = "mp"
CHUNKS = 2


def ring_shift(size, by):
    far = size // 4
    return [(i, ((i // 4 + by) % far) * 4 + i % 4) for i in range(size)]


def flip(size, bit):
    return [(i, i ^ bit) for i in range(size)]


def gather_rows(own, size):
    far = size // 4
    line = [own] + [lax.ppermute(own, AXIS, ring_shift(size, k)) for k in range(1, far)]
    across = [lax.ppermute(piece, AXIS, flip(size, 2)) for piece in line]
    mine = jnp.concatenate(line + across, axis=0)
    theirs = lax.ppermute(mine, AXIS, flip(size, 1))
    return mine, theirs


def add_bf16(a, b):
    return (a.astype(jnp.float32) + b.astype(jnp.float32)).astype(jnp.bfloat16)


def scatter_rows(mine, theirs, size):
    far = size // 4
    half = mine.shape[0] // 2
    rows = half // far
    chip = add_bf16(mine, lax.ppermute(theirs, AXIS, flip(size, 1)))
    line = add_bf16(chip[:half], lax.ppermute(chip[half:], AXIS, flip(size, 2)))
    total = line[:rows].astype(jnp.float32)
    for k in range(1, far):
        block = lax.slice_in_dim(line, k * rows, (k + 1) * rows, axis=0)
        total = total + lax.ppermute(block, AXIS, ring_shift(size, -k)).astype(jnp.float32)
    return total


def share_shrink(own, size):
    far = size // 4
    half = own.shape[0] // 2
    quarter = half // 2
    rows = quarter // far

    def swap_core(a):
        return jnp.concatenate([a[half:], a[:half]], axis=0)

    def swap_near(a):
        a = a.reshape((2, 2, quarter) + a.shape[1:])
        return jnp.concatenate([a[:, 1:], a[:, :1]], axis=1).reshape(own.shape)

    def roll_far(a, k):
        a = a.reshape(4, far, rows, a.shape[-1])
        return jnp.concatenate([a[:, k:], a[:, :k]], axis=1).reshape(own.shape)

    own = own + swap_core(lax.ppermute(own, AXIS, flip(size, 1)))
    own = own + swap_near(lax.ppermute(own, AXIS, flip(size, 2)))
    k = 1
    while k < far:
        own = own + roll_far(lax.ppermute(own, AXIS, ring_shift(size, -k)), k)
        k *= 2
    return own


def body(
    activations,
    gate_weight,
    up_weight,
    down_weight,
    norm_gain_vector,
    shrink_factors,
    expand_factors,
    adapter_ranks,
    adapter_storage_slot,
    segment_start,
    segment_adapter,
):
    size = lax.axis_size(AXIS)
    me = lax.axis_index(AXIS)
    far = size // 4
    assert far * 4 == size and far & (far - 1) == 0
    own_rows, model_width = activations.shape
    hidden_width = gate_weight.shape[1]
    storage_slots, _, largest_rank = shrink_factors.shape
    adapter_table = expand_factors.shape[0]
    segments = segment_start.shape[0]
    batch_rows = own_rows * size

    row = lax.iota(jnp.int32, batch_rows)
    block = row // own_rows
    holder = (
        (((me >> 2) + far - lax.rem(block, far)) & (far - 1)) * 4
        + (((me >> 1) & 1) ^ (block // far & 1)) * 2
        + ((me & 1) ^ (block // (2 * far)))
    )
    position = holder * own_rows + lax.rem(row, own_rows)
    segment = jnp.sum((segment_start[None, :] <= position[:, None]).astype(jnp.int32), axis=1) - 1
    seg_hot = (segment[:, None] == lax.iota(jnp.int32, segments)[None, :]).astype(jnp.int32)
    row_adapter = jnp.sum(seg_hot * segment_adapter[None, :], axis=1)
    adapt_hot = (row_adapter[:, None] == lax.iota(jnp.int32, adapter_table)[None, :]).astype(
        jnp.int32
    )
    rank_per_row = jnp.sum(adapt_hot * adapter_ranks[None, :], axis=1)
    row_slot = jnp.sum(adapt_hot * adapter_storage_slot[None, :], axis=1) - me * storage_slots

    mine, theirs = gather_rows(activations, size)
    rows = jnp.concatenate([mine, theirs], axis=0)

    own_shrink = jnp.zeros((batch_rows, largest_rank), jnp.float32)
    for slot in range(storage_slots):
        product = jnp.dot(rows, shrink_factors[slot], preferred_element_type=jnp.float32)
        own_shrink = jnp.where((row_slot == slot)[:, None], product, own_shrink)
    shrink = share_shrink(own_shrink.astype(jnp.bfloat16), size).astype(jnp.float32)

    gate = jnp.dot(rows, gate_weight, preferred_element_type=jnp.float32)
    up_output = jnp.dot(rows, up_weight, preferred_element_type=jnp.float32)

    keep = lax.iota(jnp.int32, largest_rank)[None, :] < rank_per_row[:, None]
    adapter_scale = adapter_alpha / rank_per_row.astype(jnp.float32)
    coeff = jnp.where(keep, shrink * adapter_scale[:, None], 0.0).astype(jnp.bfloat16)
    spread_rows = (adapt_hot.astype(jnp.bfloat16)[:, :, None] * coeff[:, None, :]).reshape(
        batch_rows, adapter_table * largest_rank
    )
    up_output = up_output + jnp.dot(
        spread_rows,
        expand_factors.reshape(adapter_table * largest_rank, hidden_width),
        preferred_element_type=jnp.float32,
    )
    hidden = lax.optimization_barrier((jax.nn.silu(gate) * up_output).astype(jnp.bfloat16))

    half = batch_rows // 2
    width = model_width // CHUNKS
    totals = []
    for chunk in range(CHUNKS):
        term = jnp.dot(
            hidden,
            lax.slice_in_dim(down_weight, chunk * width, (chunk + 1) * width, axis=1),
            preferred_element_type=jnp.float32,
        ).astype(jnp.bfloat16)
        totals.append(scatter_rows(term[:half], term[half:], size))
    total = jnp.concatenate(totals, axis=1)

    stream_sum = activations.astype(jnp.float32) + total
    block_out = stream_sum.astype(jnp.bfloat16)
    scale_rows = lax.rsqrt(jnp.mean(stream_sum * stream_sum, axis=1, keepdims=True) + 1e-05)
    normed = (stream_sum * scale_rows * norm_gain_vector.astype(jnp.float32)[None, :]).astype(
        jnp.bfloat16
    )
    return (block_out, normed)


def solution(mesh):
    return jax.shard_map(
        body,
        mesh=mesh,
        in_specs=(
            P(("groups", "mp"), None),
            P(None, "mp"),
            P(None, "mp"),
            P("mp", None),
            P(),
            P("mp", None, None),
            P(None, None, "mp"),
            P(),
            P(),
            P("groups"),
            P("groups"),
        ),
        out_specs=(P(("groups", "mp"), None), P(("groups", "mp"), None)),
        check_vma=False,
    )
```

```python
import functools

import jax
import jax.numpy as jnp
from jax import lax
from jax.experimental import pallas as pl
from jax.experimental.pallas import tpu as pltpu
from jax.sharding import PartitionSpec as P

adapter_alpha = 32.0
AXIS = "mp"
HALVES = 2
VMEM_LIMIT = 32 * 1024 * 1024


def chip_at(place, chips):
    if chips == 8:
        return jnp.where(place < 4, 2 * place, 2 * (7 - place) + 1)
    return place


def place_of(chip, chips):
    if chips == 8:
        return jnp.where((chip & 1) == 0, chip >> 1, 7 - (chip >> 1))
    return chip


def ring(size, by):
    chips = size // 2
    order = [0, 2, 4, 6, 7, 5, 3, 1] if chips == 8 else list(range(chips))
    pairs = []
    for place, chip in enumerate(order):
        to = order[(place + by) % chips]
        pairs += [(2 * chip + core, 2 * to + core) for core in range(2)]
    return pairs


def flip(size, bit):
    return [(i, i ^ bit) for i in range(size)]


def row_positions(me, row, own_rows, size):
    chips = size // 2
    block = row // own_rows
    index = block & (chips - 1)
    step = (index + 1) >> 1
    delta = jnp.where((index & 1) == 1, step, -step)
    place = (place_of(me >> 1, chips) - delta + chips) & (chips - 1)
    core = (me & 1) ^ (block // chips)
    return (2 * chip_at(place, chips) + core) * own_rows + (row & (own_rows - 1))


def pick(index, table):
    hot = index == lax.broadcasted_iota(jnp.int32, (1, table.shape[1]), 1)
    return jnp.sum(jnp.where(hot, table, 0), axis=1, keepdims=True)


def row_adapters(position, start, adapters):
    segment = jnp.sum((start <= position).astype(jnp.int32), axis=1, keepdims=True) - 1
    return pick(segment, adapters)


def whole(space=pltpu.VMEM):
    return pl.BlockSpec(memory_space=space)


def join(right, left):
    rows, width = right[0].shape
    pieces = right + left
    out_rows = rows * len(pieces) // HALVES

    def kernel(*refs):
        out = refs[-1]
        for i, ref in enumerate(refs[:-1]):
            at = (i // HALVES * rows, i % HALVES * width)
            out[at[0] : at[0] + rows, at[1] : at[1] + width] = ref[...]

    return pl.pallas_call(
        kernel,
        out_shape=jax.ShapeDtypeStruct((out_rows, HALVES * width), right[0].dtype),
        in_specs=[whole()] * len(pieces),
        out_specs=whole(),
        compiler_params=pltpu.CompilerParams(vmem_limit_bytes=VMEM_LIMIT),
        name="join_pieces",
    )(*pieces)


def gather_rows(own, size):
    chips = size // 2
    width = own.shape[1] // HALVES
    halves = [own[:, h * width : (h + 1) * width] for h in range(HALVES)]
    right, left = list(halves), list(halves)
    mine = [own]
    theirs = [lax.ppermute(own, AXIS, flip(size, 1))]
    for step in range(1, chips // 2 + 1):
        if step < chips // 2:
            for h in range(HALVES):
                right[h] = lax.ppermute(right[h], AXIS, ring(size, 1))
                left[h] = lax.ppermute(left[h], AXIS, ring(size, -1))
            part = join(right, left)
        else:
            part = join(
                [
                    lax.ppermute(right[0], AXIS, ring(size, 1)),
                    lax.ppermute(left[1], AXIS, ring(size, -1)),
                ],
                [],
            )
        mine.append(part)
        theirs.append(lax.ppermute(part, AXIS, flip(size, 1)))
    return mine + theirs


def shrink_kernel(own_rows, size, steps, count, *refs):
    me_ref, start, adapters, ranks, slots = refs[:5]
    parts = refs[5 : 5 + count]
    factor, rows_out, coeff_out, total = refs[5 + count :]
    k = pl.program_id(0)
    at = 0
    for part in parts:
        rows_out[at : at + part.shape[0], :] = part[...]
        at += part.shape[0]

    @pl.when(k == 0)
    def _():
        total[...] = jnp.zeros_like(total)

    total[...] += lax.dot_general(
        rows_out[...], factor[...], (((1,), (1,)), ((), ())), preferred_element_type=jnp.float32
    )

    @pl.when(k == steps - 1)
    def _():
        me = me_ref[0]
        batch_rows = total.shape[0]
        rank_limit = coeff_out.shape[1]
        held = total.shape[1] // rank_limit
        row = lax.broadcasted_iota(jnp.int32, (batch_rows, 1), 0)
        adapter = row_adapters(row_positions(me, row, own_rows, size), start[...], adapters[...])
        rank = pick(adapter, ranks[...])
        slot = pick(adapter, slots[...]) - me * held
        shrink = jnp.zeros((batch_rows, rank_limit), jnp.float32)
        for s in range(held):
            shrink = jnp.where(
                slot == s, total[:, s * rank_limit : (s + 1) * rank_limit], shrink
            )
        keep = lax.broadcasted_iota(jnp.int32, (1, rank_limit), 1) < rank
        coeff = jnp.where(keep, shrink * (adapter_alpha / rank.astype(jnp.float32)), 0.0)
        column = lax.broadcasted_iota(jnp.int32, (1, batch_rows), 1)
        place = row_positions(me, column, own_rows, size)
        to_place = (place == row).astype(jnp.bfloat16)
        coeff_out[...] = jnp.dot(
            to_place, coeff.astype(jnp.bfloat16), preferred_element_type=jnp.float32
        ).astype(jnp.bfloat16)


def shrink_rows(parts, shrink_factors, tables, me, own_rows, size):
    slots, model_width, rank_limit = shrink_factors.shape
    factor = jnp.swapaxes(shrink_factors, 1, 2).reshape(slots * rank_limit, model_width)
    steps = 8
    width = model_width // steps
    batch_rows = own_rows * size

    def columns(rows):
        return pl.BlockSpec((rows, width), lambda k: (0, k))

    return pl.pallas_call(
        functools.partial(shrink_kernel, own_rows, size, steps, len(parts)),
        out_shape=(
            jax.ShapeDtypeStruct((batch_rows, model_width), jnp.bfloat16),
            jax.ShapeDtypeStruct((batch_rows, rank_limit), jnp.bfloat16),
        ),
        grid=(steps,),
        in_specs=[whole(pltpu.SMEM)]
        + [pl.BlockSpec(table.shape, lambda k: (0, 0)) for table in tables]
        + [columns(part.shape[0]) for part in parts]
        + [columns(slots * rank_limit)],
        out_specs=(columns(batch_rows), pl.BlockSpec((batch_rows, rank_limit), lambda k: (0, 0))),
        scratch_shapes=[pltpu.VMEM((batch_rows, slots * rank_limit), jnp.float32)],
        compiler_params=pltpu.CompilerParams(vmem_limit_bytes=VMEM_LIMIT),
        cost_estimate=pl.CostEstimate(
            flops=2 * batch_rows * model_width * slots * rank_limit,
            bytes_accessed=4 * batch_rows * model_width,
            transcendentals=0,
        ),
        name="shrink_rows",
    )(me, *tables, *parts, factor)


def matmul_kernel(rows, weight, out):
    @pl.when(pl.program_id(0) == 0)
    def _():
        out[...] = jnp.zeros_like(out)

    out[...] += jnp.dot(rows[...], weight[...], preferred_element_type=jnp.float32)


def matmul(rows, weight, name):
    batch_rows, depth = rows.shape
    width = weight.shape[1]
    steps = 8
    return pl.pallas_call(
        matmul_kernel,
        out_shape=jax.ShapeDtypeStruct((batch_rows, width), jnp.float32),
        grid=(steps,),
        in_specs=[
            pl.BlockSpec((batch_rows, depth // steps), lambda k: (0, k)),
            pl.BlockSpec((depth // steps, width), lambda k: (k, 0)),
        ],
        out_specs=pl.BlockSpec((batch_rows, width), lambda k: (0, 0)),
        compiler_params=pltpu.CompilerParams(vmem_limit_bytes=VMEM_LIMIT),
        cost_estimate=pl.CostEstimate(
            flops=2 * batch_rows * depth * width,
            bytes_accessed=2 * depth * width,
            transcendentals=0,
        ),
        name=name,
    )(rows, weight)


def hidden_kernel(
    own_rows, size, me_ref, start, adapters, coeff, expand, gate, up, out, spread
):
    me = me_ref[0]
    batch_rows, rank_limit = coeff.shape
    row = lax.broadcasted_iota(jnp.int32, (batch_rows, 1), 0)
    position = row_positions(me, row, own_rows, size)
    adapter = row_adapters(position, start[...], adapters[...])
    from_place = position == lax.broadcasted_iota(jnp.int32, (1, batch_rows), 1)
    own = jnp.dot(
        from_place.astype(jnp.bfloat16), coeff[...], preferred_element_type=jnp.float32
    )
    pair = jnp.concatenate([own, own], axis=1)
    second = lax.broadcasted_iota(jnp.int32, (1, 2 * rank_limit), 1) // rank_limit
    for p in range(spread.shape[1] // (2 * rank_limit)):
        spread[:, p * 2 * rank_limit : (p + 1) * 2 * rank_limit] = jnp.where(
            adapter == second + 2 * p, pair, 0.0
        ).astype(jnp.bfloat16)
    lora = jnp.dot(spread[...], expand[...], preferred_element_type=jnp.float32)
    value = gate[...]
    out[...] = (value / (1.0 + jnp.exp(-value)) * (up[...] + lora)).astype(jnp.bfloat16)


def hidden_rows(gate, up, coeff, expand_factors, tables, me, own_rows, size):
    adapters, rank_limit, width = expand_factors.shape
    batch_rows = gate.shape[0]
    return pl.pallas_call(
        functools.partial(hidden_kernel, own_rows, size),
        out_shape=jax.ShapeDtypeStruct((batch_rows, width), jnp.bfloat16),
        in_specs=[whole(pltpu.SMEM)] + [whole()] * 6,
        out_specs=whole(),
        scratch_shapes=[pltpu.VMEM((batch_rows, adapters * rank_limit), jnp.bfloat16)],
        compiler_params=pltpu.CompilerParams(vmem_limit_bytes=VMEM_LIMIT),
        cost_estimate=pl.CostEstimate(
            flops=2 * batch_rows * adapters * rank_limit * width,
            bytes_accessed=2 * adapters * rank_limit * width,
            transcendentals=batch_rows * width,
        ),
        name="hidden_rows",
    )(
        me,
        *tables,
        coeff,
        expand_factors.reshape(adapters * rank_limit, width),
        gate,
        up,
    )


def scatter_rows(terms, own_rows, size):
    chips = size // 2
    core_rows = own_rows * chips
    received = [lax.ppermute(term[core_rows:], AXIS, flip(size, 1)) for term in terms]

    def block(h, index):
        rows = slice(index * own_rows, (index + 1) * own_rows)
        return terms[h][rows].astype(jnp.float32) + received[h][rows].astype(jnp.float32)

    def send(value, by):
        return lax.ppermute(value.astype(jnp.bfloat16), AXIS, ring(size, by)).astype(jnp.float32)

    right, left = [None] * HALVES, [None] * HALVES
    opposite = chips - 1
    right[0] = send(block(0, opposite), 1)
    left[1] = send(block(1, opposite), -1)
    for step in range(chips // 2 - 1, 0, -1):
        for h in range(HALVES):
            value = block(h, 2 * step)
            right[h] = send(value if right[h] is None else value + right[h], 1)
            value = block(h, 2 * step - 1)
            left[h] = send(value if left[h] is None else value + left[h], -1)
    return [block(h, 0) + right[h] + left[h] for h in range(HALVES)]


def body(
    activations,
    gate_weight,
    up_weight,
    down_weight,
    norm_gain_vector,
    shrink_factors,
    expand_factors,
    adapter_ranks,
    adapter_storage_slot,
    segment_start,
    segment_adapter,
):
    size = lax.axis_size(AXIS)
    me = lax.axis_index(AXIS).astype(jnp.int32).reshape(1)
    own_rows, model_width = activations.shape
    assert size & (size - 1) == 0 and own_rows & (own_rows - 1) == 0
    rows_tables = (segment_start[None], segment_adapter[None])
    all_tables = rows_tables + (adapter_ranks[None], adapter_storage_slot[None])

    parts = gather_rows(activations, size)
    rows, coeff = shrink_rows(parts, shrink_factors, all_tables, me, own_rows, size)

    bit = 1
    while bit < size:
        coeff = coeff + lax.ppermute(coeff, AXIS, flip(size, bit))
        bit *= 2
    gate = matmul(rows, gate_weight, "gate_rows")
    up = matmul(rows, up_weight, "up_rows")
    hidden = hidden_rows(gate, up, coeff, expand_factors, rows_tables, me, own_rows, size)

    width = model_width // HALVES
    terms = [
        jnp.dot(
            hidden,
            down_weight[:, h * width : (h + 1) * width],
            preferred_element_type=jnp.float32,
        ).astype(jnp.bfloat16)
        for h in range(HALVES)
    ]
    total = jnp.concatenate(scatter_rows(terms, own_rows, size), axis=1)

    stream_sum = activations.astype(jnp.float32) + total
    block_out = stream_sum.astype(jnp.bfloat16)
    scale_rows = lax.rsqrt(jnp.mean(stream_sum * stream_sum, axis=1, keepdims=True) + 1e-05)
    normed = (stream_sum * scale_rows * norm_gain_vector.astype(jnp.float32)[None, :]).astype(
        jnp.bfloat16
    )
    return (block_out, normed)


def solution(mesh):
    return jax.shard_map(
        body,
        mesh=mesh,
        in_specs=(
            P(("groups", "mp"), None),
            P(None, "mp"),
            P(None, "mp"),
            P("mp", None),
            P(),
            P("mp", None, None),
            P(None, None, "mp"),
            P(),
            P(),
            P("groups"),
            P("groups"),
        ),
        out_specs=(P(("groups", "mp"), None), P(("groups", "mp"), None)),
        check_vma=False,
    )
```

```python
import functools

import jax
import jax.numpy as jnp
from jax import lax
from jax.experimental import pallas as pl
from jax.experimental.pallas import tpu as pltpu
from jax.sharding import PartitionSpec as P

adapter_alpha = 32.0
AXIS = "mp"
HALVES = 2
DEPTH_BLOCKS = 8
VMEM_LIMIT = 16 * 1024 * 1024
STREAM_LIMIT = 48 * 1024 * 1024


def chip_at(place, chips):
    if chips == 8:
        return jnp.where(place < 4, 2 * place, 2 * (7 - place) + 1)
    return place


def place_of(chip, chips):
    if chips == 8:
        return jnp.where((chip & 1) == 0, chip >> 1, 7 - (chip >> 1))
    return chip


def ring(size, by):
    chips = size // 2
    order = [0, 2, 4, 6, 7, 5, 3, 1] if chips == 8 else list(range(chips))
    pairs = []
    for place, chip in enumerate(order):
        to = order[(place + by) % chips]
        pairs += [(2 * chip + core, 2 * to + core) for core in range(2)]
    return pairs


def flip(size, bit):
    return [(i, i ^ bit) for i in range(size)]


def row_positions(me, row, own_rows, size):
    chips = size // 2
    block = row // own_rows
    index = block & (chips - 1)
    step = (index + 1) >> 1
    delta = jnp.where((index & 1) == 1, step, -step)
    place = (place_of(me >> 1, chips) - delta + chips) & (chips - 1)
    core = (me & 1) ^ (block // chips)
    return (2 * chip_at(place, chips) + core) * own_rows + (row & (own_rows - 1))


def pick(index, table):
    hot = index == lax.broadcasted_iota(jnp.int32, (1, table.shape[1]), 1)
    return jnp.sum(jnp.where(hot, table, 0), axis=1, keepdims=True)


def row_adapters(position, start, adapters):
    segment = jnp.sum((start <= position).astype(jnp.int32), axis=1, keepdims=True) - 1
    return pick(segment, adapters)


def whole(space=pltpu.VMEM):
    return pl.BlockSpec(memory_space=space)


def call(kernel, out_shape, operands, name, ordered=(), limit=VMEM_LIMIT, **options):
    count = len(operands)

    def run(*refs):
        kernel(*refs[:count], *refs[count + len(ordered) :])

    return pl.pallas_call(
        run,
        out_shape=out_shape,
        in_specs=[
            whole(pltpu.SMEM if operand.ndim == 1 else pltpu.VMEM) for operand in operands
        ]
        + [whole(pl.ANY)] * len(ordered),
        out_specs=jax.tree.map(lambda _: whole(), out_shape),
        compiler_params=pltpu.CompilerParams(vmem_limit_bytes=limit),
        name=name,
        **options,
    )(*operands, *ordered)


def split_columns(array):
    rows, columns = array.shape
    width = columns // HALVES
    half = jax.ShapeDtypeStruct((rows, width), array.dtype)

    def kernel(ref, *outs):
        for h, out in enumerate(outs):
            out[...] = ref[:, h * width : (h + 1) * width]

    return call(kernel, (half,) * HALVES, [array], "split_columns")


def join(pieces, ordered=()):
    rows, width = pieces[0].shape

    def kernel(*refs):
        out = refs[-1]
        for i, ref in enumerate(refs[:-1]):
            top, left = i // HALVES * rows, i % HALVES * width
            out[top : top + rows, left : left + width] = ref[...]

    shape = (rows * len(pieces) // HALVES, HALVES * width)
    return call(
        kernel, jax.ShapeDtypeStruct(shape, pieces[0].dtype), pieces, "join_pieces", ordered
    )


def gather_rows(own, size):
    chips = size // 2
    last = chips // 2
    other = lax.ppermute(own, AXIS, flip(size, 1))
    halves = split_columns(own)
    right, left = list(halves), list(halves)
    pieces = []
    mine, theirs = [own], [other]
    for step in range(1, last + 1):
        if step < last:
            right[0] = lax.ppermute(right[0], AXIS, ring(size, 1))
            left[1] = lax.ppermute(left[1], AXIS, ring(size, -1))
            right[1] = lax.ppermute(right[1], AXIS, ring(size, 1))
            left[0] = lax.ppermute(left[0], AXIS, ring(size, -1))
            pieces += right + left
        else:
            pieces.append(lax.ppermute(right[0], AXIS, ring(size, 1)))
            pieces.append(lax.ppermute(left[1], AXIS, ring(size, -1)))
        if step == last - 2 or step == last:
            part = join(pieces, [other] if step < last else [])
            pieces = []
            mine.append(part)
            theirs.append(lax.ppermute(part, AXIS, flip(size, 1)))
    return mine + theirs


def shrink_kernel(own_rows, size, count, *refs):
    me_ref, start, adapters, ranks, slots = refs[:5]
    parts = refs[5 : 5 + count]
    factor, rows_out, coeff_out, total = refs[5 + count :]
    batch_rows, model_width = rows_out.shape
    width = model_width // 8

    def columns(k, _):
        at = pl.ds(pl.multiple_of(k * width, width), width)
        top = 0
        for part in parts:
            rows_out[top : top + part.shape[0], at] = part[:, at]
            top += part.shape[0]
        product = lax.dot_general(
            rows_out[:, at],
            factor[:, at],
            (((1,), (1,)), ((), ())),
            preferred_element_type=jnp.float32,
        )
        total[...] = jnp.where(k == 0, product, total[...] + product)
        return 0

    lax.fori_loop(0, model_width // width, columns, 0)

    me = me_ref[0]
    rank_limit = coeff_out.shape[1]
    held = total.shape[1] // rank_limit
    row = lax.broadcasted_iota(jnp.int32, (batch_rows, 1), 0)
    adapter = row_adapters(row_positions(me, row, own_rows, size), start[...], adapters[...])
    rank = pick(adapter, ranks[...])
    slot = pick(adapter, slots[...]) - me * held
    shrink = jnp.zeros((batch_rows, rank_limit), jnp.float32)
    for s in range(held):
        shrink = jnp.where(slot == s, total[:, s * rank_limit : (s + 1) * rank_limit], shrink)
    keep = lax.broadcasted_iota(jnp.int32, (1, rank_limit), 1) < rank
    coeff = jnp.where(keep, shrink * (adapter_alpha / rank.astype(jnp.float32)), 0.0)
    column = lax.broadcasted_iota(jnp.int32, (1, batch_rows), 1)
    place = row_positions(me, column, own_rows, size)
    to_place = (place == row).astype(jnp.bfloat16)
    coeff_out[...] = jnp.dot(
        to_place, coeff.astype(jnp.bfloat16), preferred_element_type=jnp.float32
    ).astype(jnp.bfloat16)


def shrink_rows(parts, shrink_factors, tables, me, own_rows, size):
    slots, model_width, rank_limit = shrink_factors.shape
    factor = jnp.swapaxes(shrink_factors, 1, 2).reshape(slots * rank_limit, model_width)
    batch_rows = own_rows * size
    return call(
        functools.partial(shrink_kernel, own_rows, size, len(parts)),
        (
            jax.ShapeDtypeStruct((batch_rows, model_width), jnp.bfloat16),
            jax.ShapeDtypeStruct((batch_rows, rank_limit), jnp.bfloat16),
        ),
        [me, *tables, *parts, factor],
        "shrink_rows",
        scratch_shapes=[pltpu.VMEM((batch_rows, slots * rank_limit), jnp.float32)],
        cost_estimate=pl.CostEstimate(
            flops=2 * batch_rows * model_width * slots * rank_limit,
            bytes_accessed=4 * batch_rows * model_width,
            transcendentals=0,
        ),
    )


def add_coefficients(a, b, ordered):
    def kernel(a_ref, b_ref, out):
        out[...] = a_ref[...] + b_ref[...]

    return call(
        kernel, jax.ShapeDtypeStruct(a.shape, a.dtype), [a, b], "add_coefficients", ordered
    )


def matmul(rows, weight, name, first, last, ordered=()):
    batch_rows, depth = rows.shape
    width = weight.shape[1]
    block = depth // DEPTH_BLOCKS

    def kernel(rows_ref, weight_ref, *rest):
        out = rest[-1]
        k = pl.program_id(0)
        at = pl.ds(pl.multiple_of((k + first) * block, block), block)
        product = jnp.dot(rows_ref[:, at], weight_ref[...], preferred_element_type=jnp.float32)

        @pl.when(k == 0)
        def _():
            out[...] = product

        @pl.when(k > 0)
        def _():
            out[...] += product

    return pl.pallas_call(
        kernel,
        out_shape=jax.ShapeDtypeStruct((batch_rows, width), jnp.float32),
        grid=(last - first,),
        in_specs=[whole(), pl.BlockSpec((block, width), lambda k: (k + first, 0))]
        + [whole(pl.ANY)] * len(ordered),
        out_specs=pl.BlockSpec((batch_rows, width), lambda k: (0, 0)),
        compiler_params=pltpu.CompilerParams(vmem_limit_bytes=STREAM_LIMIT),
        cost_estimate=pl.CostEstimate(
            flops=2 * batch_rows * (last - first) * block * width,
            bytes_accessed=2 * (last - first) * block * width,
            transcendentals=0,
        ),
        name=name,
    )(rows, weight, *ordered)


def hidden_kernel(
    own_rows, size, me_ref, start, adapters, coeff, recv, expand, gate, up, more, out, spread
):
    me = me_ref[0]
    batch_rows, rank_limit = coeff.shape
    row = lax.broadcasted_iota(jnp.int32, (batch_rows, 1), 0)
    position = row_positions(me, row, own_rows, size)
    adapter = row_adapters(position, start[...], adapters[...])
    from_place = position == lax.broadcasted_iota(jnp.int32, (1, batch_rows), 1)
    own = jnp.dot(
        from_place.astype(jnp.bfloat16),
        coeff[...] + recv[...],
        preferred_element_type=jnp.float32,
    )
    pair = jnp.concatenate([own, own], axis=1)
    second = lax.broadcasted_iota(jnp.int32, (1, 2 * rank_limit), 1) // rank_limit
    for p in range(spread.shape[1] // (2 * rank_limit)):
        spread[:, p * 2 * rank_limit : (p + 1) * 2 * rank_limit] = jnp.where(
            adapter == second + 2 * p, pair, 0.0
        ).astype(jnp.bfloat16)
    lora = jnp.dot(spread[...], expand[...], preferred_element_type=jnp.float32)
    value = gate[...]
    total = up[...] + more[...] + lora
    out[...] = (value / (1.0 + jnp.exp(-value)) * total).astype(jnp.bfloat16)


def hidden_rows(gate, up, more, coeff, recv, expand_factors, tables, me, own_rows, size):
    adapters, rank_limit, width = expand_factors.shape
    batch_rows = gate.shape[0]
    return call(
        functools.partial(hidden_kernel, own_rows, size),
        jax.ShapeDtypeStruct((batch_rows, width), jnp.bfloat16),
        [
            me,
            *tables,
            coeff,
            recv,
            expand_factors.reshape(adapters * rank_limit, width),
            gate,
            up,
            more,
        ],
        "hidden_rows",
        scratch_shapes=[pltpu.VMEM((batch_rows, adapters * rank_limit), jnp.bfloat16)],
        cost_estimate=pl.CostEstimate(
            flops=2 * batch_rows * adapters * rank_limit * width,
            bytes_accessed=2 * adapters * rank_limit * width,
            transcendentals=batch_rows * width,
        ),
    )


def down_rows(hidden, down_weight, half, ordered=()):
    batch_rows, hidden_width = hidden.shape
    width = down_weight.shape[1] // HALVES
    steps = 8
    block = width // steps
    core_rows = batch_rows // 2

    def kernel(hidden_ref, weight, *rest):
        mine, theirs = rest[-2:]
        product = jnp.dot(
            hidden_ref[...], weight[...], preferred_element_type=jnp.float32
        ).astype(jnp.bfloat16)
        theirs[...] = product[core_rows:]
        mine[...] = product[:core_rows]

    part = jax.ShapeDtypeStruct((core_rows, width), jnp.bfloat16)
    return pl.pallas_call(
        kernel,
        out_shape=(part, part),
        grid=(steps,),
        in_specs=[
            whole(),
            pl.BlockSpec((hidden_width, block), lambda n: (0, n + half * steps)),
        ]
        + [whole(pl.ANY)] * len(ordered),
        out_specs=[pl.BlockSpec((core_rows, block), lambda n: (0, n))] * 2,
        compiler_params=pltpu.CompilerParams(vmem_limit_bytes=STREAM_LIMIT),
        cost_estimate=pl.CostEstimate(
            flops=2 * batch_rows * hidden_width * width,
            bytes_accessed=2 * hidden_width * width,
            transcendentals=0,
        ),
        name="down_rows",
    )(hidden, down_weight, *ordered)


def add_blocks(sides, own_rows, ordered):
    operands, shapes = [], []
    for mine, theirs, _, arrived in sides:
        operands += [mine, theirs] + ([] if arrived is None else [arrived])
        shapes.append(jax.ShapeDtypeStruct((own_rows, mine.shape[1]), jnp.bfloat16))

    def kernel(*refs):
        refs = list(refs)
        outs = refs[-len(sides) :]
        for (_, _, index, arrived), out in zip(sides, outs):
            at = slice(index * own_rows, (index + 1) * own_rows)
            total = refs.pop(0)[at, :].astype(jnp.float32)
            total = total + refs.pop(0)[at, :].astype(jnp.float32)
            if arrived is not None:
                total = total + refs.pop(0)[...].astype(jnp.float32)
            out[...] = total.astype(jnp.bfloat16)

    return call(kernel, tuple(shapes), operands, "add_blocks", ordered)


def scatter_rows(mine, theirs, own_rows, size):
    chips = size // 2
    last = chips // 2
    right, left = [None] * HALVES, [None] * HALVES
    ordered = []
    for step in range(last, 0, -1):
        for r in range(HALVES):
            if step == last and r == 1:
                continue
            l = 1 - r
            if step == last:
                at_right = at_left = chips - 1
            else:
                at_right, at_left = 2 * step, 2 * step - 1
            sums = add_blocks(
                [
                    (mine[r], theirs[r], at_right, right[r]),
                    (mine[l], theirs[l], at_left, left[l]),
                ],
                own_rows,
                ordered,
            )
            ordered = [sums[0]]
            right[r] = lax.ppermute(sums[0], AXIS, ring(size, 1))
            left[l] = lax.ppermute(sums[1], AXIS, ring(size, -1))
    return list(zip(mine, theirs, right, left))


def finish_rows(halves, activations, gain, own_rows):
    width = activations.shape[1] // HALVES

    def kernel(*refs):
        refs, (act, gain_ref, block_out, normed, stream) = refs[:-5], refs[-5:]
        square = jnp.zeros((own_rows, 1), jnp.float32)
        for h in range(HALVES):
            mine, theirs, right, left = refs[4 * h : 4 * h + 4]
            at = slice(h * width, (h + 1) * width)
            total = act[:, at].astype(jnp.float32)
            for ref in (mine, theirs):
                total = total + ref[:own_rows, :].astype(jnp.float32)
            for ref in (right, left):
                total = total + ref[...].astype(jnp.float32)
            stream[:, at] = total
            block_out[:, at] = total.astype(jnp.bfloat16)
            square = square + jnp.sum(total * total, axis=1, keepdims=True)
        scale = lax.rsqrt(square * (1.0 / act.shape[1]) + 1e-05)
        normed[...] = (stream[...] * scale * gain_ref[...].astype(jnp.float32)).astype(
            jnp.bfloat16
        )

    out = jax.ShapeDtypeStruct(activations.shape, jnp.bfloat16)
    return call(
        kernel,
        (out, out),
        [array for half in halves for array in half] + [activations, gain],
        "finish_rows",
        scratch_shapes=[pltpu.VMEM(activations.shape, jnp.float32)],
    )


def body(
    activations,
    gate_weight,
    up_weight,
    down_weight,
    norm_gain_vector,
    shrink_factors,
    expand_factors,
    adapter_ranks,
    adapter_storage_slot,
    segment_start,
    segment_adapter,
):
    size = lax.axis_size(AXIS)
    me = lax.axis_index(AXIS).astype(jnp.int32).reshape(1)
    own_rows, model_width = activations.shape
    assert size & (size - 1) == 0 and own_rows & (own_rows - 1) == 0
    rows_tables = (segment_start[None], segment_adapter[None])
    all_tables = rows_tables + (adapter_ranks[None], adapter_storage_slot[None])

    parts = gather_rows(activations, size)
    rows, coeff = shrink_rows(parts, shrink_factors, all_tables, me, own_rows, size)

    bits = [1 << b for b in range(size.bit_length() - 1)]
    work = []
    for bit in bits[:-1]:
        received = lax.ppermute(coeff, AXIS, flip(size, bit))
        if bit == bits[1]:
            work = [matmul(rows, gate_weight, "gate_rows", 0, DEPTH_BLOCKS, [coeff])]
            gate = work[0]
        if bit == bits[2]:
            work = [matmul(rows, up_weight, "up_rows", 0, DEPTH_BLOCKS // 2, [coeff])]
            up = work[0]
        coeff = add_coefficients(coeff, received, work)
    received = lax.ppermute(coeff, AXIS, flip(size, bits[-1]))
    more = matmul(rows, up_weight, "up_rows", DEPTH_BLOCKS // 2, DEPTH_BLOCKS, [coeff])
    hidden = hidden_rows(
        gate, up, more, coeff, received, expand_factors, rows_tables, me, own_rows, size
    )

    mine, theirs = [None] * HALVES, [None] * HALVES
    ordered = []
    for h in range(HALVES):
        mine[h], part = down_rows(hidden, down_weight, h, ordered)
        ordered = [part]
        theirs[h] = lax.ppermute(part, AXIS, flip(size, 1))
    halves = scatter_rows(mine, theirs, own_rows, size)
    return finish_rows(halves, activations, norm_gain_vector[None], own_rows)


def solution(mesh):
    return jax.shard_map(
        body,
        mesh=mesh,
        in_specs=(
            P(("groups", "mp"), None),
            P(None, "mp"),
            P(None, "mp"),
            P("mp", None),
            P(),
            P("mp", None, None),
            P(None, None, "mp"),
            P(),
            P(),
            P("groups"),
            P("groups"),
        ),
        out_specs=(P(("groups", "mp"), None), P(("groups", "mp"), None)),
        check_vma=False,
    )
```

```python
import functools

import jax
import jax.numpy as jnp
from jax import lax
from jax.experimental import pallas as pl
from jax.experimental.pallas import tpu as pltpu
from jax.sharding import PartitionSpec as P

adapter_alpha = 32.0
AXIS = "mp"
HALVES = 2
DEPTH_BLOCK = 512
WIDTH_BLOCK = 512
IN_FLIGHT = 4
VMEM_LIMIT = 16 * 1024 * 1024
STREAM_LIMIT = 46 * 1024 * 1024


def chip_at(place, chips):
    if chips == 8:
        return jnp.where(place < 4, 2 * place, 2 * (7 - place) + 1)
    return place


def place_of(chip, chips):
    if chips == 8:
        return jnp.where((chip & 1) == 0, chip >> 1, 7 - (chip >> 1))
    return chip


def ring(size, by):
    chips = size // 2
    order = [0, 2, 4, 6, 7, 5, 3, 1] if chips == 8 else list(range(chips))
    pairs = []
    for place, chip in enumerate(order):
        to = order[(place + by) % chips]
        pairs += [(2 * chip + core, 2 * to + core) for core in range(2)]
    return pairs


def flip(size, bit):
    return [(i, i ^ bit) for i in range(size)]


def row_positions(me, row, own_rows, size):
    chips = size // 2
    block = row // own_rows
    index = block & (chips - 1)
    step = (index + 1) >> 1
    delta = jnp.where((index & 1) == 1, step, -step)
    place = (place_of(me >> 1, chips) - delta + chips) & (chips - 1)
    core = (me & 1) ^ (block // chips)
    return (2 * chip_at(place, chips) + core) * own_rows + (row & (own_rows - 1))


def pick(index, table):
    hot = index == lax.broadcasted_iota(jnp.int32, (1, table.shape[1]), 1)
    return jnp.sum(jnp.where(hot, table, 0), axis=1, keepdims=True)


def row_adapters(position, start, adapters):
    segment = jnp.sum((start <= position).astype(jnp.int32), axis=1, keepdims=True) - 1
    return pick(segment, adapters)


def whole(space=pltpu.VMEM):
    return pl.BlockSpec(memory_space=space)


def call(kernel, out_shape, operands, name, ordered=(), limit=VMEM_LIMIT, **options):
    count = len(operands)

    def run(*refs):
        kernel(*refs[:count], *refs[count + len(ordered) :])

    return pl.pallas_call(
        run,
        out_shape=out_shape,
        in_specs=[
            whole(pltpu.SMEM if operand.ndim == 1 else pltpu.VMEM) for operand in operands
        ]
        + [whole(pl.ANY)] * len(ordered),
        out_specs=jax.tree.map(lambda _: whole(), out_shape),
        compiler_params=pltpu.CompilerParams(vmem_limit_bytes=limit),
        name=name,
        **options,
    )(*operands, *ordered)


def split_columns(array):
    rows, columns = array.shape
    width = columns // HALVES
    half = jax.ShapeDtypeStruct((rows, width), array.dtype)

    def kernel(ref, *outs):
        for h, out in enumerate(outs):
            out[...] = ref[:, h * width : (h + 1) * width]

    return call(kernel, (half,) * HALVES, [array], "split_columns")


def join(pieces, ordered=()):
    rows, width = pieces[0].shape

    def kernel(*refs):
        out = refs[-1]
        for i, ref in enumerate(refs[:-1]):
            top, left = i // HALVES * rows, i % HALVES * width
            out[top : top + rows, left : left + width] = ref[...]

    shape = (rows * len(pieces) // HALVES, HALVES * width)
    return call(
        kernel, jax.ShapeDtypeStruct(shape, pieces[0].dtype), pieces, "join_pieces", ordered
    )


def gather_rows(own, size, ordered):
    chips = size // 2
    last = chips // 2
    other = lax.ppermute(own, AXIS, flip(size, 1))
    halves = split_columns(own)
    right, left = list(halves), list(halves)
    pieces = []
    mine, theirs = [own], [other]
    for step in range(1, last + 1):
        if step < last:
            right[0] = lax.ppermute(right[0], AXIS, ring(size, 1))
            left[1] = lax.ppermute(left[1], AXIS, ring(size, -1))
            right[1] = lax.ppermute(right[1], AXIS, ring(size, 1))
            left[0] = lax.ppermute(left[0], AXIS, ring(size, -1))
            pieces += right + left
        else:
            pieces.append(lax.ppermute(right[0], AXIS, ring(size, 1)))
            pieces.append(lax.ppermute(left[1], AXIS, ring(size, -1)))
        if step >= last - 1:
            part = join(pieces, ordered if step < last else [])
            pieces = []
            mine.append(part)
            theirs.append(lax.ppermute(part, AXIS, flip(size, 1)))
    return mine + theirs


def row_masks(me, tables, own_rows, size, slots, rank_limit):
    batch_rows = own_rows * size
    adapters = tables[2].shape[1]

    def kernel(me_ref, start, segment_adapter, ranks, slot_of, scale, to_place, from_place, hot):
        me = me_ref[0]
        row = lax.broadcasted_iota(jnp.int32, (batch_rows, 1), 0)
        column = lax.broadcasted_iota(jnp.int32, (1, batch_rows), 1)
        position = row_positions(me, row, own_rows, size)
        adapter = row_adapters(position, start[...], segment_adapter[...])
        rank = pick(adapter, ranks[...])
        slot = pick(adapter, slot_of[...]) - me * slots
        at = lax.broadcasted_iota(jnp.int32, (1, slots * rank_limit), 1)
        keep = (at // rank_limit == slot) & (at % rank_limit < rank)
        scale[...] = jnp.where(keep, adapter_alpha / rank.astype(jnp.float32), 0.0)
        to_place[...] = (row_positions(me, column, own_rows, size) == row).astype(jnp.bfloat16)
        from_place[...] = (position == column).astype(jnp.bfloat16)
        depth = lax.broadcasted_iota(jnp.int32, (1, adapters * rank_limit), 1)
        hot[...] = (depth // rank_limit == adapter).astype(jnp.bfloat16)

    shapes = (
        jax.ShapeDtypeStruct((batch_rows, slots * rank_limit), jnp.float32),
        jax.ShapeDtypeStruct((batch_rows, batch_rows), jnp.bfloat16),
        jax.ShapeDtypeStruct((batch_rows, batch_rows), jnp.bfloat16),
        jax.ShapeDtypeStruct((batch_rows, adapters * rank_limit), jnp.bfloat16),
    )
    return pl.pallas_call(
        kernel,
        out_shape=shapes,
        grid=(1,),
        in_specs=[whole(pltpu.SMEM)] + [pl.BlockSpec(t.shape, lambda i: (0, 0)) for t in tables],
        out_specs=[pl.BlockSpec(shape.shape, lambda i: (0, 0)) for shape in shapes],
        compiler_params=pltpu.CompilerParams(vmem_limit_bytes=VMEM_LIMIT),
        name="row_masks",
    )(me, *tables)


def shrink_rows(parts, shrink_factors, scale, to_place):
    slots, model_width, rank_limit = shrink_factors.shape
    factor = jnp.swapaxes(shrink_factors, 1, 2).reshape(slots * rank_limit, model_width)
    batch_rows = to_place.shape[0]
    width = model_width // 8

    def kernel(*refs):
        factor_ref, scale_ref, place_ref, rows_out, coeff_out, total = refs[len(parts) :]

        def columns(k, _):
            at = pl.ds(pl.multiple_of(k * width, width), width)
            top = 0
            for part in refs[: len(parts)]:
                rows_out[top : top + part.shape[0], at] = part[:, at]
                top += part.shape[0]
            product = lax.dot_general(
                rows_out[:, at],
                factor_ref[:, at],
                (((1,), (1,)), ((), ())),
                preferred_element_type=jnp.float32,
            )
            total[...] = jnp.where(k == 0, product, total[...] + product)
            return 0

        lax.fori_loop(0, model_width // width, columns, 0)
        scaled = total[...] * scale_ref[...]
        coeff = scaled[:, :rank_limit]
        for s in range(1, slots):
            coeff = coeff + scaled[:, s * rank_limit : (s + 1) * rank_limit]
        coeff_out[...] = jnp.dot(
            place_ref[...], coeff.astype(jnp.bfloat16), preferred_element_type=jnp.float32
        ).astype(jnp.bfloat16)

    return call(
        kernel,
        (
            jax.ShapeDtypeStruct((batch_rows, model_width), jnp.bfloat16),
            jax.ShapeDtypeStruct((batch_rows, rank_limit), jnp.bfloat16),
        ),
        [*parts, factor, scale, to_place],
        "shrink_rows",
        scratch_shapes=[pltpu.VMEM((batch_rows, slots * rank_limit), jnp.float32)],
        cost_estimate=pl.CostEstimate(
            flops=2 * batch_rows * model_width * slots * rank_limit,
            bytes_accessed=4 * batch_rows * model_width,
            transcendentals=0,
        ),
    )


def add_coefficients(a, b, ordered):
    def kernel(a_ref, b_ref, out):
        out[...] = a_ref[...] + b_ref[...]

    return call(
        kernel, jax.ShapeDtypeStruct(a.shape, a.dtype), [a, b], "add_coefficients", ordered
    )


def streamed(source, pieces, buffers, arrived):
    slots = buffers.shape[0]
    copies = [
        pltpu.make_async_copy(source.at[piece], buffers.at[i % slots], arrived.at[i % slots])
        for i, piece in enumerate(pieces)
    ]
    for copy in copies[:slots]:
        copy.start()
    for i, copy in enumerate(copies):
        copy.wait()
        yield i, buffers[i % slots]
        if i + slots < len(copies):
            copies[i + slots].start()


def matmul(rows, weight, name, first, last, ordered=()):
    batch_rows = rows.shape[0]
    width = weight.shape[1]
    starts = range(first, last, DEPTH_BLOCK)
    pieces = [(slice(at, at + DEPTH_BLOCK), slice(None)) for at in starts]

    def kernel(rows_ref, weight_ref, *rest):
        out, buffers, arrived = rest[-3:]
        for i, block in streamed(weight_ref, pieces, buffers, arrived):
            product = jnp.dot(
                rows_ref[:, pieces[i][0]], block, preferred_element_type=jnp.float32
            )
            out[...] = product if i == 0 else out[...] + product

    return pl.pallas_call(
        kernel,
        out_shape=jax.ShapeDtypeStruct((batch_rows, width), jnp.float32),
        in_specs=[whole(), whole(pltpu.HBM)] + [whole(pl.ANY)] * len(ordered),
        out_specs=whole(),
        scratch_shapes=[
            pltpu.VMEM((IN_FLIGHT, DEPTH_BLOCK, width), weight.dtype),
            pltpu.SemaphoreType.DMA((IN_FLIGHT,)),
        ],
        compiler_params=pltpu.CompilerParams(vmem_limit_bytes=STREAM_LIMIT),
        cost_estimate=pl.CostEstimate(
            flops=2 * batch_rows * (last - first) * width,
            bytes_accessed=2 * (last - first) * width,
            transcendentals=0,
        ),
        name=name,
    )(rows, weight, *ordered)


def hidden_kernel(coeff, recv, from_place, hot, expand, gate, up, more, out, spread):
    rank_limit = coeff.shape[1]
    own = jnp.dot(
        from_place[...], coeff[...] + recv[...], preferred_element_type=jnp.float32
    ).astype(jnp.bfloat16)
    pair = jnp.concatenate([own, own], axis=1)
    for p in range(spread.shape[1] // (2 * rank_limit)):
        at = slice(p * 2 * rank_limit, (p + 1) * 2 * rank_limit)
        spread[:, at] = hot[:, at] * pair
    lora = jnp.dot(spread[...], expand[...], preferred_element_type=jnp.float32)
    value = gate[...]
    total = up[...] + more[...] + lora
    out[...] = (value / (1.0 + jnp.exp(-value)) * total).astype(jnp.bfloat16)


def hidden_rows(gate, up, more, coeff, recv, expand_factors, from_place, hot):
    adapters, rank_limit, width = expand_factors.shape
    batch_rows = gate.shape[0]
    expand = expand_factors.reshape(adapters * rank_limit, width)
    return call(
        hidden_kernel,
        jax.ShapeDtypeStruct((batch_rows, width), jnp.bfloat16),
        [coeff, recv, from_place, hot, expand, gate, up, more],
        "hidden_rows",
        scratch_shapes=[pltpu.VMEM((batch_rows, adapters * rank_limit), jnp.bfloat16)],
        cost_estimate=pl.CostEstimate(
            flops=2 * batch_rows * adapters * rank_limit * width,
            bytes_accessed=2 * adapters * rank_limit * width,
            transcendentals=batch_rows * width,
        ),
    )


def down_rows(hidden, down_weight, half, ordered=()):
    batch_rows, hidden_width = hidden.shape
    width = down_weight.shape[1] // HALVES
    core_rows = batch_rows // 2
    starts = range(half * width, (half + 1) * width, WIDTH_BLOCK)
    pieces = [(slice(None), slice(at, at + WIDTH_BLOCK)) for at in starts]

    def kernel(hidden_ref, weight, *rest):
        mine, theirs, buffers, arrived = rest[-4:]
        for i, block in streamed(weight, pieces, buffers, arrived):
            product = jnp.dot(
                hidden_ref[...], block, preferred_element_type=jnp.float32
            ).astype(jnp.bfloat16)
            at = slice(i * WIDTH_BLOCK, (i + 1) * WIDTH_BLOCK)
            theirs[:, at] = product[core_rows:]
            mine[:, at] = product[:core_rows]

    part = jax.ShapeDtypeStruct((core_rows, width), jnp.bfloat16)
    return pl.pallas_call(
        kernel,
        out_shape=(part, part),
        in_specs=[whole(), whole(pltpu.HBM)] + [whole(pl.ANY)] * len(ordered),
        out_specs=[whole()] * 2,
        scratch_shapes=[
            pltpu.VMEM((IN_FLIGHT, hidden_width, WIDTH_BLOCK), down_weight.dtype),
            pltpu.SemaphoreType.DMA((IN_FLIGHT,)),
        ],
        compiler_params=pltpu.CompilerParams(vmem_limit_bytes=STREAM_LIMIT),
        cost_estimate=pl.CostEstimate(
            flops=2 * batch_rows * hidden_width * width,
            bytes_accessed=2 * hidden_width * width,
            transcendentals=0,
        ),
        name="down_rows",
    )(hidden, down_weight, *ordered)


def add_blocks(sides, own_rows, ordered):
    operands, shapes = [], []
    for mine, theirs, _, arrived in sides:
        operands += [mine, theirs] + ([] if arrived is None else [arrived])
        shapes.append(jax.ShapeDtypeStruct((own_rows, mine.shape[1]), jnp.bfloat16))

    def kernel(*refs):
        refs = list(refs)
        outs = refs[-len(sides) :]
        for (_, _, index, arrived), out in zip(sides, outs):
            at = slice(index * own_rows, (index + 1) * own_rows)
            total = refs.pop(0)[at, :].astype(jnp.float32)
            total = total + refs.pop(0)[at, :].astype(jnp.float32)
            if arrived is not None:
                total = total + refs.pop(0)[...].astype(jnp.float32)
            out[...] = total.astype(jnp.bfloat16)

    return call(kernel, tuple(shapes), operands, "add_blocks", ordered)


def scatter_rows(mine, theirs, own_rows, size):
    chips = size // 2
    last = chips // 2
    right, left = [None] * HALVES, [None] * HALVES
    ordered = []
    for turn in range(last):
        for h in range(HALVES):
            steps_right = last - turn - (h == 1)
            steps_left = last - turn - (h == 0)
            sides = []
            if steps_right > 0:
                index = min(2 * steps_right, chips - 1)
                sides.append((mine[h], theirs[h], index, right[h]))
            if steps_left > 0:
                sides.append((mine[h], theirs[h], 2 * steps_left - 1, left[h]))
            sums = list(add_blocks(sides, own_rows, ordered))
            ordered = [sums[0]]
            if steps_right > 0:
                right[h] = lax.ppermute(sums.pop(0), AXIS, ring(size, 1))
            if steps_left > 0:
                left[h] = lax.ppermute(sums.pop(0), AXIS, ring(size, -1))
    return list(zip(mine, theirs, right, left))


def finish_rows(halves, activations, gain, own_rows):
    width = activations.shape[1] // HALVES

    def kernel(*refs):
        refs, (act, gain_ref, block_out, normed, stream) = refs[:-5], refs[-5:]
        square = jnp.zeros((own_rows, 1), jnp.float32)
        for h in range(HALVES):
            mine, theirs, right, left = refs[4 * h : 4 * h + 4]
            at = slice(h * width, (h + 1) * width)
            total = act[:, at].astype(jnp.float32)
            for ref in (mine, theirs):
                total = total + ref[:own_rows, :].astype(jnp.float32)
            for ref in (right, left):
                total = total + ref[...].astype(jnp.float32)
            stream[:, at] = total
            block_out[:, at] = total.astype(jnp.bfloat16)
            square = square + jnp.sum(total * total, axis=1, keepdims=True)
        scale = lax.rsqrt(square * (1.0 / act.shape[1]) + 1e-05)
        normed[...] = (stream[...] * scale * gain_ref[...].astype(jnp.float32)).astype(
            jnp.bfloat16
        )

    out = jax.ShapeDtypeStruct(activations.shape, jnp.bfloat16)
    return call(
        kernel,
        (out, out),
        [array for half in halves for array in half] + [activations, gain],
        "finish_rows",
        scratch_shapes=[pltpu.VMEM(activations.shape, jnp.float32)],
    )


def body(
    activations,
    gate_weight,
    up_weight,
    down_weight,
    norm_gain_vector,
    shrink_factors,
    expand_factors,
    adapter_ranks,
    adapter_storage_slot,
    segment_start,
    segment_adapter,
):
    size = lax.axis_size(AXIS)
    me = lax.axis_index(AXIS).astype(jnp.int32).reshape(1)
    own_rows, model_width = activations.shape
    slots, _, rank_limit = shrink_factors.shape
    assert size & (size - 1) == 0 and own_rows & (own_rows - 1) == 0
    tables = [
        table[None]
        for table in (segment_start, segment_adapter, adapter_ranks, adapter_storage_slot)
    ]
    scale, to_place, from_place, hot = row_masks(me, tables, own_rows, size, slots, rank_limit)

    parts = gather_rows(activations, size, [scale])
    rows, coeff = shrink_rows(parts, shrink_factors, scale, to_place)

    bits = [1 << b for b in range(size.bit_length() - 1)]
    work = []
    for bit in bits[:-1]:
        received = lax.ppermute(coeff, AXIS, flip(size, bit))
        if bit == bits[1]:
            work = [matmul(rows, gate_weight, "gate_rows", 0, model_width, [coeff])]
            gate = work[0]
        if bit == bits[2]:
            work = [matmul(rows, up_weight, "up_rows", 0, model_width // 2, [coeff])]
            up = work[0]
        coeff = add_coefficients(coeff, received, work)
    received = lax.ppermute(coeff, AXIS, flip(size, bits[-1]))
    more = matmul(rows, up_weight, "up_rows", model_width // 2, model_width, [coeff])
    hidden = hidden_rows(gate, up, more, coeff, received, expand_factors, from_place, hot)

    mine, theirs = [None] * HALVES, [None] * HALVES
    ordered = []
    for h in range(HALVES):
        mine[h], part = down_rows(hidden, down_weight, h, ordered)
        ordered = [part]
        theirs[h] = lax.ppermute(part, AXIS, flip(size, 1))
    halves = scatter_rows(mine, theirs, own_rows, size)
    return finish_rows(halves, activations, norm_gain_vector[None], own_rows)


def solution(mesh):
    return jax.shard_map(
        body,
        mesh=mesh,
        in_specs=(
            P(("groups", "mp"), None),
            P(None, "mp"),
            P(None, "mp"),
            P("mp", None),
            P(),
            P("mp", None, None),
            P(None, None, "mp"),
            P(),
            P(),
            P("groups"),
            P("groups"),
        ),
        out_specs=(P(("groups", "mp"), None), P(("groups", "mp"), None)),
        check_vma=False,
    )
```

```python
import functools

import jax
import jax.numpy as jnp
from jax import lax
from jax.experimental import pallas as pl
from jax.experimental.pallas import tpu as pltpu
from jax.sharding import PartitionSpec as P

adapter_alpha = 32.0
AXIS = "mp"
HALVES = 2
DEPTH_BLOCK = 1024
WIDTH_BLOCK = 512
VMEM_LIMIT = 16 * 1024 * 1024
STREAM_LIMIT = 46 * 1024 * 1024


def chip_at(place, chips):
    if chips == 8:
        return jnp.where(place < 4, 2 * place, 2 * (7 - place) + 1)
    return place


def place_of(chip, chips):
    if chips == 8:
        return jnp.where((chip & 1) == 0, chip >> 1, 7 - (chip >> 1))
    return chip


def ring(size, by):
    chips = size // 2
    order = [0, 2, 4, 6, 7, 5, 3, 1] if chips == 8 else list(range(chips))
    pairs = []
    for place, chip in enumerate(order):
        to = order[(place + by) % chips]
        pairs += [(2 * chip + core, 2 * to + core) for core in range(2)]
    return pairs


def flip(size, bit):
    return [(i, i ^ bit) for i in range(size)]


def row_positions(me, row, own_rows, size):
    chips = size // 2
    block = row // own_rows
    index = block & (chips - 1)
    step = (index + 1) >> 1
    delta = jnp.where((index & 1) == 1, step, -step)
    place = (place_of(me >> 1, chips) - delta + chips) & (chips - 1)
    core = (me & 1) ^ (block // chips)
    return (2 * chip_at(place, chips) + core) * own_rows + (row & (own_rows - 1))


def pick(index, table):
    hot = index == lax.broadcasted_iota(jnp.int32, (1, table.shape[1]), 1)
    return jnp.sum(jnp.where(hot, table, 0), axis=1, keepdims=True)


def row_adapters(position, start, adapters):
    segment = jnp.sum((start <= position).astype(jnp.int32), axis=1, keepdims=True) - 1
    return pick(segment, adapters)


def whole(space=pltpu.VMEM):
    return pl.BlockSpec(memory_space=space)


def call(kernel, out_shape, operands, name, ordered=(), limit=VMEM_LIMIT, **options):
    count = len(operands)

    def run(*refs):
        kernel(*refs[:count], *refs[count + len(ordered) :])

    return pl.pallas_call(
        run,
        out_shape=out_shape,
        in_specs=[
            whole(pltpu.SMEM if operand.ndim == 1 else pltpu.VMEM) for operand in operands
        ]
        + [whole(pl.ANY)] * len(ordered),
        out_specs=jax.tree.map(lambda _: whole(), out_shape),
        compiler_params=pltpu.CompilerParams(vmem_limit_bytes=limit),
        name=name,
        **options,
    )(*operands, *ordered)


def split_columns(array):
    rows, columns = array.shape
    width = columns // HALVES
    half = jax.ShapeDtypeStruct((rows, width), array.dtype)

    def kernel(ref, *outs):
        for h, out in enumerate(outs):
            out[...] = ref[:, h * width : (h + 1) * width]

    return call(kernel, (half,) * HALVES, [array], "split_columns")


def join(pieces, ordered=()):
    rows, width = pieces[0].shape

    def kernel(*refs):
        out = refs[-1]
        for i, ref in enumerate(refs[:-1]):
            top, left = i // HALVES * rows, i % HALVES * width
            out[top : top + rows, left : left + width] = ref[...]

    shape = (rows * len(pieces) // HALVES, HALVES * width)
    return call(
        kernel, jax.ShapeDtypeStruct(shape, pieces[0].dtype), pieces, "join_pieces", ordered
    )


def gather_rows(own, size, masks_after):
    chips = size // 2
    last = chips // 2
    other = lax.ppermute(own, AXIS, flip(size, 1))
    halves = split_columns(own)
    right, left = list(halves), list(halves)
    pieces = []
    mine, theirs = [own], [other]
    for step in range(1, last + 1):
        if step < last:
            right[0] = lax.ppermute(right[0], AXIS, ring(size, 1))
            left[1] = lax.ppermute(left[1], AXIS, ring(size, -1))
            right[1] = lax.ppermute(right[1], AXIS, ring(size, 1))
            left[0] = lax.ppermute(left[0], AXIS, ring(size, -1))
            pieces += right + left
        else:
            pieces.append(lax.ppermute(right[0], AXIS, ring(size, 1)))
            pieces.append(lax.ppermute(left[1], AXIS, ring(size, -1)))
        if step >= last - 1:
            part = join(pieces, [masks[0]] if step == last else [])
            pieces = []
            mine.append(part)
            theirs.append(lax.ppermute(part, AXIS, flip(size, 1)))
            if step < last:
                masks = masks_after(part)
    return mine + theirs, masks


def row_masks(me, tables, own_rows, size, slots, rank_limit, ordered):
    batch_rows = own_rows * size
    adapters = tables[2].shape[1]

    def kernel(me_ref, start, segment_adapter, ranks, slot_of, *rest):
        scale, to_place, from_place, hot = rest[-4:]
        me = me_ref[0]
        row = lax.broadcasted_iota(jnp.int32, (batch_rows, 1), 0)
        column = lax.broadcasted_iota(jnp.int32, (1, batch_rows), 1)
        position = row_positions(me, row, own_rows, size)
        adapter = row_adapters(position, start[...], segment_adapter[...])
        rank = pick(adapter, ranks[...])
        slot = pick(adapter, slot_of[...]) - me * slots
        at = lax.broadcasted_iota(jnp.int32, (1, slots * rank_limit), 1)
        keep = (at // rank_limit == slot) & (at % rank_limit < rank)
        scale[...] = jnp.where(keep, adapter_alpha / rank.astype(jnp.float32), 0.0)
        to_place[...] = (row_positions(me, column, own_rows, size) == row).astype(jnp.bfloat16)
        from_place[...] = (position == column).astype(jnp.bfloat16)
        depth = lax.broadcasted_iota(jnp.int32, (1, adapters * rank_limit), 1)
        hot[...] = (depth // rank_limit == adapter).astype(jnp.bfloat16)

    shapes = (
        jax.ShapeDtypeStruct((batch_rows, slots * rank_limit), jnp.float32),
        jax.ShapeDtypeStruct((batch_rows, batch_rows), jnp.bfloat16),
        jax.ShapeDtypeStruct((batch_rows, batch_rows), jnp.bfloat16),
        jax.ShapeDtypeStruct((batch_rows, adapters * rank_limit), jnp.bfloat16),
    )
    return pl.pallas_call(
        kernel,
        out_shape=shapes,
        grid=(1,),
        in_specs=[whole(pltpu.SMEM)]
        + [pl.BlockSpec(t.shape, lambda i: (0, 0)) for t in tables]
        + [whole(pl.ANY)] * len(ordered),
        out_specs=[pl.BlockSpec(shape.shape, lambda i: (0, 0)) for shape in shapes],
        compiler_params=pltpu.CompilerParams(vmem_limit_bytes=VMEM_LIMIT),
        name="row_masks",
    )(me, *tables, *ordered)


def shrink_rows(parts, shrink_factors, scale, to_place):
    slots, model_width, rank_limit = shrink_factors.shape
    factor = jnp.swapaxes(shrink_factors, 1, 2).reshape(slots * rank_limit, model_width)
    batch_rows = to_place.shape[0]
    width = model_width // 8

    def kernel(*refs):
        factor_ref, scale_ref, place_ref, rows_out, coeff_out, total = refs[len(parts) :]

        def columns(k, _):
            at = pl.ds(pl.multiple_of(k * width, width), width)
            top = 0
            for part in refs[: len(parts)]:
                rows_out[top : top + part.shape[0], at] = part[:, at]
                top += part.shape[0]
            product = lax.dot_general(
                rows_out[:, at],
                factor_ref[:, at],
                (((1,), (1,)), ((), ())),
                preferred_element_type=jnp.float32,
            )
            total[...] = jnp.where(k == 0, product, total[...] + product)
            return 0

        lax.fori_loop(0, model_width // width, columns, 0)
        scaled = total[...] * scale_ref[...]
        coeff = scaled[:, :rank_limit]
        for s in range(1, slots):
            coeff = coeff + scaled[:, s * rank_limit : (s + 1) * rank_limit]
        coeff_out[...] = jnp.dot(
            place_ref[...], coeff.astype(jnp.bfloat16), preferred_element_type=jnp.float32
        ).astype(jnp.bfloat16)

    return call(
        kernel,
        (
            jax.ShapeDtypeStruct((batch_rows, model_width), jnp.bfloat16),
            jax.ShapeDtypeStruct((batch_rows, rank_limit), jnp.bfloat16),
        ),
        [*parts, factor, scale, to_place],
        "shrink_rows",
        scratch_shapes=[pltpu.VMEM((batch_rows, slots * rank_limit), jnp.float32)],
        cost_estimate=pl.CostEstimate(
            flops=2 * batch_rows * model_width * slots * rank_limit,
            bytes_accessed=4 * batch_rows * model_width,
            transcendentals=0,
        ),
    )


def add_coefficients(a, b, ordered):
    def kernel(a_ref, b_ref, out):
        out[...] = a_ref[...] + b_ref[...]

    return call(
        kernel, jax.ShapeDtypeStruct(a.shape, a.dtype), [a, b], "add_coefficients", ordered
    )


def streamed(source, blocks, buffers, arrived):
    slots, depth = buffers.shape[:2]
    parts = arrived.shape[1]
    step = depth // parts

    def copies(i):
        rows, columns = blocks[i]
        return [
            pltpu.make_async_copy(
                source.at[rows + p * step : rows + (p + 1) * step, columns],
                buffers.at[i % slots, p * step : (p + 1) * step],
                arrived.at[i % slots, p],
            )
            for p in range(parts)
        ]

    def start(i):
        for copy in copies(i):
            copy.start()

    for i in range(min(slots, len(blocks))):
        start(i)
    for i in range(len(blocks)):
        for copy in copies(i):
            copy.wait()
        yield i, buffers[i % slots]
        if i + slots < len(blocks):
            start(i + slots)


def matmul(rows, weight, name, first, last, ordered=()):
    batch_rows = rows.shape[0]
    width = weight.shape[1]
    starts = range(first, last, DEPTH_BLOCK)
    blocks = [(at, slice(None)) for at in starts]

    def kernel(rows_ref, weight_ref, *rest):
        out, buffers, arrived = rest[-3:]
        for i, block in streamed(weight_ref, blocks, buffers, arrived):
            at = slice(blocks[i][0], blocks[i][0] + DEPTH_BLOCK)
            product = jnp.dot(rows_ref[:, at], block, preferred_element_type=jnp.float32)
            out[...] = product if i == 0 else out[...] + product

    return pl.pallas_call(
        kernel,
        out_shape=jax.ShapeDtypeStruct((batch_rows, width), jnp.float32),
        in_specs=[whole(), whole(pltpu.HBM)] + [whole(pl.ANY)] * len(ordered),
        out_specs=whole(),
        scratch_shapes=[
            pltpu.VMEM((3, DEPTH_BLOCK, width), weight.dtype),
            pltpu.SemaphoreType.DMA((3, 4)),
        ],
        compiler_params=pltpu.CompilerParams(vmem_limit_bytes=STREAM_LIMIT),
        cost_estimate=pl.CostEstimate(
            flops=2 * batch_rows * (last - first) * width,
            bytes_accessed=2 * (last - first) * width,
            transcendentals=0,
        ),
        name=name,
    )(rows, weight, *ordered)


def hidden_kernel(coeff, recv, from_place, hot, expand, gate, up, more, out, spread):
    rank_limit = coeff.shape[1]
    own = jnp.dot(
        from_place[...], coeff[...] + recv[...], preferred_element_type=jnp.float32
    ).astype(jnp.bfloat16)
    pair = jnp.concatenate([own, own], axis=1)
    for p in range(spread.shape[1] // (2 * rank_limit)):
        at = slice(p * 2 * rank_limit, (p + 1) * 2 * rank_limit)
        spread[:, at] = hot[:, at] * pair
    lora = jnp.dot(spread[...], expand[...], preferred_element_type=jnp.float32)
    value = gate[...]
    total = up[...] + more[...] + lora
    out[...] = (value / (1.0 + jnp.exp(-value)) * total).astype(jnp.bfloat16)


def hidden_rows(gate, up, more, coeff, recv, expand_factors, from_place, hot):
    adapters, rank_limit, width = expand_factors.shape
    batch_rows = gate.shape[0]
    expand = expand_factors.reshape(adapters * rank_limit, width)
    return call(
        hidden_kernel,
        jax.ShapeDtypeStruct((batch_rows, width), jnp.bfloat16),
        [coeff, recv, from_place, hot, expand, gate, up, more],
        "hidden_rows",
        scratch_shapes=[pltpu.VMEM((batch_rows, adapters * rank_limit), jnp.bfloat16)],
        cost_estimate=pl.CostEstimate(
            flops=2 * batch_rows * adapters * rank_limit * width,
            bytes_accessed=2 * adapters * rank_limit * width,
            transcendentals=batch_rows * width,
        ),
    )


def down_rows(hidden, down_weight, half, ordered=()):
    batch_rows, hidden_width = hidden.shape
    width = down_weight.shape[1] // HALVES
    core_rows = batch_rows // 2
    starts = range(half * width, (half + 1) * width, WIDTH_BLOCK)
    blocks = [(0, slice(at, at + WIDTH_BLOCK)) for at in starts]

    def kernel(hidden_ref, weight, *rest):
        mine, theirs, buffers, arrived = rest[-4:]
        for i, block in streamed(weight, blocks, buffers, arrived):
            product = jnp.dot(
                hidden_ref[...], block, preferred_element_type=jnp.float32
            ).astype(jnp.bfloat16)
            at = slice(i * WIDTH_BLOCK, (i + 1) * WIDTH_BLOCK)
            theirs[:, at] = product[core_rows:]
            mine[:, at] = product[:core_rows]

    part = jax.ShapeDtypeStruct((core_rows, width), jnp.bfloat16)
    return pl.pallas_call(
        kernel,
        out_shape=(part, part),
        in_specs=[whole(), whole(pltpu.HBM)] + [whole(pl.ANY)] * len(ordered),
        out_specs=[whole()] * 2,
        scratch_shapes=[
            pltpu.VMEM((6, hidden_width, WIDTH_BLOCK), down_weight.dtype),
            pltpu.SemaphoreType.DMA((6, 2)),
        ],
        compiler_params=pltpu.CompilerParams(vmem_limit_bytes=STREAM_LIMIT),
        cost_estimate=pl.CostEstimate(
            flops=2 * batch_rows * hidden_width * width,
            bytes_accessed=2 * hidden_width * width,
            transcendentals=0,
        ),
        name="down_rows",
    )(hidden, down_weight, *ordered)


def add_blocks(sides, own_rows, ordered):
    operands, shapes = [], []
    for mine, theirs, _, arrived in sides:
        operands += [mine, theirs] + ([] if arrived is None else [arrived])
        shapes.append(jax.ShapeDtypeStruct((own_rows, mine.shape[1]), jnp.bfloat16))

    def kernel(*refs):
        refs = list(refs)
        outs = refs[-len(sides) :]
        for (_, _, index, arrived), out in zip(sides, outs):
            at = slice(index * own_rows, (index + 1) * own_rows)
            total = refs.pop(0)[at, :].astype(jnp.float32)
            total = total + refs.pop(0)[at, :].astype(jnp.float32)
            if arrived is not None:
                total = total + refs.pop(0)[...].astype(jnp.float32)
            out[...] = total.astype(jnp.bfloat16)

    return call(kernel, tuple(shapes), operands, "add_blocks", ordered)


def scatter_rows(mine, theirs, own_rows, size):
    chips = size // 2
    last = chips // 2
    right, left = [None] * HALVES, [None] * HALVES
    ordered = []
    for turn in range(last):
        for h in range(HALVES):
            steps_right = last - turn - (h == 1)
            steps_left = last - turn - (h == 0)
            sides = []
            if steps_right > 0:
                index = min(2 * steps_right, chips - 1)
                sides.append((right, 1, index))
            if steps_left > 0:
                sides.append((left, -1, 2 * steps_left - 1))
            if h == 1:
                sides.reverse()
            sums = add_blocks(
                [(mine[h], theirs[h], index, chain[h]) for chain, _, index in sides],
                own_rows,
                ordered,
            )
            ordered = [sums[0]]
            for (chain, by, _), value in zip(sides, sums):
                chain[h] = lax.ppermute(value, AXIS, ring(size, by))
    return list(zip(mine, theirs, right, left))


def finish_rows(halves, activations, gain, own_rows):
    width = activations.shape[1] // HALVES

    def kernel(*refs):
        refs, (act, gain_ref, block_out, normed, stream) = refs[:-5], refs[-5:]
        square = jnp.zeros((own_rows, 1), jnp.float32)
        for h in range(HALVES):
            mine, theirs, right, left = refs[4 * h : 4 * h + 4]
            at = slice(h * width, (h + 1) * width)
            total = act[:, at].astype(jnp.float32)
            for ref in (mine, theirs):
                total = total + ref[:own_rows, :].astype(jnp.float32)
            for ref in (right, left):
                total = total + ref[...].astype(jnp.float32)
            stream[:, at] = total
            block_out[:, at] = total.astype(jnp.bfloat16)
            square = square + jnp.sum(total * total, axis=1, keepdims=True)
        scale = lax.rsqrt(square * (1.0 / act.shape[1]) + 1e-05)
        normed[...] = (stream[...] * scale * gain_ref[...].astype(jnp.float32)).astype(
            jnp.bfloat16
        )

    out = jax.ShapeDtypeStruct(activations.shape, jnp.bfloat16)
    return call(
        kernel,
        (out, out),
        [array for half in halves for array in half] + [activations, gain],
        "finish_rows",
        scratch_shapes=[pltpu.VMEM(activations.shape, jnp.float32)],
    )


def body(
    activations,
    gate_weight,
    up_weight,
    down_weight,
    norm_gain_vector,
    shrink_factors,
    expand_factors,
    adapter_ranks,
    adapter_storage_slot,
    segment_start,
    segment_adapter,
):
    size = lax.axis_size(AXIS)
    me = lax.axis_index(AXIS).astype(jnp.int32).reshape(1)
    own_rows, model_width = activations.shape
    slots, _, rank_limit = shrink_factors.shape
    assert size & (size - 1) == 0 and own_rows & (own_rows - 1) == 0
    tables = [
        table[None]
        for table in (segment_start, segment_adapter, adapter_ranks, adapter_storage_slot)
    ]
    parts, (scale, to_place, from_place, hot) = gather_rows(
        activations,
        size,
        lambda part: row_masks(me, tables, own_rows, size, slots, rank_limit, [part]),
    )
    rows, coeff = shrink_rows(parts, shrink_factors, scale, to_place)

    bits = [1 << b for b in range(size.bit_length() - 1)]
    work = []
    for bit in bits[:-1]:
        received = lax.ppermute(coeff, AXIS, flip(size, bit))
        if bit == bits[1]:
            work = [matmul(rows, gate_weight, "gate_rows", 0, model_width, [coeff])]
            gate = work[0]
        if bit == bits[2]:
            work = [matmul(rows, up_weight, "up_rows", 0, model_width // 2, [coeff])]
            up = work[0]
        coeff = add_coefficients(coeff, received, work)
    received = lax.ppermute(coeff, AXIS, flip(size, bits[-1]))
    more = matmul(rows, up_weight, "up_rows", model_width // 2, model_width, [coeff])
    hidden = hidden_rows(gate, up, more, coeff, received, expand_factors, from_place, hot)

    mine, theirs = [None] * HALVES, [None] * HALVES
    ordered = []
    for h in range(HALVES):
        mine[h], part = down_rows(hidden, down_weight, h, ordered)
        ordered = [part]
        theirs[h] = lax.ppermute(part, AXIS, flip(size, 1))
    halves = scatter_rows(mine, theirs, own_rows, size)
    return finish_rows(halves, activations, norm_gain_vector[None], own_rows)


def solution(mesh):
    return jax.shard_map(
        body,
        mesh=mesh,
        in_specs=(
            P(("groups", "mp"), None),
            P(None, "mp"),
            P(None, "mp"),
            P("mp", None),
            P(),
            P("mp", None, None),
            P(None, None, "mp"),
            P(),
            P(),
            P("groups"),
            P("groups"),
        ),
        out_specs=(P(("groups", "mp"), None), P(("groups", "mp"), None)),
        check_vma=False,
    )
```

```python
import functools

import jax
import jax.numpy as jnp
from jax import lax
from jax.experimental import pallas as pl
from jax.experimental.pallas import tpu as pltpu
from jax.sharding import PartitionSpec as P

adapter_alpha = 32.0
AXIS = "mp"
HALVES = 2
DEPTH_BLOCK = 1024
VMEM_LIMIT = 16 * 1024 * 1024
STREAM_LIMIT = 38 * 1024 * 1024


def chip_at(place, chips):
    if chips == 8:
        return jnp.where(place < 4, 2 * place, 2 * (7 - place) + 1)
    return place


def place_of(chip, chips):
    if chips == 8:
        return jnp.where((chip & 1) == 0, chip >> 1, 7 - (chip >> 1))
    return chip


def ring(size, by):
    chips = size // 2
    order = [0, 2, 4, 6, 7, 5, 3, 1] if chips == 8 else list(range(chips))
    pairs = []
    for place, chip in enumerate(order):
        to = order[(place + by) % chips]
        pairs += [(2 * chip + core, 2 * to + core) for core in range(2)]
    return pairs


def flip(size, bit):
    return [(i, i ^ bit) for i in range(size)]


def row_positions(me, row, own_rows, size):
    chips = size // 2
    block = row // own_rows
    index = block & (chips - 1)
    step = (index + 1) >> 1
    delta = jnp.where((index & 1) == 1, step, -step)
    place = (place_of(me >> 1, chips) - delta + chips) & (chips - 1)
    core = (me & 1) ^ (block // chips)
    return (2 * chip_at(place, chips) + core) * own_rows + (row & (own_rows - 1))


def pick(index, table):
    hot = index == lax.broadcasted_iota(jnp.int32, (1, table.shape[1]), 1)
    return jnp.sum(jnp.where(hot, table, 0), axis=1, keepdims=True)


def row_adapters(position, start, adapters):
    segment = jnp.sum((start <= position).astype(jnp.int32), axis=1, keepdims=True) - 1
    return pick(segment, adapters)


def whole(space=pltpu.VMEM):
    return pl.BlockSpec(memory_space=space)


def call(kernel, out_shape, operands, name, ordered=(), limit=VMEM_LIMIT, **options):
    count = len(operands)

    def run(*refs):
        kernel(*refs[:count], *refs[count + len(ordered) :])

    return pl.pallas_call(
        run,
        out_shape=out_shape,
        in_specs=[
            whole(pltpu.SMEM if operand.ndim == 1 else pltpu.VMEM) for operand in operands
        ]
        + [whole(pl.ANY)] * len(ordered),
        out_specs=jax.tree.map(lambda _: whole(), out_shape),
        compiler_params=pltpu.CompilerParams(vmem_limit_bytes=limit),
        name=name,
        **options,
    )(*operands, *ordered)


def split_columns(array):
    rows, columns = array.shape
    width = columns // HALVES
    half = jax.ShapeDtypeStruct((rows, width), array.dtype)

    def kernel(ref, *outs):
        for h, out in enumerate(outs):
            out[...] = ref[:, h * width : (h + 1) * width]

    return call(kernel, (half,) * HALVES, [array], "split_columns")


def join(pieces, ordered=()):
    rows, width = pieces[0].shape

    def kernel(*refs):
        out = refs[-1]
        for i, ref in enumerate(refs[:-1]):
            top, left = i // HALVES * rows, i % HALVES * width
            out[top : top + rows, left : left + width] = ref[...]

    shape = (rows * len(pieces) // HALVES, HALVES * width)
    return call(
        kernel, jax.ShapeDtypeStruct(shape, pieces[0].dtype), pieces, "join_pieces", ordered
    )


def gather_rows(own, size, ordered):
    chips = size // 2
    last = chips // 2
    other = lax.ppermute(own, AXIS, flip(size, 1))
    halves = split_columns(own)
    right, left = list(halves), list(halves)
    pieces = []
    mine, theirs = [own], [other]
    for step in range(1, last + 1):
        if step < last:
            right[0] = lax.ppermute(right[0], AXIS, ring(size, 1))
            left[1] = lax.ppermute(left[1], AXIS, ring(size, -1))
            right[1] = lax.ppermute(right[1], AXIS, ring(size, 1))
            left[0] = lax.ppermute(left[0], AXIS, ring(size, -1))
            pieces += right + left
        else:
            pieces.append(lax.ppermute(right[0], AXIS, ring(size, 1)))
            pieces.append(lax.ppermute(left[1], AXIS, ring(size, -1)))
        if step >= last - 1:
            part = join(pieces, ordered if step < last else [])
            pieces = []
            mine.append(part)
            theirs.append(lax.ppermute(part, AXIS, flip(size, 1)))
    return mine + theirs


def row_masks(me, tables, shrink_factors, own_rows, size):
    batch_rows = own_rows * size
    slots, model_width, rank_limit = shrink_factors.shape
    factor = jnp.swapaxes(shrink_factors, 1, 2).reshape(slots * rank_limit, model_width)
    lengths = [table.shape[0] for table in tables]
    starts = [sum(lengths[:i]) for i in range(len(lengths))]
    adapters = lengths[2]

    def kernel(me_ref, all_tables, factor_in, scale, to_place, from_place, hot, factor_out):
        factor_out[...] = factor_in[...]
        me = me_ref[0]
        start, segment_adapter, ranks, slot_of = (
            all_tables[:, at : at + length] for at, length in zip(starts, lengths)
        )
        row = lax.broadcasted_iota(jnp.int32, (batch_rows, 1), 0)
        column = lax.broadcasted_iota(jnp.int32, (1, batch_rows), 1)
        position = row_positions(me, row, own_rows, size)
        adapter = row_adapters(position, start, segment_adapter)
        rank = pick(adapter, ranks)
        slot = pick(adapter, slot_of) - me * slots
        at = lax.broadcasted_iota(jnp.int32, (1, slots * rank_limit), 1)
        keep = (at // rank_limit == slot) & (at % rank_limit < rank)
        scale[...] = jnp.where(keep, adapter_alpha / rank.astype(jnp.float32), 0.0)
        to_place[...] = (row_positions(me, column, own_rows, size) == row).astype(jnp.bfloat16)
        from_place[...] = (position == column).astype(jnp.bfloat16)
        depth = lax.broadcasted_iota(jnp.int32, (1, adapters * rank_limit), 1)
        hot[...] = (depth // rank_limit == adapter).astype(jnp.bfloat16)

    shapes = (
        jax.ShapeDtypeStruct((batch_rows, slots * rank_limit), jnp.float32),
        jax.ShapeDtypeStruct((batch_rows, batch_rows), jnp.bfloat16),
        jax.ShapeDtypeStruct((batch_rows, batch_rows), jnp.bfloat16),
        jax.ShapeDtypeStruct((batch_rows, adapters * rank_limit), jnp.bfloat16),
        jax.ShapeDtypeStruct(factor.shape, factor.dtype),
    )
    return call(kernel, shapes, [me, jnp.concatenate(tables)[None], factor], "row_masks")


def shrink_rows(parts, factor, scale, to_place, rank_limit):
    model_width = factor.shape[1]
    slots = factor.shape[0] // rank_limit
    batch_rows = to_place.shape[0]
    width = model_width // 8

    def kernel(*refs):
        factor_ref, scale_ref, place_ref, rows_out, coeff_out, total = refs[len(parts) :]

        def columns(k, _):
            at = pl.ds(pl.multiple_of(k * width, width), width)
            top = 0
            for part in refs[: len(parts)]:
                rows_out[top : top + part.shape[0], at] = part[:, at]
                top += part.shape[0]
            product = lax.dot_general(
                rows_out[:, at],
                factor_ref[:, at],
                (((1,), (1,)), ((), ())),
                preferred_element_type=jnp.float32,
            )
            total[...] = jnp.where(k == 0, product, total[...] + product)
            return 0

        lax.fori_loop(0, model_width // width, columns, 0)
        scaled = total[...] * scale_ref[...]
        coeff = scaled[:, :rank_limit]
        for s in range(1, slots):
            coeff = coeff + scaled[:, s * rank_limit : (s + 1) * rank_limit]
        coeff_out[...] = jnp.dot(
            place_ref[...], coeff.astype(jnp.bfloat16), preferred_element_type=jnp.float32
        ).astype(jnp.bfloat16)

    return call(
        kernel,
        (
            jax.ShapeDtypeStruct((batch_rows, model_width), jnp.bfloat16),
            jax.ShapeDtypeStruct((batch_rows, rank_limit), jnp.bfloat16),
        ),
        [*parts, factor, scale, to_place],
        "shrink_rows",
        scratch_shapes=[pltpu.VMEM((batch_rows, slots * rank_limit), jnp.float32)],
        cost_estimate=pl.CostEstimate(
            flops=2 * batch_rows * model_width * slots * rank_limit,
            bytes_accessed=4 * batch_rows * model_width,
            transcendentals=0,
        ),
    )


def add_coefficients(a, b, ordered):
    def kernel(a_ref, b_ref, out):
        out[...] = a_ref[...] + b_ref[...]

    return call(
        kernel, jax.ShapeDtypeStruct(a.shape, a.dtype), [a, b], "add_coefficients", ordered
    )


def lane_tiles(width):
    return -(-width // 128) * 128


def mixed_rows(rows, weights, before, first, last, ordered):
    batch_rows = rows.shape[0]
    widths = [weight.shape[1] for weight in weights]
    lefts = [sum(lane_tiles(width) for width in widths[:w]) for w in range(len(weights))]
    width = sum(lane_tiles(width) for width in widths)
    if width == sum(widths):
        buffer_of, offsets = [0] * len(weights), lefts
        products = [(0, width)]
    else:
        buffer_of, offsets = list(range(len(weights))), [0] * len(weights)
        products = list(zip(lefts, widths))
    blocks = []
    at = first
    while at < last:
        depth = min(DEPTH_BLOCK if blocks else DEPTH_BLOCK // 2, last - at)
        blocks.append((at, depth))
        at += depth

    def kernel(rows_ref, *refs):
        sources = refs[: len(weights)]
        arrived = refs[-1]
        buffers = refs[-1 - len(products) : -1]
        out = refs[-2 - len(products)]
        copies = []
        for b, (at, depth) in enumerate(blocks):
            copies.append([])
            half = depth // 2
            for p in range(2):
                for w, source in enumerate(sources):
                    top = at - first + p * half
                    copy = pltpu.make_async_copy(
                        source.at[at + p * half : at + (p + 1) * half, :],
                        buffers[buffer_of[w]].at[
                            top : top + half, offsets[w] : offsets[w] + widths[w]
                        ],
                        arrived.at[b, 2 * w + p],
                    )
                    copy.start()
                    copies[-1].append(copy)
        for (at, depth), group in zip(blocks, copies):
            for copy in group:
                copy.wait()
            for (left, wide), buffer in zip(products, buffers):
                columns = slice(left, left + wide)
                product = jnp.dot(
                    rows_ref[:, at : at + depth],
                    buffer[at - first : at - first + depth, :],
                    preferred_element_type=jnp.float32,
                )
                if at > first:
                    product = out[:, columns] + product
                elif before is not None:
                    product = refs[len(weights)][:, columns] + product
                out[:, columns] = product

    return pl.pallas_call(
        kernel,
        out_shape=jax.ShapeDtypeStruct((batch_rows, width), jnp.float32),
        in_specs=[whole()]
        + [whole(pltpu.HBM)] * len(weights)
        + [whole()] * (before is not None)
        + [whole(pl.ANY)] * len(ordered),
        out_specs=whole(),
        scratch_shapes=[pltpu.VMEM((last - first, wide), rows.dtype) for _, wide in products]
        + [pltpu.SemaphoreType.DMA((len(blocks), 2 * len(weights)))],
        compiler_params=pltpu.CompilerParams(vmem_limit_bytes=STREAM_LIMIT),
        cost_estimate=pl.CostEstimate(
            flops=2 * batch_rows * (last - first) * width,
            bytes_accessed=2 * (last - first) * width,
            transcendentals=0,
        ),
        name="mixed_rows",
    )(rows, *weights, *([] if before is None else [before]), *ordered)


def hidden_kernel(coeff, recv, from_place, hot, expand, mixed, out, spread):
    rank_limit = coeff.shape[1]
    own = jnp.dot(
        from_place[...], coeff[...] + recv[...], preferred_element_type=jnp.float32
    ).astype(jnp.bfloat16)
    pair = jnp.concatenate([own, own], axis=1)
    for p in range(spread.shape[1] // (2 * rank_limit)):
        at = slice(p * 2 * rank_limit, (p + 1) * 2 * rank_limit)
        spread[:, at] = hot[:, at] * pair
    lora = jnp.dot(spread[...], expand[...], preferred_element_type=jnp.float32)
    width = out.shape[1]
    value = mixed[:, :width]
    total = mixed[:, lane_tiles(width) : lane_tiles(width) + width] + lora
    out[...] = (value / (1.0 + jnp.exp(-value)) * total).astype(jnp.bfloat16)


def hidden_rows(mixed, coeff, recv, expand_factors, from_place, hot):
    adapters, rank_limit, width = expand_factors.shape
    batch_rows = mixed.shape[0]
    expand = expand_factors.reshape(adapters * rank_limit, width)
    return call(
        hidden_kernel,
        jax.ShapeDtypeStruct((batch_rows, width), jnp.bfloat16),
        [coeff, recv, from_place, hot, expand, mixed],
        "hidden_rows",
        scratch_shapes=[pltpu.VMEM((batch_rows, adapters * rank_limit), jnp.bfloat16)],
        cost_estimate=pl.CostEstimate(
            flops=2 * batch_rows * adapters * rank_limit * width,
            bytes_accessed=2 * adapters * rank_limit * width,
            transcendentals=batch_rows * width,
        ),
    )


def add_blocks(sides, own_rows, ordered):
    operands, shapes = [], []
    for mine, theirs, _, arrived in sides:
        operands += [mine, theirs] + ([] if arrived is None else [arrived])
        shapes.append(jax.ShapeDtypeStruct((own_rows, mine.shape[1]), jnp.bfloat16))

    def kernel(*refs):
        refs = list(refs)
        outs = refs[-len(sides) :]
        for (_, _, index, arrived), out in zip(sides, outs):
            at = slice(index * own_rows, (index + 1) * own_rows)
            total = refs.pop(0)[at, :].astype(jnp.float32)
            total = total + refs.pop(0)[at, :].astype(jnp.float32)
            if arrived is not None:
                total = total + refs.pop(0)[...].astype(jnp.float32)
            out[...] = total.astype(jnp.bfloat16)

    return call(kernel, tuple(shapes), operands, "add_blocks", ordered)


def scatter_rows(mine, theirs, own_rows, size):
    chips = size // 2
    last = chips // 2
    right, left = [None] * HALVES, [None] * HALVES
    ordered = []
    for turn in range(last):
        for h in range(HALVES):
            steps_right = last - turn - (h == 1)
            steps_left = last - turn - (h == 0)
            sides = []
            if steps_right > 0:
                index = min(2 * steps_right, chips - 1)
                sides.append((right, 1, index))
            if steps_left > 0:
                sides.append((left, -1, 2 * steps_left - 1))
            if h == 1:
                sides.reverse()
            sums = add_blocks(
                [(mine[h], theirs[h], index, chain[h]) for chain, _, index in sides],
                own_rows,
                ordered,
            )
            ordered = [sums[0]]
            for (chain, by, _), value in zip(sides, sums):
                chain[h] = lax.ppermute(value, AXIS, ring(size, by))
    return list(zip(mine, theirs, right, left))


def finish_rows(halves, activations, gain, own_rows):
    width = activations.shape[1] // HALVES

    def kernel(*refs):
        refs, (act, gain_ref, block_out, normed, stream) = refs[:-5], refs[-5:]
        square = jnp.zeros((own_rows, 1), jnp.float32)
        for h in range(HALVES):
            mine, theirs, right, left = refs[4 * h : 4 * h + 4]
            at = slice(h * width, (h + 1) * width)
            total = act[:, at].astype(jnp.float32)
            for ref in (mine, theirs):
                total = total + ref[:own_rows, :].astype(jnp.float32)
            for ref in (right, left):
                total = total + ref[...].astype(jnp.float32)
            stream[:, at] = total
            block_out[:, at] = total.astype(jnp.bfloat16)
            square = square + jnp.sum(total * total, axis=1, keepdims=True)
        scale = lax.rsqrt(square * (1.0 / act.shape[1]) + 1e-05)
        normed[...] = (stream[...] * scale * gain_ref[...].astype(jnp.float32)).astype(
            jnp.bfloat16
        )

    out = jax.ShapeDtypeStruct(activations.shape, jnp.bfloat16)
    return call(
        kernel,
        (out, out),
        [array for half in halves for array in half] + [activations, gain],
        "finish_rows",
        scratch_shapes=[pltpu.VMEM(activations.shape, jnp.float32)],
    )


def body(
    activations,
    gate_weight,
    up_weight,
    down_weight,
    norm_gain_vector,
    shrink_factors,
    expand_factors,
    adapter_ranks,
    adapter_storage_slot,
    segment_start,
    segment_adapter,
):
    size = lax.axis_size(AXIS)
    me = lax.axis_index(AXIS).astype(jnp.int32).reshape(1)
    own_rows, model_width = activations.shape
    assert size & (size - 1) == 0 and own_rows & (own_rows - 1) == 0
    tables = (segment_start, segment_adapter, adapter_ranks, adapter_storage_slot)
    scale, to_place, from_place, hot, factor = row_masks(
        me, tables, shrink_factors, own_rows, size
    )

    parts = gather_rows(activations, size, [scale])
    rows, coeff = shrink_rows(parts, factor, scale, to_place, shrink_factors.shape[2])

    bits = [1 << b for b in range(size.bit_length() - 1)]
    units = model_width // (DEPTH_BLOCK // 2)
    cuts = [0] + [(units - units * k // 3) * (DEPTH_BLOCK // 2) for k in (2, 1, 0)]
    mixed = None
    for step, bit in enumerate(bits):
        received = lax.ppermute(coeff, AXIS, flip(size, bit))
        part = step - (len(bits) - 3)
        if part >= 0:
            mixed = mixed_rows(
                rows, (gate_weight, up_weight), mixed, cuts[part], cuts[part + 1], [coeff]
            )
        if bit < bits[-1]:
            coeff = add_coefficients(coeff, received, [] if mixed is None else [mixed])
    hidden = hidden_rows(mixed, coeff, received, expand_factors, from_place, hot)

    half = size * own_rows // 2
    width = model_width // HALVES
    mine, theirs = [None] * HALVES, [None] * HALVES
    for h in range(HALVES):
        term = jnp.dot(
            hidden,
            down_weight[:, h * width : (h + 1) * width],
            preferred_element_type=jnp.float32,
        ).astype(jnp.bfloat16)
        mine[h] = term
        theirs[h] = lax.ppermute(term[half:], AXIS, flip(size, 1))
    halves = scatter_rows(mine, theirs, own_rows, size)
    return finish_rows(halves, activations, norm_gain_vector[None], own_rows)


def solution(mesh):
    return jax.shard_map(
        body,
        mesh=mesh,
        in_specs=(
            P(("groups", "mp"), None),
            P(None, "mp"),
            P(None, "mp"),
            P("mp", None),
            P(),
            P("mp", None, None),
            P(None, None, "mp"),
            P(),
            P(),
            P("groups"),
            P("groups"),
        ),
        out_specs=(P(("groups", "mp"), None), P(("groups", "mp"), None)),
        check_vma=False,
    )
```

```python
import functools

import jax
import jax.numpy as jnp
from jax import lax
from jax.experimental import pallas as pl
from jax.experimental.pallas import tpu as pltpu
from jax.sharding import PartitionSpec as P

adapter_alpha = 32.0
AXIS = "mp"
HALVES = 2
DEPTH_BLOCK = 256
LOADS = 2
VMEM_LIMIT = 12 * 1024 * 1024
LOAD_LIMITS = [mb * 1024 * 1024 for mb in (42, 37)]
STREAM_LIMIT = 34 * 1024 * 1024
STREAM_COST = 4


def chip_at(place, chips):
    if chips == 8:
        return jnp.where(place < 4, 2 * place, 2 * (7 - place) + 1)
    return place


def place_of(chip, chips):
    if chips == 8:
        return jnp.where((chip & 1) == 0, chip >> 1, 7 - (chip >> 1))
    return chip


def ring(size, by):
    chips = size // 2
    order = [0, 2, 4, 6, 7, 5, 3, 1] if chips == 8 else list(range(chips))
    pairs = []
    for place, chip in enumerate(order):
        to = order[(place + by) % chips]
        pairs += [(2 * chip + core, 2 * to + core) for core in range(2)]
    return pairs


def flip(size, bit):
    return [(i, i ^ bit) for i in range(size)]


def row_positions(me, row, own_rows, size):
    chips = size // 2
    block = row // own_rows
    index = block & (chips - 1)
    step = (index + 1) >> 1
    delta = jnp.where((index & 1) == 1, step, -step)
    place = (place_of(me >> 1, chips) - delta + chips) & (chips - 1)
    core = (me & 1) ^ (block // chips)
    return (2 * chip_at(place, chips) + core) * own_rows + (row & (own_rows - 1))


def pick(index, table):
    hot = index == lax.broadcasted_iota(jnp.int32, (1, table.shape[1]), 1)
    return jnp.sum(jnp.where(hot, table, 0), axis=1, keepdims=True)


def row_adapters(position, start, adapters):
    segment = jnp.sum((start <= position).astype(jnp.int32), axis=1, keepdims=True) - 1
    return pick(segment, adapters)


def whole(space=pltpu.VMEM):
    return pl.BlockSpec(memory_space=space)


def call(kernel, out_shape, operands, name, ordered=(), limit=VMEM_LIMIT, **options):
    count = len(operands)

    def run(*refs):
        kernel(*refs[:count], *refs[count + len(ordered) :])

    return pl.pallas_call(
        run,
        out_shape=out_shape,
        in_specs=[
            whole(pltpu.SMEM if operand.ndim == 1 else pltpu.VMEM) for operand in operands
        ]
        + [whole(pl.ANY)] * len(ordered),
        out_specs=jax.tree.map(lambda _: whole(), out_shape),
        compiler_params=pltpu.CompilerParams(vmem_limit_bytes=limit),
        name=name,
        **options,
    )(*operands, *ordered)


def column_half(array, h):
    rows, columns = array.shape
    width = columns // HALVES

    def kernel(ref, out):
        out[...] = ref[:, h * width : (h + 1) * width]

    return call(
        kernel, jax.ShapeDtypeStruct((rows, width), array.dtype), [array], "column_half"
    )


def pass_on(array, ordered):
    def kernel(ref, out):
        out[...] = ref[...]

    return call(
        kernel, jax.ShapeDtypeStruct(array.shape, array.dtype), [array], "pass_on", ordered
    )


def join(pieces, columns, ordered=()):
    rows, width = pieces[0].shape
    across = columns // width

    def kernel(*refs):
        out = refs[-1]
        for i, ref in enumerate(refs[:-1]):
            top, left = i // across * rows, i % across * width
            out[top : top + rows, left : left + width] = ref[...]

    shape = (rows * len(pieces) // across, columns)
    return call(
        kernel, jax.ShapeDtypeStruct(shape, pieces[0].dtype), pieces, "join_pieces", ordered
    )


def gather_rows(own, size, weights, ordered):
    chips = size // 2
    last = chips // 2
    columns = own.shape[1]
    right = left = own
    pieces, loads = [], []
    mine, theirs = [own], []
    for step in range(1, last):
        before = right
        right = lax.ppermute(right, AXIS, ring(size, 1))
        left = lax.ppermute(left, AXIS, ring(size, -1))
        if step == 1:
            theirs.append(lax.ppermute(own, AXIS, flip(size, 1)))
        pieces += [right, left]
        if step <= LOADS:
            loads.append(load_rows(weights, step - 1, [before] if step > 1 else []))
            right = pass_on(right, loads[-1])
    part = join(pieces, columns, ordered)
    mine.append(part)
    theirs.append(lax.ppermute(part, AXIS, flip(size, 1)))
    part = join(
        [
            lax.ppermute(column_half(right, 0), AXIS, ring(size, 1)),
            lax.ppermute(column_half(left, 1), AXIS, ring(size, -1)),
        ],
        columns,
    )
    mine.append(part)
    theirs.append(lax.ppermute(part, AXIS, flip(size, 1)))
    return mine + theirs, loads


def row_masks(me, tables, shrink_factors, own_rows, size):
    batch_rows = own_rows * size
    slots, model_width, rank_limit = shrink_factors.shape
    factor = jnp.swapaxes(shrink_factors, 1, 2).reshape(slots * rank_limit, model_width)
    lengths = [table.shape[0] for table in tables]
    starts = [sum(lengths[:i]) for i in range(len(lengths))]
    adapters = lengths[2]

    def kernel(me_ref, all_tables, factor_in, scale, to_place, from_place, hot, factor_out):
        factor_out[...] = factor_in[...]
        me = me_ref[0]
        start, segment_adapter, ranks, slot_of = (
            all_tables[:, at : at + length] for at, length in zip(starts, lengths)
        )
        row = lax.broadcasted_iota(jnp.int32, (batch_rows, 1), 0)
        column = lax.broadcasted_iota(jnp.int32, (1, batch_rows), 1)
        position = row_positions(me, row, own_rows, size)
        adapter = row_adapters(position, start, segment_adapter)
        rank = pick(adapter, ranks)
        slot = pick(adapter, slot_of) - me * slots
        at = lax.broadcasted_iota(jnp.int32, (1, slots * rank_limit), 1)
        keep = (at // rank_limit == slot) & (at % rank_limit < rank)
        scale[...] = jnp.where(keep, adapter_alpha / rank.astype(jnp.float32), 0.0)
        to_place[...] = (row_positions(me, column, own_rows, size) == row).astype(jnp.bfloat16)
        from_place[...] = (position == column).astype(jnp.bfloat16)
        depth = lax.broadcasted_iota(jnp.int32, (1, adapters * rank_limit), 1)
        hot[...] = (depth // rank_limit == adapter).astype(jnp.bfloat16)

    shapes = (
        jax.ShapeDtypeStruct((batch_rows, slots * rank_limit), jnp.float32),
        jax.ShapeDtypeStruct((batch_rows, batch_rows), jnp.bfloat16),
        jax.ShapeDtypeStruct((batch_rows, batch_rows), jnp.bfloat16),
        jax.ShapeDtypeStruct((batch_rows, adapters * rank_limit), jnp.bfloat16),
        jax.ShapeDtypeStruct(factor.shape, factor.dtype),
    )
    return call(kernel, shapes, [me, jnp.concatenate(tables)[None], factor], "row_masks")


def shrink_rows(parts, factor, scale, to_place, rank_limit):
    model_width = factor.shape[1]
    slots = factor.shape[0] // rank_limit
    batch_rows = to_place.shape[0]
    width = model_width // 8

    def kernel(*refs):
        factor_ref, scale_ref, place_ref, rows_out, coeff_out, total = refs[len(parts) :]

        def columns(k, _):
            at = pl.ds(pl.multiple_of(k * width, width), width)
            top = 0
            for part in refs[: len(parts)]:
                rows_out[top : top + part.shape[0], at] = part[:, at]
                top += part.shape[0]
            product = lax.dot_general(
                rows_out[:, at],
                factor_ref[:, at],
                (((1,), (1,)), ((), ())),
                preferred_element_type=jnp.float32,
            )
            total[...] = jnp.where(k == 0, product, total[...] + product)
            return 0

        lax.fori_loop(0, model_width // width, columns, 0)
        scaled = total[...] * scale_ref[...]
        coeff = scaled[:, :rank_limit]
        for s in range(1, slots):
            coeff = coeff + scaled[:, s * rank_limit : (s + 1) * rank_limit]
        coeff_out[...] = jnp.dot(
            place_ref[...], coeff.astype(jnp.bfloat16), preferred_element_type=jnp.float32
        ).astype(jnp.bfloat16)

    return call(
        kernel,
        (
            jax.ShapeDtypeStruct((batch_rows, model_width), jnp.bfloat16),
            jax.ShapeDtypeStruct((batch_rows, rank_limit), jnp.bfloat16),
        ),
        [*parts, factor, scale, to_place],
        "shrink_rows",
        scratch_shapes=[pltpu.VMEM((batch_rows, slots * rank_limit), jnp.float32)],
        cost_estimate=pl.CostEstimate(
            flops=2 * batch_rows * model_width * slots * rank_limit,
            bytes_accessed=4 * batch_rows * model_width,
            transcendentals=0,
        ),
    )


def add_coefficients(a, b, ordered):
    def kernel(a_ref, b_ref, out):
        out[...] = a_ref[...] + b_ref[...]

    return call(
        kernel, jax.ShapeDtypeStruct(a.shape, a.dtype), [a, b], "add_coefficients", ordered
    )


def lane_tiles(width):
    return -(-width // 128) * 128


def depth_cuts(depth):
    part = -(-3 * depth // 8 // DEPTH_BLOCK) * DEPTH_BLOCK
    return [part * p for p in range(LOADS + 1)] + [depth]


def load_rows(weights, part, ordered):
    depth = weights[0].shape[0]
    first, last = depth_cuts(depth)[part : part + 2]
    widths = [weight.shape[1] for weight in weights]
    if all(width % 128 == 0 for width in widths):
        places = [(0, sum(widths[:w])) for w in range(len(weights))]
        shapes = [(last - first, sum(widths))]
    else:
        places = [(w, 0) for w in range(len(weights))]
        shapes = [(last - first, width) for width in widths]

    def kernel(*refs):
        sources = refs[: len(weights)]
        outs = refs[len(weights) + len(ordered) : -1]
        arrived = refs[-1]
        copies = []
        for i, top in enumerate(range(0, last - first, DEPTH_BLOCK)):
            for w, (out, left) in enumerate(places):
                copy = pltpu.make_async_copy(
                    sources[w].at[first + top : first + top + DEPTH_BLOCK, :],
                    outs[out].at[top : top + DEPTH_BLOCK, left : left + widths[w]],
                    arrived.at[i, w],
                )
                copy.start()
                copies.append(copy)
        for copy in copies:
            copy.wait()

    return pl.pallas_call(
        kernel,
        out_shape=[jax.ShapeDtypeStruct(shape, weights[0].dtype) for shape in shapes],
        in_specs=[whole(pltpu.HBM)] * len(weights) + [whole(pl.ANY)] * len(ordered),
        out_specs=[whole()] * len(shapes),
        scratch_shapes=[
            pltpu.SemaphoreType.DMA(((last - first) // DEPTH_BLOCK, len(weights)))
        ],
        compiler_params=pltpu.CompilerParams(vmem_limit_bytes=LOAD_LIMITS[part]),
        cost_estimate=pl.CostEstimate(
            flops=0, bytes_accessed=4 * (last - first) * sum(widths), transcendentals=0
        ),
        name="load_rows",
    )(*weights, *ordered)


def mixed_rows(rows, loaded, part, before, ordered):
    batch_rows, depth = rows.shape
    first, last = depth_cuts(depth)[part : part + 2]
    widths = [block.shape[1] for block in loaded]
    lefts = [sum(lane_tiles(width) for width in widths[:w]) for w in range(len(widths))]
    width = sum(lane_tiles(width) for width in widths)

    def kernel(rows_ref, *refs):
        out = refs[-1]
        for block, left, wide in zip(refs, lefts, widths):
            columns = slice(left, left + wide)
            product = jnp.dot(
                rows_ref[:, first:last], block[...], preferred_element_type=jnp.float32
            )
            if before is not None:
                product = refs[len(widths)][:, columns] + product
            out[:, columns] = product

    return call(
        kernel,
        jax.ShapeDtypeStruct((batch_rows, width), jnp.float32),
        [rows, *loaded] + ([] if before is None else [before]),
        "mixed_rows",
        ordered,
        cost_estimate=pl.CostEstimate(
            flops=2 * batch_rows * (last - first) * width,
            bytes_accessed=2 * (last - first) * width,
            transcendentals=0,
        ),
    )


def stream_rows(rows, weights, before, first, last, ordered):
    batch_rows = rows.shape[0]
    widths = [weight.shape[1] for weight in weights]
    lefts = [sum(lane_tiles(width) for width in widths[:w]) for w in range(len(weights))]
    width = sum(lane_tiles(width) for width in widths)
    if width == sum(widths):
        buffer_of, offsets = [0] * len(weights), lefts
        products = [(0, width)]
    else:
        buffer_of, offsets = list(range(len(weights))), [0] * len(weights)
        products = list(zip(lefts, widths))
    blocks = []
    at = first
    while at < last:
        depth = min(4 * DEPTH_BLOCK if blocks else 2 * DEPTH_BLOCK, last - at)
        blocks.append((at, depth))
        at += depth

    def kernel(rows_ref, *refs):
        sources = refs[: len(weights)]
        arrived = refs[-1]
        buffers = refs[-1 - len(products) : -1]
        out = refs[-2 - len(products)]
        copies = []
        for b, (at, depth) in enumerate(blocks):
            copies.append([])
            half = depth // 2
            for p in range(2):
                for w, source in enumerate(sources):
                    top = at - first + p * half
                    copy = pltpu.make_async_copy(
                        source.at[at + p * half : at + (p + 1) * half, :],
                        buffers[buffer_of[w]].at[
                            top : top + half, offsets[w] : offsets[w] + widths[w]
                        ],
                        arrived.at[b, 2 * w + p],
                    )
                    copy.start()
                    copies[-1].append(copy)
        for (at, depth), group in zip(blocks, copies):
            for copy in group:
                copy.wait()
            for (left, wide), buffer in zip(products, buffers):
                columns = slice(left, left + wide)
                product = jnp.dot(
                    rows_ref[:, at : at + depth],
                    buffer[at - first : at - first + depth, :],
                    preferred_element_type=jnp.float32,
                )
                if at > first:
                    product = out[:, columns] + product
                elif before is not None:
                    product = refs[len(weights)][:, columns] + product
                out[:, columns] = product

    return pl.pallas_call(
        kernel,
        out_shape=jax.ShapeDtypeStruct((batch_rows, width), jnp.float32),
        in_specs=[whole()]
        + [whole(pltpu.HBM)] * len(weights)
        + [whole()] * (before is not None)
        + [whole(pl.ANY)] * len(ordered),
        out_specs=whole(),
        scratch_shapes=[pltpu.VMEM((last - first, wide), rows.dtype) for _, wide in products]
        + [pltpu.SemaphoreType.DMA((len(blocks), 2 * len(weights)))],
        compiler_params=pltpu.CompilerParams(vmem_limit_bytes=STREAM_LIMIT),
        cost_estimate=pl.CostEstimate(
            flops=2 * batch_rows * (last - first) * width,
            bytes_accessed=STREAM_COST * (last - first) * width,
            transcendentals=0,
        ),
        name="stream_rows",
    )(rows, *weights, *([] if before is None else [before]), *ordered)


def hidden_kernel(coeff, recv, from_place, hot, expand, mixed, out, spread):
    rank_limit = coeff.shape[1]
    own = jnp.dot(
        from_place[...], coeff[...] + recv[...], preferred_element_type=jnp.float32
    ).astype(jnp.bfloat16)
    pair = jnp.concatenate([own, own], axis=1)
    for p in range(spread.shape[1] // (2 * rank_limit)):
        at = slice(p * 2 * rank_limit, (p + 1) * 2 * rank_limit)
        spread[:, at] = hot[:, at] * pair
    lora = jnp.dot(spread[...], expand[...], preferred_element_type=jnp.float32)
    width = out.shape[1]
    value = mixed[:, :width]
    total = mixed[:, lane_tiles(width) : lane_tiles(width) + width] + lora
    out[...] = (value / (1.0 + jnp.exp(-value)) * total).astype(jnp.bfloat16)


def hidden_rows(mixed, coeff, recv, expand_factors, from_place, hot):
    adapters, rank_limit, width = expand_factors.shape
    batch_rows = mixed.shape[0]
    expand = expand_factors.reshape(adapters * rank_limit, width)
    return call(
        hidden_kernel,
        jax.ShapeDtypeStruct((batch_rows, width), jnp.bfloat16),
        [coeff, recv, from_place, hot, expand, mixed],
        "hidden_rows",
        scratch_shapes=[pltpu.VMEM((batch_rows, adapters * rank_limit), jnp.bfloat16)],
        cost_estimate=pl.CostEstimate(
            flops=2 * batch_rows * adapters * rank_limit * width,
            bytes_accessed=2 * adapters * rank_limit * width,
            transcendentals=batch_rows * width,
        ),
    )


def add_blocks(sides, own_rows, ordered):
    operands, shapes = [], []
    for mine, theirs, _, arrived in sides:
        operands += [mine, theirs] + ([] if arrived is None else [arrived])
        shapes.append(jax.ShapeDtypeStruct((own_rows, mine.shape[1]), jnp.bfloat16))

    def kernel(*refs):
        refs = list(refs)
        outs = refs[-len(sides) :]
        for (_, _, index, arrived), out in zip(sides, outs):
            at = slice(index * own_rows, (index + 1) * own_rows)
            total = refs.pop(0)[at, :].astype(jnp.float32)
            total = total + refs.pop(0)[at, :].astype(jnp.float32)
            if arrived is not None:
                total = total + refs.pop(0)[...].astype(jnp.float32)
            out[...] = total.astype(jnp.bfloat16)

    return call(kernel, tuple(shapes), operands, "add_blocks", ordered)


def scatter_rows(mine, theirs, own_rows, size):
    chips = size // 2
    last = chips // 2
    right, left = [None] * HALVES, [None] * HALVES
    ordered = []
    for turn in range(last):
        for h in range(HALVES):
            steps_right = last - turn - (h == 1)
            steps_left = last - turn - (h == 0)
            sides = []
            if steps_right > 0:
                index = min(2 * steps_right, chips - 1)
                sides.append((right, 1, index))
            if steps_left > 0:
                sides.append((left, -1, 2 * steps_left - 1))
            if h == 1:
                sides.reverse()
            sums = add_blocks(
                [(mine[h], theirs[h], index, chain[h]) for chain, _, index in sides],
                own_rows,
                ordered,
            )
            ordered = [sums[0]]
            for (chain, by, _), value in zip(sides, sums):
                chain[h] = lax.ppermute(value, AXIS, ring(size, by))
    return list(zip(mine, theirs, right, left))


def finish_rows(halves, activations, gain, own_rows):
    width = activations.shape[1] // HALVES

    def kernel(*refs):
        refs, (act, gain_ref, block_out, normed, stream) = refs[:-5], refs[-5:]
        square = jnp.zeros((own_rows, 1), jnp.float32)
        for h in range(HALVES):
            mine, theirs, right, left = refs[4 * h : 4 * h + 4]
            at = slice(h * width, (h + 1) * width)
            total = act[:, at].astype(jnp.float32)
            for ref in (mine, theirs):
                total = total + ref[:own_rows, :].astype(jnp.float32)
            for ref in (right, left):
                total = total + ref[...].astype(jnp.float32)
            stream[:, at] = total
            block_out[:, at] = total.astype(jnp.bfloat16)
            square = square + jnp.sum(total * total, axis=1, keepdims=True)
        scale = lax.rsqrt(square * (1.0 / act.shape[1]) + 1e-05)
        normed[...] = (stream[...] * scale * gain_ref[...].astype(jnp.float32)).astype(
            jnp.bfloat16
        )

    out = jax.ShapeDtypeStruct(activations.shape, jnp.bfloat16)
    return call(
        kernel,
        (out, out),
        [array for half in halves for array in half] + [activations, gain],
        "finish_rows",
        scratch_shapes=[pltpu.VMEM(activations.shape, jnp.float32)],
    )


def body(
    activations,
    gate_weight,
    up_weight,
    down_weight,
    norm_gain_vector,
    shrink_factors,
    expand_factors,
    adapter_ranks,
    adapter_storage_slot,
    segment_start,
    segment_adapter,
):
    size = lax.axis_size(AXIS)
    me = lax.axis_index(AXIS).astype(jnp.int32).reshape(1)
    own_rows, model_width = activations.shape
    assert size & (size - 1) == 0 and own_rows & (own_rows - 1) == 0
    tables = (segment_start, segment_adapter, adapter_ranks, adapter_storage_slot)
    scale, to_place, from_place, hot, factor = row_masks(
        me, tables, shrink_factors, own_rows, size
    )

    parts, loads = gather_rows(activations, size, (gate_weight, up_weight), [scale])
    rows, coeff = shrink_rows(parts, factor, scale, to_place, shrink_factors.shape[2])

    bits = [1 << b for b in range(size.bit_length() - 1)]
    mixed = None
    for step, bit in enumerate(bits):
        received = lax.ppermute(coeff, AXIS, flip(size, bit))
        part = step - (len(bits) - LOADS - 1)
        if part == LOADS:
            cuts = depth_cuts(model_width)
            mixed = stream_rows(
                rows, (gate_weight, up_weight), mixed, cuts[part], cuts[part + 1], [coeff]
            )
        elif part >= 0:
            mixed = mixed_rows(rows, loads[part], part, mixed, [coeff])
        if bit < bits[-1]:
            coeff = add_coefficients(coeff, received, [] if mixed is None else [mixed])
    hidden = hidden_rows(mixed, coeff, received, expand_factors, from_place, hot)

    half = size * own_rows // 2
    width = model_width // HALVES
    mine, theirs = [None] * HALVES, [None] * HALVES
    for h in range(HALVES):
        term = jnp.dot(
            hidden,
            down_weight[:, h * width : (h + 1) * width],
            preferred_element_type=jnp.float32,
        ).astype(jnp.bfloat16)
        mine[h] = term
        theirs[h] = lax.ppermute(term[half:], AXIS, flip(size, 1))
    halves = scatter_rows(mine, theirs, own_rows, size)
    return finish_rows(halves, activations, norm_gain_vector[None], own_rows)


def solution(mesh):
    return jax.shard_map(
        body,
        mesh=mesh,
        in_specs=(
            P(("groups", "mp"), None),
            P(None, "mp"),
            P(None, "mp"),
            P("mp", None),
            P(),
            P("mp", None, None),
            P(None, None, "mp"),
            P(),
            P(),
            P("groups"),
            P("groups"),
        ),
        out_specs=(P(("groups", "mp"), None), P(("groups", "mp"), None)),
        check_vma=False,
    )
```

```python
import functools

import jax
import jax.numpy as jnp
from jax import lax
from jax.experimental import pallas as pl
from jax.experimental.pallas import tpu as pltpu
from jax.sharding import PartitionSpec as P

adapter_alpha = 32.0
AXIS = "mp"
HALVES = 2
DEPTH_BLOCK = 256
LOADS = 2
VMEM_LIMIT = 12 * 1024 * 1024
LOAD_LIMITS = [mb * 1024 * 1024 for mb in (42, 37)]
STREAM_LIMIT = 34 * 1024 * 1024
STREAM_COST = 4


def chip_at(place, chips):
    if chips == 8:
        return jnp.where(place < 4, 2 * place, 2 * (7 - place) + 1)
    return place


def place_of(chip, chips):
    if chips == 8:
        return jnp.where((chip & 1) == 0, chip >> 1, 7 - (chip >> 1))
    return chip


def ring(size, by):
    chips = size // 2
    order = [0, 2, 4, 6, 7, 5, 3, 1] if chips == 8 else list(range(chips))
    pairs = []
    for place, chip in enumerate(order):
        to = order[(place + by) % chips]
        pairs += [(2 * chip + core, 2 * to + core) for core in range(2)]
    return pairs


def flip(size, bit):
    return [(i, i ^ bit) for i in range(size)]


def row_positions(me, row, own_rows, size):
    chips = size // 2
    block = row // own_rows
    index = block & (chips - 1)
    step = (index + 1) >> 1
    delta = jnp.where((index & 1) == 1, step, -step)
    place = (place_of(me >> 1, chips) - delta + chips) & (chips - 1)
    core = (me & 1) ^ (block // chips)
    return (2 * chip_at(place, chips) + core) * own_rows + (row & (own_rows - 1))


def pick(index, table):
    hot = index == lax.broadcasted_iota(jnp.int32, (1, table.shape[1]), 1)
    return jnp.sum(jnp.where(hot, table, 0), axis=1, keepdims=True)


def row_adapters(position, start, adapters):
    segment = jnp.sum((start <= position).astype(jnp.int32), axis=1, keepdims=True) - 1
    return pick(segment, adapters)


def whole(space=pltpu.VMEM):
    return pl.BlockSpec(memory_space=space)


def call(kernel, out_shape, operands, name, ordered=(), limit=VMEM_LIMIT, **options):
    count = len(operands)

    def run(*refs):
        kernel(*refs[:count], *refs[count + len(ordered) :])

    return pl.pallas_call(
        run,
        out_shape=out_shape,
        in_specs=[
            whole(pltpu.SMEM if operand.ndim == 1 else pltpu.VMEM) for operand in operands
        ]
        + [whole(pl.ANY)] * len(ordered),
        out_specs=jax.tree.map(lambda _: whole(), out_shape),
        compiler_params=pltpu.CompilerParams(vmem_limit_bytes=limit),
        name=name,
        **options,
    )(*operands, *ordered)


def column_half(array, h):
    rows, columns = array.shape
    width = columns // HALVES

    def kernel(ref, out):
        out[...] = ref[:, h * width : (h + 1) * width]

    return call(
        kernel, jax.ShapeDtypeStruct((rows, width), array.dtype), [array], "column_half"
    )


def pass_on(array, ordered):
    def kernel(ref, out):
        out[...] = ref[...]

    return call(
        kernel, jax.ShapeDtypeStruct(array.shape, array.dtype), [array], "pass_on", ordered
    )


def join(pieces, columns, ordered=()):
    rows, width = pieces[0].shape
    across = columns // width

    def kernel(*refs):
        out = refs[-1]
        for i, ref in enumerate(refs[:-1]):
            top, left = i // across * rows, i % across * width
            out[top : top + rows, left : left + width] = ref[...]

    shape = (rows * len(pieces) // across, columns)
    return call(
        kernel, jax.ShapeDtypeStruct(shape, pieces[0].dtype), pieces, "join_pieces", ordered
    )


def gather_rows(own, size, weights, ordered):
    chips = size // 2
    last = chips // 2
    columns = own.shape[1]
    right = left = own
    pieces, loads = [], []
    mine, theirs = [own], []
    for step in range(1, last):
        before = right
        right = lax.ppermute(right, AXIS, ring(size, 1))
        left = lax.ppermute(left, AXIS, ring(size, -1))
        if step == 1:
            theirs.append(lax.ppermute(own, AXIS, flip(size, 1)))
        pieces += [right, left]
        if step <= LOADS:
            loads.append(load_rows(weights, step - 1, [before] if step > 1 else []))
            right = pass_on(right, loads[-1])
    part = join(pieces, columns, ordered)
    mine.append(part)
    theirs.append(lax.ppermute(part, AXIS, flip(size, 1)))
    part = join(
        [
            lax.ppermute(column_half(right, 0), AXIS, ring(size, 1)),
            lax.ppermute(column_half(left, 1), AXIS, ring(size, -1)),
        ],
        columns,
    )
    mine.append(part)
    theirs.append(lax.ppermute(part, AXIS, flip(size, 1)))
    return mine + theirs, loads


def row_masks(tables, shrink_factors, own_rows, size):
    batch_rows = own_rows * size
    slots, model_width, rank_limit = shrink_factors.shape
    factor = jnp.swapaxes(shrink_factors, 1, 2).reshape(slots * rank_limit, model_width)
    adapters = tables[2].shape[0]

    def kernel(*refs):
        start, segment_adapter, ranks, slot_of = (ref[...] for ref in refs[:4])
        factor_in, scale, to_place, from_place, hot, factor_out = refs[4:]
        factor_out[...] = factor_in[...]
        me = lax.axis_index(AXIS)
        row = lax.broadcasted_iota(jnp.int32, (batch_rows, 1), 0)
        column = lax.broadcasted_iota(jnp.int32, (1, batch_rows), 1)
        position = row_positions(me, row, own_rows, size)
        adapter = row_adapters(position, start, segment_adapter)
        rank = pick(adapter, ranks)
        slot = pick(adapter, slot_of) - me * slots
        at = lax.broadcasted_iota(jnp.int32, (1, slots * rank_limit), 1)
        keep = (at // rank_limit == slot) & (at % rank_limit < rank)
        scale[...] = jnp.where(keep, adapter_alpha / rank.astype(jnp.float32), 0.0)
        to_place[...] = (row_positions(me, column, own_rows, size) == row).astype(jnp.bfloat16)
        from_place[...] = (position == column).astype(jnp.bfloat16)
        depth = lax.broadcasted_iota(jnp.int32, (1, adapters * rank_limit), 1)
        hot[...] = (depth // rank_limit == adapter).astype(jnp.bfloat16)

    shapes = (
        jax.ShapeDtypeStruct((batch_rows, slots * rank_limit), jnp.float32),
        jax.ShapeDtypeStruct((batch_rows, batch_rows), jnp.bfloat16),
        jax.ShapeDtypeStruct((batch_rows, batch_rows), jnp.bfloat16),
        jax.ShapeDtypeStruct((batch_rows, adapters * rank_limit), jnp.bfloat16),
        jax.ShapeDtypeStruct(factor.shape, factor.dtype),
    )
    return call(kernel, shapes, [*(table[None] for table in tables), factor], "row_masks")


def shrink_rows(parts, factor, scale, to_place, rank_limit):
    model_width = factor.shape[1]
    slots = factor.shape[0] // rank_limit
    batch_rows = to_place.shape[0]
    width = model_width // 8

    def kernel(*refs):
        factor_ref, scale_ref, place_ref, rows_out, coeff_out, total = refs[len(parts) :]

        def columns(k, _):
            at = pl.ds(pl.multiple_of(k * width, width), width)
            top = 0
            for part in refs[: len(parts)]:
                rows_out[top : top + part.shape[0], at] = part[:, at]
                top += part.shape[0]
            product = lax.dot_general(
                rows_out[:, at],
                factor_ref[:, at],
                (((1,), (1,)), ((), ())),
                preferred_element_type=jnp.float32,
            )
            total[...] = jnp.where(k == 0, product, total[...] + product)
            return 0

        lax.fori_loop(0, model_width // width, columns, 0)
        scaled = total[...] * scale_ref[...]
        coeff = scaled[:, :rank_limit]
        for s in range(1, slots):
            coeff = coeff + scaled[:, s * rank_limit : (s + 1) * rank_limit]
        coeff_out[...] = jnp.dot(
            place_ref[...], coeff.astype(jnp.bfloat16), preferred_element_type=jnp.float32
        ).astype(jnp.bfloat16)

    return call(
        kernel,
        (
            jax.ShapeDtypeStruct((batch_rows, model_width), jnp.bfloat16),
            jax.ShapeDtypeStruct((batch_rows, rank_limit), jnp.bfloat16),
        ),
        [*parts, factor, scale, to_place],
        "shrink_rows",
        scratch_shapes=[pltpu.VMEM((batch_rows, slots * rank_limit), jnp.float32)],
        cost_estimate=pl.CostEstimate(
            flops=2 * batch_rows * model_width * slots * rank_limit,
            bytes_accessed=4 * batch_rows * model_width,
            transcendentals=0,
        ),
    )


def add_coefficients(a, b, ordered):
    def kernel(a_ref, b_ref, out):
        out[...] = a_ref[...] + b_ref[...]

    return call(
        kernel, jax.ShapeDtypeStruct(a.shape, a.dtype), [a, b], "add_coefficients", ordered
    )


def lane_tiles(width):
    return -(-width // 128) * 128


def depth_cuts(depth):
    part = -(-3 * depth // 8 // DEPTH_BLOCK) * DEPTH_BLOCK
    return [part * p for p in range(LOADS + 1)] + [depth]


def load_rows(weights, part, ordered):
    depth = weights[0].shape[0]
    first, last = depth_cuts(depth)[part : part + 2]
    widths = [weight.shape[1] for weight in weights]
    if all(width % 128 == 0 for width in widths):
        places = [(0, sum(widths[:w])) for w in range(len(weights))]
        shapes = [(last - first, sum(widths))]
    else:
        places = [(w, 0) for w in range(len(weights))]
        shapes = [(last - first, width) for width in widths]

    def kernel(*refs):
        sources = refs[: len(weights)]
        outs = refs[len(weights) + len(ordered) : -1]
        arrived = refs[-1]
        copies = []
        for i, top in enumerate(range(0, last - first, DEPTH_BLOCK)):
            for w, (out, left) in enumerate(places):
                copy = pltpu.make_async_copy(
                    sources[w].at[first + top : first + top + DEPTH_BLOCK, :],
                    outs[out].at[top : top + DEPTH_BLOCK, left : left + widths[w]],
                    arrived.at[i, w],
                )
                copy.start()
                copies.append(copy)
        for copy in copies:
            copy.wait()

    return pl.pallas_call(
        kernel,
        out_shape=[jax.ShapeDtypeStruct(shape, weights[0].dtype) for shape in shapes],
        in_specs=[whole(pltpu.HBM)] * len(weights) + [whole(pl.ANY)] * len(ordered),
        out_specs=[whole()] * len(shapes),
        scratch_shapes=[
            pltpu.SemaphoreType.DMA(((last - first) // DEPTH_BLOCK, len(weights)))
        ],
        compiler_params=pltpu.CompilerParams(vmem_limit_bytes=LOAD_LIMITS[part]),
        cost_estimate=pl.CostEstimate(
            flops=0, bytes_accessed=4 * (last - first) * sum(widths), transcendentals=0
        ),
        name="load_rows",
    )(*weights, *ordered)


def mixed_rows(rows, loaded, part, before, ordered):
    batch_rows, depth = rows.shape
    first, last = depth_cuts(depth)[part : part + 2]
    widths = [block.shape[1] for block in loaded]
    lefts = [sum(lane_tiles(width) for width in widths[:w]) for w in range(len(widths))]
    width = sum(lane_tiles(width) for width in widths)

    def kernel(rows_ref, *refs):
        out = refs[-1]
        for block, left, wide in zip(refs, lefts, widths):
            columns = slice(left, left + wide)
            product = jnp.dot(
                rows_ref[:, first:last], block[...], preferred_element_type=jnp.float32
            )
            if before is not None:
                product = refs[len(widths)][:, columns] + product
            out[:, columns] = product

    return call(
        kernel,
        jax.ShapeDtypeStruct((batch_rows, width), jnp.float32),
        [rows, *loaded] + ([] if before is None else [before]),
        "mixed_rows",
        ordered,
        cost_estimate=pl.CostEstimate(
            flops=2 * batch_rows * (last - first) * width,
            bytes_accessed=2 * (last - first) * width,
            transcendentals=0,
        ),
    )


def stream_rows(rows, weights, before, first, last, ordered):
    batch_rows = rows.shape[0]
    widths = [weight.shape[1] for weight in weights]
    lefts = [sum(lane_tiles(width) for width in widths[:w]) for w in range(len(weights))]
    width = sum(lane_tiles(width) for width in widths)
    if width == sum(widths):
        buffer_of, offsets = [0] * len(weights), lefts
        products = [(0, width)]
    else:
        buffer_of, offsets = list(range(len(weights))), [0] * len(weights)
        products = list(zip(lefts, widths))
    blocks = []
    at = first
    while at < last:
        depth = min(4 * DEPTH_BLOCK if blocks else 2 * DEPTH_BLOCK, last - at)
        blocks.append((at, depth))
        at += depth

    def kernel(rows_ref, *refs):
        sources = refs[: len(weights)]
        arrived = refs[-1]
        buffers = refs[-1 - len(products) : -1]
        out = refs[-2 - len(products)]
        copies = []
        for b, (at, depth) in enumerate(blocks):
            copies.append([])
            half = depth // 2
            for p in range(2):
                for w, source in enumerate(sources):
                    top = at - first + p * half
                    copy = pltpu.make_async_copy(
                        source.at[at + p * half : at + (p + 1) * half, :],
                        buffers[buffer_of[w]].at[
                            top : top + half, offsets[w] : offsets[w] + widths[w]
                        ],
                        arrived.at[b, 2 * w + p],
                    )
                    copy.start()
                    copies[-1].append(copy)
        for (at, depth), group in zip(blocks, copies):
            for copy in group:
                copy.wait()
            for (left, wide), buffer in zip(products, buffers):
                columns = slice(left, left + wide)
                product = jnp.dot(
                    rows_ref[:, at : at + depth],
                    buffer[at - first : at - first + depth, :],
                    preferred_element_type=jnp.float32,
                )
                if at > first:
                    product = out[:, columns] + product
                elif before is not None:
                    product = refs[len(weights)][:, columns] + product
                out[:, columns] = product

    return pl.pallas_call(
        kernel,
        out_shape=jax.ShapeDtypeStruct((batch_rows, width), jnp.float32),
        in_specs=[whole()]
        + [whole(pltpu.HBM)] * len(weights)
        + [whole()] * (before is not None)
        + [whole(pl.ANY)] * len(ordered),
        out_specs=whole(),
        scratch_shapes=[pltpu.VMEM((last - first, wide), rows.dtype) for _, wide in products]
        + [pltpu.SemaphoreType.DMA((len(blocks), 2 * len(weights)))],
        compiler_params=pltpu.CompilerParams(vmem_limit_bytes=STREAM_LIMIT),
        cost_estimate=pl.CostEstimate(
            flops=2 * batch_rows * (last - first) * width,
            bytes_accessed=STREAM_COST * (last - first) * width,
            transcendentals=0,
        ),
        name="stream_rows",
    )(rows, *weights, *([] if before is None else [before]), *ordered)


def hidden_kernel(coeff, recv, from_place, hot, expand, mixed, out, spread):
    rank_limit = coeff.shape[1]
    own = jnp.dot(
        from_place[...], coeff[...] + recv[...], preferred_element_type=jnp.float32
    ).astype(jnp.bfloat16)
    pair = jnp.concatenate([own, own], axis=1)
    for p in range(spread.shape[1] // (2 * rank_limit)):
        at = slice(p * 2 * rank_limit, (p + 1) * 2 * rank_limit)
        spread[:, at] = hot[:, at] * pair
    lora = jnp.dot(spread[...], expand[...], preferred_element_type=jnp.float32)
    width = out.shape[1]
    value = mixed[:, :width]
    total = mixed[:, lane_tiles(width) : lane_tiles(width) + width] + lora
    out[...] = (value / (1.0 + jnp.exp(-value)) * total).astype(jnp.bfloat16)


def hidden_rows(mixed, coeff, recv, expand_factors, from_place, hot):
    adapters, rank_limit, width = expand_factors.shape
    batch_rows = mixed.shape[0]
    expand = expand_factors.reshape(adapters * rank_limit, width)
    return call(
        hidden_kernel,
        jax.ShapeDtypeStruct((batch_rows, width), jnp.bfloat16),
        [coeff, recv, from_place, hot, expand, mixed],
        "hidden_rows",
        scratch_shapes=[pltpu.VMEM((batch_rows, adapters * rank_limit), jnp.bfloat16)],
        cost_estimate=pl.CostEstimate(
            flops=2 * batch_rows * adapters * rank_limit * width,
            bytes_accessed=2 * adapters * rank_limit * width,
            transcendentals=batch_rows * width,
        ),
    )


def add_blocks(sides, own_rows, ordered):
    operands, shapes = [], []
    for mine, theirs, _, arrived in sides:
        operands += [mine, theirs] + ([] if arrived is None else [arrived])
        shapes.append(jax.ShapeDtypeStruct((own_rows, mine.shape[1]), jnp.bfloat16))

    def kernel(*refs):
        refs = list(refs)
        outs = refs[-len(sides) :]
        for (_, _, index, arrived), out in zip(sides, outs):
            at = slice(index * own_rows, (index + 1) * own_rows)
            total = refs.pop(0)[at, :].astype(jnp.float32)
            total = total + refs.pop(0)[at, :].astype(jnp.float32)
            if arrived is not None:
                total = total + refs.pop(0)[...].astype(jnp.float32)
            out[...] = total.astype(jnp.bfloat16)

    return call(kernel, tuple(shapes), operands, "add_blocks", ordered)


def scatter_rows(mine, theirs, own_rows, size):
    chips = size // 2
    last = chips // 2
    right, left = [None] * HALVES, [None] * HALVES
    ordered = []
    for turn in range(last):
        for h in range(HALVES):
            steps_right = last - turn - (h == 1)
            steps_left = last - turn - (h == 0)
            sides = []
            if steps_right > 0:
                index = min(2 * steps_right, chips - 1)
                sides.append((right, 1, index))
            if steps_left > 0:
                sides.append((left, -1, 2 * steps_left - 1))
            if h == 1:
                sides.reverse()
            sums = add_blocks(
                [(mine[h], theirs[h], index, chain[h]) for chain, _, index in sides],
                own_rows,
                ordered,
            )
            ordered = [sums[0]]
            for (chain, by, _), value in zip(sides, sums):
                chain[h] = lax.ppermute(value, AXIS, ring(size, by))
    return list(zip(mine, theirs, right, left))


def finish_rows(halves, activations, gain, own_rows):
    width = activations.shape[1] // HALVES

    def kernel(*refs):
        refs, (act, gain_ref, block_out, normed, stream) = refs[:-5], refs[-5:]
        square = jnp.zeros((own_rows, 1), jnp.float32)
        for h in range(HALVES):
            mine, theirs, right, left = refs[4 * h : 4 * h + 4]
            at = slice(h * width, (h + 1) * width)
            total = act[:, at].astype(jnp.float32)
            for ref in (mine, theirs):
                total = total + ref[:own_rows, :].astype(jnp.float32)
            for ref in (right, left):
                total = total + ref[...].astype(jnp.float32)
            stream[:, at] = total
            block_out[:, at] = total.astype(jnp.bfloat16)
            square = square + jnp.sum(total * total, axis=1, keepdims=True)
        scale = lax.rsqrt(square * (1.0 / act.shape[1]) + 1e-05)
        normed[...] = (stream[...] * scale * gain_ref[...].astype(jnp.float32)).astype(
            jnp.bfloat16
        )

    out = jax.ShapeDtypeStruct(activations.shape, jnp.bfloat16)
    return call(
        kernel,
        (out, out),
        [array for half in halves for array in half] + [activations, gain],
        "finish_rows",
        scratch_shapes=[pltpu.VMEM(activations.shape, jnp.float32)],
    )


def body(
    activations,
    gate_weight,
    up_weight,
    down_weight,
    norm_gain_vector,
    shrink_factors,
    expand_factors,
    adapter_ranks,
    adapter_storage_slot,
    segment_start,
    segment_adapter,
):
    size = lax.axis_size(AXIS)
    own_rows, model_width = activations.shape
    assert size & (size - 1) == 0 and own_rows & (own_rows - 1) == 0
    tables = (segment_start, segment_adapter, adapter_ranks, adapter_storage_slot)
    scale, to_place, from_place, hot, factor = row_masks(
        tables, shrink_factors, own_rows, size
    )

    parts, loads = gather_rows(activations, size, (gate_weight, up_weight), [scale])
    rows, coeff = shrink_rows(parts, factor, scale, to_place, shrink_factors.shape[2])

    bits = [1 << b for b in range(size.bit_length() - 1)]
    mixed = None
    for step, bit in enumerate(bits):
        received = lax.ppermute(coeff, AXIS, flip(size, bit))
        part = step - (len(bits) - LOADS - 1)
        if part == LOADS:
            cuts = depth_cuts(model_width)
            mixed = stream_rows(
                rows, (gate_weight, up_weight), mixed, cuts[part], cuts[part + 1], [coeff]
            )
        elif part >= 0:
            mixed = mixed_rows(rows, loads[part], part, mixed, [coeff])
        if bit < bits[-1]:
            coeff = add_coefficients(coeff, received, [] if mixed is None else [mixed])
    hidden = hidden_rows(mixed, coeff, received, expand_factors, from_place, hot)

    half = size * own_rows // 2
    width = model_width // HALVES
    mine, theirs = [None] * HALVES, [None] * HALVES
    for h in range(HALVES):
        term = jnp.dot(
            hidden,
            down_weight[:, h * width : (h + 1) * width],
            preferred_element_type=jnp.float32,
        ).astype(jnp.bfloat16)
        mine[h] = term
        theirs[h] = lax.ppermute(term[half:], AXIS, flip(size, 1))
    halves = scatter_rows(mine, theirs, own_rows, size)
    return finish_rows(halves, activations, norm_gain_vector[None], own_rows)


def solution(mesh):
    return jax.shard_map(
        body,
        mesh=mesh,
        in_specs=(
            P(("groups", "mp"), None),
            P(None, "mp"),
            P(None, "mp"),
            P("mp", None),
            P(),
            P("mp", None, None),
            P(None, None, "mp"),
            P(),
            P(),
            P("groups"),
            P("groups"),
        ),
        out_specs=(P(("groups", "mp"), None), P(("groups", "mp"), None)),
        check_vma=False,
    )
```

```python
import functools

import jax
import jax.numpy as jnp
from jax import lax
from jax.experimental import pallas as pl
from jax.experimental.pallas import tpu as pltpu
from jax.sharding import PartitionSpec as P

adapter_alpha = 32.0
AXIS = "mp"
HALVES = 2
DEPTH_BLOCK = 256
LOADS = 2
VMEM_LIMIT = 12 * 1024 * 1024
LOAD_LIMITS = [mb * 1024 * 1024 for mb in (42, 37)]
STREAM_LIMIT = 34 * 1024 * 1024
STREAM_COST = 4


def chip_at(place, chips):
    if chips == 8:
        return jnp.where(place < 4, 2 * place, 2 * (7 - place) + 1)
    return place


def place_of(chip, chips):
    if chips == 8:
        return jnp.where((chip & 1) == 0, chip >> 1, 7 - (chip >> 1))
    return chip


def ring(size, by):
    chips = size // 2
    order = [0, 2, 4, 6, 7, 5, 3, 1] if chips == 8 else list(range(chips))
    pairs = []
    for place, chip in enumerate(order):
        to = order[(place + by) % chips]
        pairs += [(2 * chip + core, 2 * to + core) for core in range(2)]
    return pairs


def flip(size, bit):
    return [(i, i ^ bit) for i in range(size)]


def row_positions(me, row, own_rows, size):
    chips = size // 2
    block = row // own_rows
    index = block & (chips - 1)
    step = (index + 1) >> 1
    delta = jnp.where((index & 1) == 1, step, -step)
    place = (place_of(me >> 1, chips) - delta + chips) & (chips - 1)
    core = (me & 1) ^ (block // chips)
    return (2 * chip_at(place, chips) + core) * own_rows + (row & (own_rows - 1))


def pick(index, table):
    hot = index == lax.broadcasted_iota(jnp.int32, (1, table.shape[1]), 1)
    return jnp.sum(jnp.where(hot, table, 0), axis=1, keepdims=True)


def row_adapters(position, start, adapters):
    segment = jnp.sum((start <= position).astype(jnp.int32), axis=1, keepdims=True) - 1
    return pick(segment, adapters)


def whole(space=pltpu.VMEM):
    return pl.BlockSpec(memory_space=space)


def call(kernel, out_shape, operands, name, ordered=(), limit=VMEM_LIMIT, **options):
    count = len(operands)

    def run(*refs):
        kernel(*refs[:count], *refs[count + len(ordered) :])

    return pl.pallas_call(
        run,
        out_shape=out_shape,
        in_specs=[
            whole(pltpu.SMEM if operand.ndim == 1 else pltpu.VMEM) for operand in operands
        ]
        + [whole(pl.ANY)] * len(ordered),
        out_specs=jax.tree.map(lambda _: whole(), out_shape),
        compiler_params=pltpu.CompilerParams(vmem_limit_bytes=limit),
        name=name,
        **options,
    )(*operands, *ordered)


def column_half(array, h):
    rows, columns = array.shape
    width = columns // HALVES

    def kernel(ref, out):
        out[...] = ref[:, h * width : (h + 1) * width]

    return call(
        kernel, jax.ShapeDtypeStruct((rows, width), array.dtype), [array], "column_half"
    )


def pass_on(array, ordered):
    def kernel(ref, out):
        out[...] = ref[...]

    return call(
        kernel, jax.ShapeDtypeStruct(array.shape, array.dtype), [array], "pass_on", ordered
    )


def join(pieces, columns, ordered=()):
    rows, width = pieces[0].shape
    across = columns // width

    def kernel(*refs):
        out = refs[-1]
        for i, ref in enumerate(refs[:-1]):
            top, left = i // across * rows, i % across * width
            out[top : top + rows, left : left + width] = ref[...]

    shape = (rows * len(pieces) // across, columns)
    return call(
        kernel, jax.ShapeDtypeStruct(shape, pieces[0].dtype), pieces, "join_pieces", ordered
    )


def gather_rows(own, size, weights, ordered):
    chips = size // 2
    last = chips // 2
    columns = own.shape[1]
    right = left = own
    pieces, loads = [], []
    mine, theirs = [own], []
    for step in range(1, last):
        before = right
        right = lax.ppermute(right, AXIS, ring(size, 1))
        left = lax.ppermute(left, AXIS, ring(size, -1))
        if step == 1:
            theirs.append(lax.ppermute(own, AXIS, flip(size, 1)))
        pieces += [right, left]
        if step <= LOADS:
            loads.append(load_rows(weights, step - 1, [before] if step > 1 else []))
            right = pass_on(right, loads[-1])
    part = join(pieces, columns, ordered)
    mine.append(part)
    theirs.append(lax.ppermute(part, AXIS, flip(size, 1)))
    part = join(
        [
            lax.ppermute(column_half(right, 0), AXIS, ring(size, 1)),
            lax.ppermute(column_half(left, 1), AXIS, ring(size, -1)),
        ],
        columns,
    )
    mine.append(part)
    theirs.append(lax.ppermute(part, AXIS, flip(size, 1)))
    return mine + theirs, loads


def row_masks(tables, shrink_factors, own_rows, size):
    batch_rows = own_rows * size
    slots, model_width, rank_limit = shrink_factors.shape
    factor = jnp.swapaxes(shrink_factors, 1, 2).reshape(slots * rank_limit, model_width)
    adapters = tables[2].shape[0]

    def kernel(*refs):
        start, segment_adapter, ranks, slot_of = (ref[...] for ref in refs[:4])
        factor_in, scale, to_place, from_place, hot, factor_out = refs[4:]
        factor_out[...] = factor_in[...]
        me = lax.axis_index(AXIS)
        row = lax.broadcasted_iota(jnp.int32, (batch_rows, 1), 0)
        column = lax.broadcasted_iota(jnp.int32, (1, batch_rows), 1)
        position = row_positions(me, row, own_rows, size)
        adapter = row_adapters(position, start, segment_adapter)
        rank = pick(adapter, ranks)
        slot = pick(adapter, slot_of) - me * slots
        at = lax.broadcasted_iota(jnp.int32, (1, slots * rank_limit), 1)
        keep = (at // rank_limit == slot) & (at % rank_limit < rank)
        scale[...] = jnp.where(keep, adapter_alpha / rank.astype(jnp.float32), 0.0)
        to_place[...] = (row_positions(me, column, own_rows, size) == row).astype(jnp.bfloat16)
        from_place[...] = (position == column).astype(jnp.bfloat16)
        depth = lax.broadcasted_iota(jnp.int32, (1, adapters * rank_limit), 1)
        hot[...] = (depth // rank_limit == adapter).astype(jnp.bfloat16)

    shapes = (
        jax.ShapeDtypeStruct((batch_rows, slots * rank_limit), jnp.float32),
        jax.ShapeDtypeStruct((batch_rows, batch_rows), jnp.bfloat16),
        jax.ShapeDtypeStruct((batch_rows, batch_rows), jnp.bfloat16),
        jax.ShapeDtypeStruct((batch_rows, adapters * rank_limit), jnp.bfloat16),
        jax.ShapeDtypeStruct(factor.shape, factor.dtype),
    )
    return call(kernel, shapes, [*(table[None] for table in tables), factor], "row_masks")


def shrink_rows(parts, factor, scale, to_place, rank_limit):
    model_width = factor.shape[1]
    slots = factor.shape[0] // rank_limit
    batch_rows = to_place.shape[0]
    width = model_width // 8

    def kernel(*refs):
        factor_ref, scale_ref, place_ref, rows_out, coeff_out, total = refs[len(parts) :]

        def columns(k, _):
            at = pl.ds(pl.multiple_of(k * width, width), width)
            top = 0
            for part in refs[: len(parts)]:
                rows_out[top : top + part.shape[0], at] = part[:, at]
                top += part.shape[0]
            product = lax.dot_general(
                rows_out[:, at],
                factor_ref[:, at],
                (((1,), (1,)), ((), ())),
                preferred_element_type=jnp.float32,
            )
            total[...] = jnp.where(k == 0, product, total[...] + product)
            return 0

        lax.fori_loop(0, model_width // width, columns, 0)
        scaled = total[...] * scale_ref[...]
        coeff = scaled[:, :rank_limit]
        for s in range(1, slots):
            coeff = coeff + scaled[:, s * rank_limit : (s + 1) * rank_limit]
        coeff_out[...] = jnp.dot(
            place_ref[...], coeff.astype(jnp.bfloat16), preferred_element_type=jnp.float32
        ).astype(jnp.bfloat16)

    return call(
        kernel,
        (
            jax.ShapeDtypeStruct((batch_rows, model_width), jnp.bfloat16),
            jax.ShapeDtypeStruct((batch_rows, rank_limit), jnp.bfloat16),
        ),
        [*parts, factor, scale, to_place],
        "shrink_rows",
        scratch_shapes=[pltpu.VMEM((batch_rows, slots * rank_limit), jnp.float32)],
        cost_estimate=pl.CostEstimate(
            flops=2 * batch_rows * model_width * slots * rank_limit,
            bytes_accessed=4 * batch_rows * model_width,
            transcendentals=0,
        ),
    )


def add_coefficients(a, b, ordered):
    def kernel(a_ref, b_ref, out):
        out[...] = a_ref[...] + b_ref[...]

    return call(
        kernel, jax.ShapeDtypeStruct(a.shape, a.dtype), [a, b], "add_coefficients", ordered
    )


def lane_tiles(width):
    return -(-width // 128) * 128


def depth_cuts(depth):
    part = -(-3 * depth // 8 // DEPTH_BLOCK) * DEPTH_BLOCK
    return [part * p for p in range(LOADS + 1)] + [depth]


def load_rows(weights, part, ordered):
    depth = weights[0].shape[0]
    first, last = depth_cuts(depth)[part : part + 2]
    widths = [weight.shape[1] for weight in weights]
    if all(width % 128 == 0 for width in widths):
        places = [(0, sum(widths[:w])) for w in range(len(weights))]
        shapes = [(last - first, sum(widths))]
    else:
        places = [(w, 0) for w in range(len(weights))]
        shapes = [(last - first, width) for width in widths]

    def kernel(*refs):
        sources = refs[: len(weights)]
        outs = refs[len(weights) + len(ordered) : -1]
        arrived = refs[-1]
        copies = []
        for i, top in enumerate(range(0, last - first, DEPTH_BLOCK)):
            for w, (out, left) in enumerate(places):
                copy = pltpu.make_async_copy(
                    sources[w].at[first + top : first + top + DEPTH_BLOCK, :],
                    outs[out].at[top : top + DEPTH_BLOCK, left : left + widths[w]],
                    arrived.at[i, w],
                )
                copy.start()
                copies.append(copy)
        for copy in copies:
            copy.wait()

    return pl.pallas_call(
        kernel,
        out_shape=[jax.ShapeDtypeStruct(shape, weights[0].dtype) for shape in shapes],
        in_specs=[whole(pltpu.HBM)] * len(weights) + [whole(pl.ANY)] * len(ordered),
        out_specs=[whole()] * len(shapes),
        scratch_shapes=[
            pltpu.SemaphoreType.DMA(((last - first) // DEPTH_BLOCK, len(weights)))
        ],
        compiler_params=pltpu.CompilerParams(vmem_limit_bytes=LOAD_LIMITS[part]),
        cost_estimate=pl.CostEstimate(
            flops=0, bytes_accessed=4 * (last - first) * sum(widths), transcendentals=0
        ),
        name="load_rows",
    )(*weights, *ordered)


def mixed_rows(rows, loaded, part, before, ordered):
    batch_rows, depth = rows.shape
    first, last = depth_cuts(depth)[part : part + 2]
    widths = [block.shape[1] for block in loaded]
    lefts = [sum(lane_tiles(width) for width in widths[:w]) for w in range(len(widths))]
    width = sum(lane_tiles(width) for width in widths)

    def kernel(rows_ref, *refs):
        out = refs[-1]
        for block, left, wide in zip(refs, lefts, widths):
            columns = slice(left, left + wide)
            product = jnp.dot(
                rows_ref[:, first:last], block[...], preferred_element_type=jnp.float32
            )
            if before is not None:
                product = refs[len(widths)][:, columns] + product
            out[:, columns] = product

    return call(
        kernel,
        jax.ShapeDtypeStruct((batch_rows, width), jnp.float32),
        [rows, *loaded] + ([] if before is None else [before]),
        "mixed_rows",
        ordered,
        cost_estimate=pl.CostEstimate(
            flops=2 * batch_rows * (last - first) * width,
            bytes_accessed=2 * (last - first) * width,
            transcendentals=0,
        ),
    )


def stream_rows(rows, weights, before, first, last, ordered):
    batch_rows = rows.shape[0]
    widths = [weight.shape[1] for weight in weights]
    lefts = [sum(lane_tiles(width) for width in widths[:w]) for w in range(len(weights))]
    width = sum(lane_tiles(width) for width in widths)
    if width == sum(widths):
        buffer_of, offsets = [0] * len(weights), lefts
        products = [(0, width)]
    else:
        buffer_of, offsets = list(range(len(weights))), [0] * len(weights)
        products = list(zip(lefts, widths))
    blocks = []
    at = first
    while at < last:
        depth = min(4 * DEPTH_BLOCK if blocks else 2 * DEPTH_BLOCK, last - at)
        blocks.append((at, depth))
        at += depth

    def kernel(rows_ref, *refs):
        sources = refs[: len(weights)]
        arrived = refs[-1]
        buffers = refs[-1 - len(products) : -1]
        out = refs[-2 - len(products)]
        copies = []
        for b, (at, depth) in enumerate(blocks):
            copies.append([])
            half = depth // 2
            for p in range(2):
                for w, source in enumerate(sources):
                    top = at - first + p * half
                    copy = pltpu.make_async_copy(
                        source.at[at + p * half : at + (p + 1) * half, :],
                        buffers[buffer_of[w]].at[
                            top : top + half, offsets[w] : offsets[w] + widths[w]
                        ],
                        arrived.at[b, 2 * w + p],
                    )
                    copy.start()
                    copies[-1].append(copy)
        for (at, depth), group in zip(blocks, copies):
            for copy in group:
                copy.wait()
            for (left, wide), buffer in zip(products, buffers):
                columns = slice(left, left + wide)
                product = jnp.dot(
                    rows_ref[:, at : at + depth],
                    buffer[at - first : at - first + depth, :],
                    preferred_element_type=jnp.float32,
                )
                if at > first:
                    product = out[:, columns] + product
                elif before is not None:
                    product = refs[len(weights)][:, columns] + product
                out[:, columns] = product

    return pl.pallas_call(
        kernel,
        out_shape=jax.ShapeDtypeStruct((batch_rows, width), jnp.float32),
        in_specs=[whole()]
        + [whole(pltpu.HBM)] * len(weights)
        + [whole()] * (before is not None)
        + [whole(pl.ANY)] * len(ordered),
        out_specs=whole(),
        scratch_shapes=[pltpu.VMEM((last - first, wide), rows.dtype) for _, wide in products]
        + [pltpu.SemaphoreType.DMA((len(blocks), 2 * len(weights)))],
        compiler_params=pltpu.CompilerParams(vmem_limit_bytes=STREAM_LIMIT),
        cost_estimate=pl.CostEstimate(
            flops=2 * batch_rows * (last - first) * width,
            bytes_accessed=STREAM_COST * (last - first) * width,
            transcendentals=0,
        ),
        name="stream_rows",
    )(rows, *weights, *([] if before is None else [before]), *ordered)


def hidden_kernel(coeff, recv, from_place, hot, expand, mixed, out, spread):
    rank_limit = coeff.shape[1]
    own = jnp.dot(
        from_place[...], coeff[...] + recv[...], preferred_element_type=jnp.float32
    ).astype(jnp.bfloat16)
    pair = jnp.concatenate([own, own], axis=1)
    for p in range(spread.shape[1] // (2 * rank_limit)):
        at = slice(p * 2 * rank_limit, (p + 1) * 2 * rank_limit)
        spread[:, at] = hot[:, at] * pair
    lora = jnp.dot(spread[...], expand[...], preferred_element_type=jnp.float32)
    width = out.shape[1]
    value = mixed[:, :width]
    total = mixed[:, lane_tiles(width) : lane_tiles(width) + width] + lora
    out[...] = (value / (1.0 + jnp.exp(-value)) * total).astype(jnp.bfloat16)


def hidden_rows(mixed, coeff, recv, expand_factors, from_place, hot):
    adapters, rank_limit, width = expand_factors.shape
    batch_rows = mixed.shape[0]
    expand = expand_factors.reshape(adapters * rank_limit, width)
    return call(
        hidden_kernel,
        jax.ShapeDtypeStruct((batch_rows, width), jnp.bfloat16),
        [coeff, recv, from_place, hot, expand, mixed],
        "hidden_rows",
        scratch_shapes=[pltpu.VMEM((batch_rows, adapters * rank_limit), jnp.bfloat16)],
        cost_estimate=pl.CostEstimate(
            flops=2 * batch_rows * adapters * rank_limit * width,
            bytes_accessed=2 * adapters * rank_limit * width,
            transcendentals=batch_rows * width,
        ),
    )


def add_blocks(sides, own_rows, ordered):
    operands, shapes = [], []
    for mine, theirs, _, arrived in sides:
        operands += [mine, theirs] + ([] if arrived is None else [arrived])
        shapes.append(jax.ShapeDtypeStruct((own_rows, mine.shape[1]), jnp.bfloat16))

    def kernel(*refs):
        refs = list(refs)
        outs = refs[-len(sides) :]
        for (_, _, index, arrived), out in zip(sides, outs):
            at = slice(index * own_rows, (index + 1) * own_rows)
            total = refs.pop(0)[at, :].astype(jnp.float32)
            total = total + refs.pop(0)[at, :].astype(jnp.float32)
            if arrived is not None:
                total = total + refs.pop(0)[...].astype(jnp.float32)
            out[...] = total.astype(jnp.bfloat16)

    return call(kernel, tuple(shapes), operands, "add_blocks", ordered)


def scatter_rows(mine, theirs, own_rows, size):
    chips = size // 2
    last = chips // 2
    right, left = [None] * HALVES, [None] * HALVES
    ordered = []
    for turn in range(last):
        chains = [(right, 1, 0), (left, -1, 1), (left, -1, 0), (right, 1, 1)]
        if turn == 0:
            chains = [chains[0], chains[2], chains[1], chains[3]]
        groups = [[chain] for chain in chains] if turn < last - 1 else [chains[:2]]
        for group in groups:
            sides = []
            for chain, by, h in group:
                longer = (by == 1) == (h == 0)
                steps = last - turn - (not longer)
                index = min(2 * steps, chips - 1) if by == 1 else 2 * steps - 1
                sides.append((mine[h], theirs[h], index, chain[h]))
            sums = add_blocks(sides, own_rows, ordered)
            ordered = [sums[0]]
            for (chain, by, h), value in zip(group, sums):
                chain[h] = lax.ppermute(value, AXIS, ring(size, by))
    return list(zip(mine, theirs, right, left))


def finish_rows(halves, activations, gain, own_rows):
    width = activations.shape[1] // HALVES

    def kernel(*refs):
        refs, (act, gain_ref, block_out, normed, stream) = refs[:-5], refs[-5:]
        square = jnp.zeros((own_rows, 1), jnp.float32)
        for h in range(HALVES):
            mine, theirs, right, left = refs[4 * h : 4 * h + 4]
            at = slice(h * width, (h + 1) * width)
            total = act[:, at].astype(jnp.float32)
            for ref in (mine, theirs):
                total = total + ref[:own_rows, :].astype(jnp.float32)
            for ref in (right, left):
                total = total + ref[...].astype(jnp.float32)
            stream[:, at] = total
            block_out[:, at] = total.astype(jnp.bfloat16)
            square = square + jnp.sum(total * total, axis=1, keepdims=True)
        scale = lax.rsqrt(square * (1.0 / act.shape[1]) + 1e-05)
        normed[...] = (stream[...] * scale * gain_ref[...].astype(jnp.float32)).astype(
            jnp.bfloat16
        )

    out = jax.ShapeDtypeStruct(activations.shape, jnp.bfloat16)
    return call(
        kernel,
        (out, out),
        [array for half in halves for array in half] + [activations, gain],
        "finish_rows",
        scratch_shapes=[pltpu.VMEM(activations.shape, jnp.float32)],
    )


def body(
    activations,
    gate_weight,
    up_weight,
    down_weight,
    norm_gain_vector,
    shrink_factors,
    expand_factors,
    adapter_ranks,
    adapter_storage_slot,
    segment_start,
    segment_adapter,
):
    size = lax.axis_size(AXIS)
    own_rows, model_width = activations.shape
    assert size & (size - 1) == 0 and own_rows & (own_rows - 1) == 0
    tables = (segment_start, segment_adapter, adapter_ranks, adapter_storage_slot)
    scale, to_place, from_place, hot, factor = row_masks(
        tables, shrink_factors, own_rows, size
    )

    parts, loads = gather_rows(activations, size, (gate_weight, up_weight), [scale])
    rows, coeff = shrink_rows(parts, factor, scale, to_place, shrink_factors.shape[2])

    bits = [1 << b for b in range(size.bit_length() - 1)]
    mixed = None
    for step, bit in enumerate(bits):
        received = lax.ppermute(coeff, AXIS, flip(size, bit))
        part = step - (len(bits) - LOADS - 1)
        if part == LOADS:
            cuts = depth_cuts(model_width)
            mixed = stream_rows(
                rows, (gate_weight, up_weight), mixed, cuts[part], cuts[part + 1], [coeff]
            )
        elif part >= 0:
            mixed = mixed_rows(rows, loads[part], part, mixed, [coeff])
        if bit < bits[-1]:
            coeff = add_coefficients(coeff, received, [] if mixed is None else [mixed])
    hidden = hidden_rows(mixed, coeff, received, expand_factors, from_place, hot)

    half = size * own_rows // 2
    width = model_width // HALVES
    mine, theirs = [None] * HALVES, [None] * HALVES
    for h in range(HALVES):
        term = jnp.dot(
            hidden,
            down_weight[:, h * width : (h + 1) * width],
            preferred_element_type=jnp.float32,
        ).astype(jnp.bfloat16)
        mine[h] = term
        theirs[h] = lax.ppermute(term[half:], AXIS, flip(size, 1))
    halves = scatter_rows(mine, theirs, own_rows, size)
    return finish_rows(halves, activations, norm_gain_vector[None], own_rows)


def solution(mesh):
    return jax.shard_map(
        body,
        mesh=mesh,
        in_specs=(
            P(("groups", "mp"), None),
            P(None, "mp"),
            P(None, "mp"),
            P("mp", None),
            P(),
            P("mp", None, None),
            P(None, None, "mp"),
            P(),
            P(),
            P("groups"),
            P("groups"),
        ),
        out_specs=(P(("groups", "mp"), None), P(("groups", "mp"), None)),
        check_vma=False,
    )
```

```python
import functools

import jax
import jax.numpy as jnp
from jax import lax
from jax.experimental import pallas as pl
from jax.experimental.pallas import tpu as pltpu
from jax.sharding import PartitionSpec as P

adapter_alpha = 32.0
AXIS = "mp"
HALVES = 2
DEPTH_BLOCK = 256
LOADS = 2
VMEM_LIMIT = 12 * 1024 * 1024
LOAD_LIMITS = [mb * 1024 * 1024 for mb in (42, 37)]
STREAM_LIMIT = 34 * 1024 * 1024
STREAM_COST = 4


def chip_at(place, chips):
    if chips == 8:
        return jnp.where(place < 4, 2 * place, 2 * (7 - place) + 1)
    return place


def place_of(chip, chips):
    if chips == 8:
        return jnp.where((chip & 1) == 0, chip >> 1, 7 - (chip >> 1))
    return chip


def ring(size, by):
    chips = size // 2
    order = [0, 2, 4, 6, 7, 5, 3, 1] if chips == 8 else list(range(chips))
    pairs = []
    for place, chip in enumerate(order):
        to = order[(place + by) % chips]
        pairs += [(2 * chip + core, 2 * to + core) for core in range(2)]
    return pairs


def flip(size, bit):
    return [(i, i ^ bit) for i in range(size)]


def row_positions(me, row, own_rows, size):
    chips = size // 2
    block = row // own_rows
    index = block & (chips - 1)
    step = (index + 1) >> 1
    delta = jnp.where((index & 1) == 1, step, -step)
    place = (place_of(me >> 1, chips) - delta + chips) & (chips - 1)
    core = (me & 1) ^ (block // chips)
    return (2 * chip_at(place, chips) + core) * own_rows + (row & (own_rows - 1))


def pick(index, table):
    hot = index == lax.broadcasted_iota(jnp.int32, (1, table.shape[1]), 1)
    return jnp.sum(jnp.where(hot, table, 0), axis=1, keepdims=True)


def row_adapters(position, start, adapters):
    segment = jnp.sum((start <= position).astype(jnp.int32), axis=1, keepdims=True) - 1
    return pick(segment, adapters)


def whole(space=pltpu.VMEM):
    return pl.BlockSpec(memory_space=space)


def call(kernel, out_shape, operands, name, ordered=(), limit=VMEM_LIMIT, **options):
    count = len(operands)

    def run(*refs):
        kernel(*refs[:count], *refs[count + len(ordered) :])

    return pl.pallas_call(
        run,
        out_shape=out_shape,
        in_specs=[
            whole(pltpu.SMEM if operand.ndim == 1 else pltpu.VMEM) for operand in operands
        ]
        + [whole(pl.ANY)] * len(ordered),
        out_specs=jax.tree.map(lambda _: whole(), out_shape),
        compiler_params=pltpu.CompilerParams(vmem_limit_bytes=limit),
        name=name,
        **options,
    )(*operands, *ordered)


def column_half(array, h):
    rows, columns = array.shape
    width = columns // HALVES

    def kernel(ref, out):
        out[...] = ref[:, h * width : (h + 1) * width]

    return call(
        kernel, jax.ShapeDtypeStruct((rows, width), array.dtype), [array], "column_half"
    )


def pass_on(array, ordered):
    def kernel(ref, out):
        out[...] = ref[...]

    return call(
        kernel, jax.ShapeDtypeStruct(array.shape, array.dtype), [array], "pass_on", ordered
    )


def join(pieces, columns, ordered=()):
    rows, width = pieces[0].shape
    across = columns // width

    def kernel(*refs):
        out = refs[-1]
        for i, ref in enumerate(refs[:-1]):
            top, left = i // across * rows, i % across * width
            out[top : top + rows, left : left + width] = ref[...]

    shape = (rows * len(pieces) // across, columns)
    return call(
        kernel, jax.ShapeDtypeStruct(shape, pieces[0].dtype), pieces, "join_pieces", ordered
    )


def gather_rows(own, size, weights, ordered):
    chips = size // 2
    last = chips // 2
    columns = own.shape[1]
    right = left = own
    pieces, loads = [], []
    mine, theirs = [own], []
    for step in range(1, last):
        before = right
        right = lax.ppermute(right, AXIS, ring(size, 1))
        left = lax.ppermute(left, AXIS, ring(size, -1))
        if step == 1:
            theirs.append(lax.ppermute(own, AXIS, flip(size, 1)))
        pieces += [right, left]
        if step <= LOADS:
            loads.append(load_rows(weights, step - 1, [before] if step > 1 else []))
            right = pass_on(right, loads[-1])
    part = join(pieces, columns, ordered)
    mine.append(part)
    theirs.append(lax.ppermute(part, AXIS, flip(size, 1)))
    part = join(
        [
            lax.ppermute(column_half(right, 0), AXIS, ring(size, 1)),
            lax.ppermute(column_half(left, 1), AXIS, ring(size, -1)),
        ],
        columns,
    )
    mine.append(part)
    theirs.append(lax.ppermute(part, AXIS, flip(size, 1)))
    return mine + theirs, loads


def row_masks(tables, shrink_factors, own_rows, size):
    batch_rows = own_rows * size
    slots, model_width, rank_limit = shrink_factors.shape
    factor = jnp.swapaxes(shrink_factors, 1, 2).reshape(slots * rank_limit, model_width)
    adapters = tables[2].shape[0]

    def kernel(*refs):
        start, segment_adapter, ranks, slot_of = (ref[...] for ref in refs[:4])
        factor_in, scale, to_place, from_place, hot, factor_out = refs[4:]
        factor_out[...] = factor_in[...]
        me = lax.axis_index(AXIS)
        row = lax.broadcasted_iota(jnp.int32, (batch_rows, 1), 0)
        column = lax.broadcasted_iota(jnp.int32, (1, batch_rows), 1)
        position = row_positions(me, row, own_rows, size)
        adapter = row_adapters(position, start, segment_adapter)
        rank = pick(adapter, ranks)
        slot = pick(adapter, slot_of) - me * slots
        at = lax.broadcasted_iota(jnp.int32, (1, slots * rank_limit), 1)
        keep = (at // rank_limit == slot) & (at % rank_limit < rank)
        scale[...] = jnp.where(keep, adapter_alpha / rank.astype(jnp.float32), 0.0)
        to_place[...] = (row_positions(me, column, own_rows, size) == row).astype(jnp.bfloat16)
        from_place[...] = (position == column).astype(jnp.bfloat16)
        depth = lax.broadcasted_iota(jnp.int32, (1, adapters * rank_limit), 1)
        hot[...] = (depth // rank_limit == adapter).astype(jnp.bfloat16)

    shapes = (
        jax.ShapeDtypeStruct((batch_rows, slots * rank_limit), jnp.float32),
        jax.ShapeDtypeStruct((batch_rows, batch_rows), jnp.bfloat16),
        jax.ShapeDtypeStruct((batch_rows, batch_rows), jnp.bfloat16),
        jax.ShapeDtypeStruct((batch_rows, adapters * rank_limit), jnp.bfloat16),
        jax.ShapeDtypeStruct(factor.shape, factor.dtype),
    )
    return call(kernel, shapes, [*(table[None] for table in tables), factor], "row_masks")


def shrink_rows(parts, factor, scale, to_place, rank_limit):
    model_width = factor.shape[1]
    slots = factor.shape[0] // rank_limit
    batch_rows = to_place.shape[0]
    width = model_width // 8

    def kernel(*refs):
        factor_ref, scale_ref, place_ref, rows_out, coeff_out, total = refs[len(parts) :]

        def columns(k, _):
            at = pl.ds(pl.multiple_of(k * width, width), width)
            top = 0
            for part in refs[: len(parts)]:
                rows_out[top : top + part.shape[0], at] = part[:, at]
                top += part.shape[0]
            product = lax.dot_general(
                rows_out[:, at],
                factor_ref[:, at],
                (((1,), (1,)), ((), ())),
                preferred_element_type=jnp.float32,
            )
            total[...] = jnp.where(k == 0, product, total[...] + product)
            return 0

        lax.fori_loop(0, model_width // width, columns, 0)
        scaled = total[...] * scale_ref[...]
        coeff = scaled[:, :rank_limit]
        for s in range(1, slots):
            coeff = coeff + scaled[:, s * rank_limit : (s + 1) * rank_limit]
        coeff_out[...] = jnp.dot(
            place_ref[...], coeff.astype(jnp.bfloat16), preferred_element_type=jnp.float32
        ).astype(jnp.bfloat16)

    return call(
        kernel,
        (
            jax.ShapeDtypeStruct((batch_rows, model_width), jnp.bfloat16),
            jax.ShapeDtypeStruct((batch_rows, rank_limit), jnp.bfloat16),
        ),
        [*parts, factor, scale, to_place],
        "shrink_rows",
        scratch_shapes=[pltpu.VMEM((batch_rows, slots * rank_limit), jnp.float32)],
        cost_estimate=pl.CostEstimate(
            flops=2 * batch_rows * model_width * slots * rank_limit,
            bytes_accessed=4 * batch_rows * model_width,
            transcendentals=0,
        ),
    )


def add_coefficients(a, b, ordered):
    def kernel(a_ref, b_ref, out):
        out[...] = a_ref[...] + b_ref[...]

    return call(
        kernel, jax.ShapeDtypeStruct(a.shape, a.dtype), [a, b], "add_coefficients", ordered
    )


def lane_tiles(width):
    return -(-width // 128) * 128


def depth_cuts(depth):
    part = -(-3 * depth // 8 // DEPTH_BLOCK) * DEPTH_BLOCK
    return [part * p for p in range(LOADS + 1)] + [depth]


def load_rows(weights, part, ordered):
    depth = weights[0].shape[0]
    first, last = depth_cuts(depth)[part : part + 2]
    widths = [weight.shape[1] for weight in weights]
    if all(width % 128 == 0 for width in widths):
        places = [(0, sum(widths[:w])) for w in range(len(weights))]
        shapes = [(last - first, sum(widths))]
    else:
        places = [(w, 0) for w in range(len(weights))]
        shapes = [(last - first, width) for width in widths]

    def kernel(*refs):
        sources = refs[: len(weights)]
        outs = refs[len(weights) + len(ordered) : -1]
        arrived = refs[-1]
        copies = []
        for i, top in enumerate(range(0, last - first, DEPTH_BLOCK)):
            for w, (out, left) in enumerate(places):
                copy = pltpu.make_async_copy(
                    sources[w].at[first + top : first + top + DEPTH_BLOCK, :],
                    outs[out].at[top : top + DEPTH_BLOCK, left : left + widths[w]],
                    arrived.at[i, w],
                )
                copy.start()
                copies.append(copy)
        for copy in copies:
            copy.wait()

    return pl.pallas_call(
        kernel,
        out_shape=[jax.ShapeDtypeStruct(shape, weights[0].dtype) for shape in shapes],
        in_specs=[whole(pltpu.HBM)] * len(weights) + [whole(pl.ANY)] * len(ordered),
        out_specs=[whole()] * len(shapes),
        scratch_shapes=[
            pltpu.SemaphoreType.DMA(((last - first) // DEPTH_BLOCK, len(weights)))
        ],
        compiler_params=pltpu.CompilerParams(vmem_limit_bytes=LOAD_LIMITS[part]),
        cost_estimate=pl.CostEstimate(
            flops=0, bytes_accessed=4 * (last - first) * sum(widths), transcendentals=0
        ),
        name="load_rows",
    )(*weights, *ordered)


def mixed_rows(rows, loaded, part, before, ordered):
    batch_rows, depth = rows.shape
    first, last = depth_cuts(depth)[part : part + 2]
    widths = [block.shape[1] for block in loaded]
    lefts = [sum(lane_tiles(width) for width in widths[:w]) for w in range(len(widths))]
    width = sum(lane_tiles(width) for width in widths)

    def kernel(rows_ref, *refs):
        out = refs[-1]
        for block, left, wide in zip(refs, lefts, widths):
            columns = slice(left, left + wide)
            product = jnp.dot(
                rows_ref[:, first:last], block[...], preferred_element_type=jnp.float32
            )
            if before is not None:
                product = refs[len(widths)][:, columns] + product
            out[:, columns] = product

    return call(
        kernel,
        jax.ShapeDtypeStruct((batch_rows, width), jnp.float32),
        [rows, *loaded] + ([] if before is None else [before]),
        "mixed_rows",
        ordered,
        cost_estimate=pl.CostEstimate(
            flops=2 * batch_rows * (last - first) * width,
            bytes_accessed=2 * (last - first) * width,
            transcendentals=0,
        ),
    )


def stream_rows(rows, weights, before, first, last, ordered):
    batch_rows = rows.shape[0]
    widths = [weight.shape[1] for weight in weights]
    lefts = [sum(lane_tiles(width) for width in widths[:w]) for w in range(len(weights))]
    width = sum(lane_tiles(width) for width in widths)
    if width == sum(widths):
        buffer_of, offsets = [0] * len(weights), lefts
        products = [(0, width)]
    else:
        buffer_of, offsets = list(range(len(weights))), [0] * len(weights)
        products = list(zip(lefts, widths))
    blocks = []
    at = first
    while at < last:
        depth = min(4 * DEPTH_BLOCK if blocks else 2 * DEPTH_BLOCK, last - at)
        blocks.append((at, depth))
        at += depth

    def kernel(rows_ref, *refs):
        sources = refs[: len(weights)]
        arrived = refs[-1]
        buffers = refs[-1 - len(products) : -1]
        out = refs[-2 - len(products)]
        copies = []
        for b, (at, depth) in enumerate(blocks):
            copies.append([])
            half = depth // 2
            for p in range(2):
                for w, source in enumerate(sources):
                    top = at - first + p * half
                    copy = pltpu.make_async_copy(
                        source.at[at + p * half : at + (p + 1) * half, :],
                        buffers[buffer_of[w]].at[
                            top : top + half, offsets[w] : offsets[w] + widths[w]
                        ],
                        arrived.at[b, 2 * w + p],
                    )
                    copy.start()
                    copies[-1].append(copy)
        for (at, depth), group in zip(blocks, copies):
            for copy in group:
                copy.wait()
            for (left, wide), buffer in zip(products, buffers):
                columns = slice(left, left + wide)
                product = jnp.dot(
                    rows_ref[:, at : at + depth],
                    buffer[at - first : at - first + depth, :],
                    preferred_element_type=jnp.float32,
                )
                if at > first:
                    product = out[:, columns] + product
                elif before is not None:
                    product = refs[len(weights)][:, columns] + product
                out[:, columns] = product

    return pl.pallas_call(
        kernel,
        out_shape=jax.ShapeDtypeStruct((batch_rows, width), jnp.float32),
        in_specs=[whole()]
        + [whole(pltpu.HBM)] * len(weights)
        + [whole()] * (before is not None)
        + [whole(pl.ANY)] * len(ordered),
        out_specs=whole(),
        scratch_shapes=[pltpu.VMEM((last - first, wide), rows.dtype) for _, wide in products]
        + [pltpu.SemaphoreType.DMA((len(blocks), 2 * len(weights)))],
        compiler_params=pltpu.CompilerParams(vmem_limit_bytes=STREAM_LIMIT),
        cost_estimate=pl.CostEstimate(
            flops=2 * batch_rows * (last - first) * width,
            bytes_accessed=STREAM_COST * (last - first) * width,
            transcendentals=0,
        ),
        name="stream_rows",
    )(rows, *weights, *([] if before is None else [before]), *ordered)


def hidden_kernel(coeff, recv, from_place, hot, expand, mixed, out, spread):
    rank_limit = coeff.shape[1]
    own = jnp.dot(
        from_place[...], coeff[...] + recv[...], preferred_element_type=jnp.float32
    ).astype(jnp.bfloat16)
    pair = jnp.concatenate([own, own], axis=1)
    for p in range(spread.shape[1] // (2 * rank_limit)):
        at = slice(p * 2 * rank_limit, (p + 1) * 2 * rank_limit)
        spread[:, at] = hot[:, at] * pair
    lora = jnp.dot(spread[...], expand[...], preferred_element_type=jnp.float32)
    width = out.shape[1]
    value = mixed[:, :width]
    total = mixed[:, lane_tiles(width) : lane_tiles(width) + width] + lora
    out[...] = (value / (1.0 + jnp.exp(-value)) * total).astype(jnp.bfloat16)


def hidden_rows(mixed, coeff, recv, expand_factors, from_place, hot):
    adapters, rank_limit, width = expand_factors.shape
    batch_rows = mixed.shape[0]
    expand = expand_factors.reshape(adapters * rank_limit, width)
    return call(
        hidden_kernel,
        jax.ShapeDtypeStruct((batch_rows, width), jnp.bfloat16),
        [coeff, recv, from_place, hot, expand, mixed],
        "hidden_rows",
        scratch_shapes=[pltpu.VMEM((batch_rows, adapters * rank_limit), jnp.bfloat16)],
        cost_estimate=pl.CostEstimate(
            flops=2 * batch_rows * adapters * rank_limit * width,
            bytes_accessed=2 * adapters * rank_limit * width,
            transcendentals=batch_rows * width,
        ),
    )


def add_blocks(sides, own_rows, ordered):
    operands, shapes = [], []
    for mine, theirs, _, arrived in sides:
        operands += [mine, theirs] + ([] if arrived is None else [arrived])
        shapes.append(jax.ShapeDtypeStruct((own_rows, mine.shape[1]), jnp.bfloat16))

    def kernel(*refs):
        refs = list(refs)
        outs = refs[-len(sides) :]
        for (_, _, index, arrived), out in zip(sides, outs):
            at = slice(index * own_rows, (index + 1) * own_rows)
            total = refs.pop(0)[at, :].astype(jnp.float32)
            total = total + refs.pop(0)[at, :].astype(jnp.float32)
            if arrived is not None:
                total = total + refs.pop(0)[...].astype(jnp.float32)
            out[...] = total.astype(jnp.bfloat16)

    return call(kernel, tuple(shapes), operands, "add_blocks", ordered)


def scatter_rows(mine, theirs, own_rows, size):
    chips = size // 2
    last = chips // 2
    right, left = [None] * HALVES, [None] * HALVES
    ordered = []
    for turn in range(last):
        chains = [(right, 1, 0), (left, -1, 1), (right, 1, 1), (left, -1, 0)]
        if turn == 0:
            chains = [chains[0], chains[3], chains[2], chains[1]]
        groups = [[chain] for chain in chains] if turn < last - 1 else [chains[:2]]
        for group in groups:
            sides = []
            for chain, by, h in group:
                longer = (by == 1) == (h == 0)
                steps = last - turn - (not longer)
                index = min(2 * steps, chips - 1) if by == 1 else 2 * steps - 1
                sides.append((mine[h], theirs[h], index, chain[h]))
            sums = add_blocks(sides, own_rows, ordered)
            ordered = [sums[0]]
            for (chain, by, h), value in zip(group, sums):
                chain[h] = lax.ppermute(value, AXIS, ring(size, by))
    return list(zip(mine, theirs, right, left))


def finish_rows(halves, activations, gain, own_rows):
    width = activations.shape[1] // HALVES

    def kernel(*refs):
        refs, (act, gain_ref, block_out, normed, stream) = refs[:-5], refs[-5:]
        square = jnp.zeros((own_rows, 1), jnp.float32)
        for h in range(HALVES):
            mine, theirs, right, left = refs[4 * h : 4 * h + 4]
            at = slice(h * width, (h + 1) * width)
            total = act[:, at].astype(jnp.float32)
            for ref in (mine, theirs):
                total = total + ref[:own_rows, :].astype(jnp.float32)
            for ref in (right, left):
                total = total + ref[...].astype(jnp.float32)
            stream[:, at] = total
            block_out[:, at] = total.astype(jnp.bfloat16)
            square = square + jnp.sum(total * total, axis=1, keepdims=True)
        scale = lax.rsqrt(square * (1.0 / act.shape[1]) + 1e-05)
        normed[...] = (stream[...] * scale * gain_ref[...].astype(jnp.float32)).astype(
            jnp.bfloat16
        )

    out = jax.ShapeDtypeStruct(activations.shape, jnp.bfloat16)
    return call(
        kernel,
        (out, out),
        [array for half in halves for array in half] + [activations, gain],
        "finish_rows",
        scratch_shapes=[pltpu.VMEM(activations.shape, jnp.float32)],
    )


def body(
    activations,
    gate_weight,
    up_weight,
    down_weight,
    norm_gain_vector,
    shrink_factors,
    expand_factors,
    adapter_ranks,
    adapter_storage_slot,
    segment_start,
    segment_adapter,
):
    size = lax.axis_size(AXIS)
    own_rows, model_width = activations.shape
    assert size & (size - 1) == 0 and own_rows & (own_rows - 1) == 0
    tables = (segment_start, segment_adapter, adapter_ranks, adapter_storage_slot)
    scale, to_place, from_place, hot, factor = row_masks(
        tables, shrink_factors, own_rows, size
    )

    parts, loads = gather_rows(activations, size, (gate_weight, up_weight), [scale])
    rows, coeff = shrink_rows(parts, factor, scale, to_place, shrink_factors.shape[2])

    bits = [1 << b for b in range(size.bit_length() - 1)]
    mixed = None
    for step, bit in enumerate(bits):
        received = lax.ppermute(coeff, AXIS, flip(size, bit))
        part = step - (len(bits) - LOADS - 1)
        if part == LOADS:
            cuts = depth_cuts(model_width)
            mixed = stream_rows(
                rows, (gate_weight, up_weight), mixed, cuts[part], cuts[part + 1], [coeff]
            )
        elif part >= 0:
            mixed = mixed_rows(rows, loads[part], part, mixed, [coeff])
        if bit < bits[-1]:
            coeff = add_coefficients(coeff, received, [] if mixed is None else [mixed])
    hidden = hidden_rows(mixed, coeff, received, expand_factors, from_place, hot)

    half = size * own_rows // 2
    width = model_width // HALVES
    mine, theirs = [None] * HALVES, [None] * HALVES
    for h in range(HALVES):
        term = jnp.dot(
            hidden,
            down_weight[:, h * width : (h + 1) * width],
            preferred_element_type=jnp.float32,
        ).astype(jnp.bfloat16)
        mine[h] = term
        theirs[h] = lax.ppermute(term[half:], AXIS, flip(size, 1))
    halves = scatter_rows(mine, theirs, own_rows, size)
    return finish_rows(halves, activations, norm_gain_vector[None], own_rows)


def solution(mesh):
    return jax.shard_map(
        body,
        mesh=mesh,
        in_specs=(
            P(("groups", "mp"), None),
            P(None, "mp"),
            P(None, "mp"),
            P("mp", None),
            P(),
            P("mp", None, None),
            P(None, None, "mp"),
            P(),
            P(),
            P("groups"),
            P("groups"),
        ),
        out_specs=(P(("groups", "mp"), None), P(("groups", "mp"), None)),
        check_vma=False,
    )
```

```python
import functools

import jax
import jax.numpy as jnp
from jax import lax
from jax.experimental import pallas as pl
from jax.experimental.pallas import tpu as pltpu
from jax.sharding import PartitionSpec as P

adapter_alpha = 32.0
AXIS = "mp"
HALVES = 2
DEPTH_BLOCK = 256
LOADS = 2
VMEM_LIMIT = 12 * 1024 * 1024
LOAD_LIMITS = [mb * 1024 * 1024 for mb in (42, 36)]
STREAM_LIMIT = 34 * 1024 * 1024
STREAM_COST = 4


def chip_at(place, chips):
    if chips == 8:
        return jnp.where(place < 4, 2 * place, 2 * (7 - place) + 1)
    return place


def place_of(chip, chips):
    if chips == 8:
        return jnp.where((chip & 1) == 0, chip >> 1, 7 - (chip >> 1))
    return chip


def ring(size, by):
    chips = size // 2
    order = [0, 2, 4, 6, 7, 5, 3, 1] if chips == 8 else list(range(chips))
    pairs = []
    for place, chip in enumerate(order):
        to = order[(place + by) % chips]
        pairs += [(2 * chip + core, 2 * to + core) for core in range(2)]
    return pairs


def flip(size, bit):
    return [(i, i ^ bit) for i in range(size)]


def row_positions(me, row, own_rows, size):
    chips = size // 2
    block = row // own_rows
    index = block & (chips - 1)
    step = (index + 1) >> 1
    delta = jnp.where((index & 1) == 1, step, -step)
    place = (place_of(me >> 1, chips) - delta + chips) & (chips - 1)
    core = (me & 1) ^ (block // chips)
    return (2 * chip_at(place, chips) + core) * own_rows + (row & (own_rows - 1))


def pick(index, table):
    hot = index == lax.broadcasted_iota(jnp.int32, (1, table.shape[1]), 1)
    return jnp.sum(jnp.where(hot, table, 0), axis=1, keepdims=True)


def row_adapters(position, start, adapters):
    segment = jnp.sum((start <= position).astype(jnp.int32), axis=1, keepdims=True) - 1
    return pick(segment, adapters)


def whole(space=pltpu.VMEM):
    return pl.BlockSpec(memory_space=space)


def call(kernel, out_shape, operands, name, ordered=(), limit=VMEM_LIMIT, **options):
    count = len(operands)

    def run(*refs):
        kernel(*refs[:count], *refs[count + len(ordered) :])

    return pl.pallas_call(
        run,
        out_shape=out_shape,
        in_specs=[
            whole(pltpu.SMEM if operand.ndim == 1 else pltpu.VMEM) for operand in operands
        ]
        + [whole(pl.ANY)] * len(ordered),
        out_specs=jax.tree.map(lambda _: whole(), out_shape),
        compiler_params=pltpu.CompilerParams(vmem_limit_bytes=limit),
        name=name,
        **options,
    )(*operands, *ordered)


def column_half(array, h):
    rows, columns = array.shape
    width = columns // HALVES

    def kernel(ref, out):
        out[...] = ref[:, h * width : (h + 1) * width]

    return call(
        kernel, jax.ShapeDtypeStruct((rows, width), array.dtype), [array], "column_half"
    )


def pass_on(array, ordered):
    def kernel(ref, out):
        out[...] = ref[...]

    return call(
        kernel, jax.ShapeDtypeStruct(array.shape, array.dtype), [array], "pass_on", ordered
    )


def join(pieces, columns, ordered=()):
    rows, width = pieces[0].shape
    across = columns // width

    def kernel(*refs):
        out = refs[-1]
        for i, ref in enumerate(refs[:-1]):
            top, left = i // across * rows, i % across * width
            out[top : top + rows, left : left + width] = ref[...]

    shape = (rows * len(pieces) // across, columns)
    return call(
        kernel, jax.ShapeDtypeStruct(shape, pieces[0].dtype), pieces, "join_pieces", ordered
    )


def gather_rows(own, size, weights, ordered):
    chips = size // 2
    last = chips // 2
    columns = own.shape[1]
    right = left = own
    pieces, loads = [], []
    mine, theirs = [own], []
    for step in range(1, last):
        before = right
        right = lax.ppermute(right, AXIS, ring(size, 1))
        left = lax.ppermute(left, AXIS, ring(size, -1))
        if step == 1:
            theirs.append(lax.ppermute(own, AXIS, flip(size, 1)))
        pieces += [right, left]
        if step <= LOADS:
            loads.append(load_rows(weights, step - 1, [before] if step > 1 else []))
            right = pass_on(right, loads[-1])
    part = join(pieces, columns, ordered)
    mine.append(part)
    theirs.append(lax.ppermute(part, AXIS, flip(size, 1)))
    part = join(
        [
            lax.ppermute(column_half(right, 0), AXIS, ring(size, 1)),
            lax.ppermute(column_half(left, 1), AXIS, ring(size, -1)),
        ],
        columns,
    )
    mine.append(part)
    theirs.append(lax.ppermute(part, AXIS, flip(size, 1)))
    return mine + theirs, loads


def row_masks(tables, shrink_factors, own_rows, size):
    batch_rows = own_rows * size
    slots, model_width, rank_limit = shrink_factors.shape
    factor = jnp.swapaxes(shrink_factors, 1, 2).reshape(slots * rank_limit, model_width)
    adapters = tables[2].shape[0]

    def kernel(*refs):
        start, segment_adapter, ranks, slot_of = (ref[...] for ref in refs[:4])
        factor_in, scale, to_place, from_place, hot, factor_out = refs[4:]
        factor_out[...] = factor_in[...]
        me = lax.axis_index(AXIS)
        row = lax.broadcasted_iota(jnp.int32, (batch_rows, 1), 0)
        column = lax.broadcasted_iota(jnp.int32, (1, batch_rows), 1)
        position = row_positions(me, row, own_rows, size)
        adapter = row_adapters(position, start, segment_adapter)
        rank = pick(adapter, ranks)
        slot = pick(adapter, slot_of) - me * slots
        at = lax.broadcasted_iota(jnp.int32, (1, slots * rank_limit), 1)
        keep = (at // rank_limit == slot) & (at % rank_limit < rank)
        scale[...] = jnp.where(keep, adapter_alpha / rank.astype(jnp.float32), 0.0)
        to_place[...] = (row_positions(me, column, own_rows, size) == row).astype(jnp.bfloat16)
        from_place[...] = (position == column).astype(jnp.bfloat16)
        depth = lax.broadcasted_iota(jnp.int32, (1, adapters * rank_limit), 1)
        hot[...] = (depth // rank_limit == adapter).astype(jnp.bfloat16)

    shapes = (
        jax.ShapeDtypeStruct((batch_rows, slots * rank_limit), jnp.float32),
        jax.ShapeDtypeStruct((batch_rows, batch_rows), jnp.bfloat16),
        jax.ShapeDtypeStruct((batch_rows, batch_rows), jnp.bfloat16),
        jax.ShapeDtypeStruct((batch_rows, adapters * rank_limit), jnp.bfloat16),
        jax.ShapeDtypeStruct(factor.shape, factor.dtype),
    )
    return call(kernel, shapes, [*(table[None] for table in tables), factor], "row_masks")


def shrink_rows(parts, factor, scale, to_place, rank_limit):
    model_width = factor.shape[1]
    slots = factor.shape[0] // rank_limit
    batch_rows = to_place.shape[0]
    width = model_width // 4

    def kernel(*refs):
        factor_ref, scale_ref, place_ref, rows_out, coeff_out, total = refs[len(parts) :]

        def columns(k, _):
            at = pl.ds(pl.multiple_of(k * width, width), width)
            top = 0
            for part in refs[: len(parts)]:
                rows_out[top : top + part.shape[0], at] = part[:, at]
                top += part.shape[0]
            product = lax.dot_general(
                rows_out[:, at],
                factor_ref[:, at],
                (((1,), (1,)), ((), ())),
                preferred_element_type=jnp.float32,
            )
            total[...] = jnp.where(k == 0, product, total[...] + product)
            return 0

        lax.fori_loop(0, model_width // width, columns, 0)
        scaled = total[...] * scale_ref[...]
        coeff = scaled[:, :rank_limit]
        for s in range(1, slots):
            coeff = coeff + scaled[:, s * rank_limit : (s + 1) * rank_limit]
        coeff_out[...] = jnp.dot(
            place_ref[...], coeff.astype(jnp.bfloat16), preferred_element_type=jnp.float32
        ).astype(jnp.bfloat16)

    return call(
        kernel,
        (
            jax.ShapeDtypeStruct((batch_rows, model_width), jnp.bfloat16),
            jax.ShapeDtypeStruct((batch_rows, rank_limit), jnp.bfloat16),
        ),
        [*parts, factor, scale, to_place],
        "shrink_rows",
        scratch_shapes=[pltpu.VMEM((batch_rows, slots * rank_limit), jnp.float32)],
        cost_estimate=pl.CostEstimate(
            flops=2 * batch_rows * model_width * slots * rank_limit,
            bytes_accessed=4 * batch_rows * model_width,
            transcendentals=0,
        ),
    )


def add_coefficients(a, b, ordered):
    def kernel(a_ref, b_ref, out):
        out[...] = a_ref[...] + b_ref[...]

    return call(
        kernel, jax.ShapeDtypeStruct(a.shape, a.dtype), [a, b], "add_coefficients", ordered
    )


def lane_tiles(width):
    return -(-width // 128) * 128


def depth_cuts(depth):
    part = -(-13 * depth // 32 // DEPTH_BLOCK) * DEPTH_BLOCK
    return [part * p for p in range(LOADS + 1)] + [depth]


def load_rows(weights, part, ordered):
    depth = weights[0].shape[0]
    first, last = depth_cuts(depth)[part : part + 2]
    widths = [weight.shape[1] for weight in weights]
    if all(width % 128 == 0 for width in widths):
        places = [(0, sum(widths[:w])) for w in range(len(weights))]
        shapes = [(last - first, sum(widths))]
    else:
        places = [(w, 0) for w in range(len(weights))]
        shapes = [(last - first, width) for width in widths]

    def kernel(*refs):
        sources = refs[: len(weights)]
        outs = refs[len(weights) + len(ordered) : -1]
        arrived = refs[-1]
        copies = []
        for i, top in enumerate(range(0, last - first, DEPTH_BLOCK)):
            for w, (out, left) in enumerate(places):
                copy = pltpu.make_async_copy(
                    sources[w].at[first + top : first + top + DEPTH_BLOCK, :],
                    outs[out].at[top : top + DEPTH_BLOCK, left : left + widths[w]],
                    arrived.at[i, w],
                )
                copy.start()
                copies.append(copy)
        for copy in copies:
            copy.wait()

    return pl.pallas_call(
        kernel,
        out_shape=[jax.ShapeDtypeStruct(shape, weights[0].dtype) for shape in shapes],
        in_specs=[whole(pltpu.HBM)] * len(weights) + [whole(pl.ANY)] * len(ordered),
        out_specs=[whole()] * len(shapes),
        scratch_shapes=[
            pltpu.SemaphoreType.DMA(((last - first) // DEPTH_BLOCK, len(weights)))
        ],
        compiler_params=pltpu.CompilerParams(vmem_limit_bytes=LOAD_LIMITS[part]),
        cost_estimate=pl.CostEstimate(
            flops=0, bytes_accessed=4 * (last - first) * sum(widths), transcendentals=0
        ),
        name="load_rows",
    )(*weights, *ordered)


def mixed_rows(rows, loaded, part, before, ordered):
    batch_rows, depth = rows.shape
    first, last = depth_cuts(depth)[part : part + 2]
    widths = [block.shape[1] for block in loaded]
    lefts = [sum(lane_tiles(width) for width in widths[:w]) for w in range(len(widths))]
    width = sum(lane_tiles(width) for width in widths)

    def kernel(rows_ref, *refs):
        out = refs[-1]
        for block, left, wide in zip(refs, lefts, widths):
            columns = slice(left, left + wide)
            product = jnp.dot(
                rows_ref[:, first:last], block[...], preferred_element_type=jnp.float32
            )
            if before is not None:
                product = refs[len(widths)][:, columns] + product
            out[:, columns] = product

    return call(
        kernel,
        jax.ShapeDtypeStruct((batch_rows, width), jnp.float32),
        [rows, *loaded] + ([] if before is None else [before]),
        "mixed_rows",
        ordered,
        cost_estimate=pl.CostEstimate(
            flops=2 * batch_rows * (last - first) * width,
            bytes_accessed=2 * (last - first) * width,
            transcendentals=0,
        ),
    )


def stream_rows(rows, weights, before, first, last, ordered):
    batch_rows = rows.shape[0]
    widths = [weight.shape[1] for weight in weights]
    lefts = [sum(lane_tiles(width) for width in widths[:w]) for w in range(len(weights))]
    width = sum(lane_tiles(width) for width in widths)
    if width == sum(widths):
        buffer_of, offsets = [0] * len(weights), lefts
        products = [(0, width)]
    else:
        buffer_of, offsets = list(range(len(weights))), [0] * len(weights)
        products = list(zip(lefts, widths))
    blocks = []
    at = first
    while at < last:
        depth = min(4 * DEPTH_BLOCK if blocks else 2 * DEPTH_BLOCK, last - at)
        blocks.append((at, depth))
        at += depth

    def kernel(rows_ref, *refs):
        sources = refs[: len(weights)]
        arrived = refs[-1]
        buffers = refs[-1 - len(products) : -1]
        out = refs[-2 - len(products)]
        copies = []
        for b, (at, depth) in enumerate(blocks):
            copies.append([])
            half = depth // 2
            for p in range(2):
                for w, source in enumerate(sources):
                    top = at - first + p * half
                    copy = pltpu.make_async_copy(
                        source.at[at + p * half : at + (p + 1) * half, :],
                        buffers[buffer_of[w]].at[
                            top : top + half, offsets[w] : offsets[w] + widths[w]
                        ],
                        arrived.at[b, 2 * w + p],
                    )
                    copy.start()
                    copies[-1].append(copy)
        for (at, depth), group in zip(blocks, copies):
            for copy in group:
                copy.wait()
            for (left, wide), buffer in zip(products, buffers):
                columns = slice(left, left + wide)
                product = jnp.dot(
                    rows_ref[:, at : at + depth],
                    buffer[at - first : at - first + depth, :],
                    preferred_element_type=jnp.float32,
                )
                if at > first:
                    product = out[:, columns] + product
                elif before is not None:
                    product = refs[len(weights)][:, columns] + product
                out[:, columns] = product

    return pl.pallas_call(
        kernel,
        out_shape=jax.ShapeDtypeStruct((batch_rows, width), jnp.float32),
        in_specs=[whole()]
        + [whole(pltpu.HBM)] * len(weights)
        + [whole()] * (before is not None)
        + [whole(pl.ANY)] * len(ordered),
        out_specs=whole(),
        scratch_shapes=[pltpu.VMEM((last - first, wide), rows.dtype) for _, wide in products]
        + [pltpu.SemaphoreType.DMA((len(blocks), 2 * len(weights)))],
        compiler_params=pltpu.CompilerParams(vmem_limit_bytes=STREAM_LIMIT),
        cost_estimate=pl.CostEstimate(
            flops=2 * batch_rows * (last - first) * width,
            bytes_accessed=STREAM_COST * (last - first) * width,
            transcendentals=0,
        ),
        name="stream_rows",
    )(rows, *weights, *([] if before is None else [before]), *ordered)


def hidden_kernel(coeff, recv, from_place, hot, expand, mixed, out, spread):
    rank_limit = coeff.shape[1]
    own = jnp.dot(
        from_place[...], coeff[...] + recv[...], preferred_element_type=jnp.float32
    ).astype(jnp.bfloat16)
    pair = jnp.concatenate([own, own], axis=1)
    for p in range(spread.shape[1] // (2 * rank_limit)):
        at = slice(p * 2 * rank_limit, (p + 1) * 2 * rank_limit)
        spread[:, at] = hot[:, at] * pair
    lora = jnp.dot(spread[...], expand[...], preferred_element_type=jnp.float32)
    width = out.shape[1]
    value = mixed[:, :width]
    total = mixed[:, lane_tiles(width) : lane_tiles(width) + width] + lora
    out[...] = (value / (1.0 + jnp.exp(-value)) * total).astype(jnp.bfloat16)


def hidden_rows(mixed, coeff, recv, expand_factors, from_place, hot):
    adapters, rank_limit, width = expand_factors.shape
    batch_rows = mixed.shape[0]
    expand = expand_factors.reshape(adapters * rank_limit, width)
    return call(
        hidden_kernel,
        jax.ShapeDtypeStruct((batch_rows, width), jnp.bfloat16),
        [coeff, recv, from_place, hot, expand, mixed],
        "hidden_rows",
        scratch_shapes=[pltpu.VMEM((batch_rows, adapters * rank_limit), jnp.bfloat16)],
        cost_estimate=pl.CostEstimate(
            flops=2 * batch_rows * adapters * rank_limit * width,
            bytes_accessed=2 * adapters * rank_limit * width,
            transcendentals=batch_rows * width,
        ),
    )


def add_blocks(sides, own_rows, ordered):
    operands, shapes = [], []
    for mine, theirs, _, arrived in sides:
        operands += [mine, theirs] + ([] if arrived is None else [arrived])
        shapes.append(jax.ShapeDtypeStruct((own_rows, mine.shape[1]), jnp.bfloat16))

    def kernel(*refs):
        refs = list(refs)
        outs = refs[-len(sides) :]
        for (_, _, index, arrived), out in zip(sides, outs):
            at = slice(index * own_rows, (index + 1) * own_rows)
            total = refs.pop(0)[at, :].astype(jnp.float32)
            total = total + refs.pop(0)[at, :].astype(jnp.float32)
            if arrived is not None:
                total = total + refs.pop(0)[...].astype(jnp.float32)
            out[...] = total.astype(jnp.bfloat16)

    return call(kernel, tuple(shapes), operands, "add_blocks", ordered)


def scatter_rows(mine, theirs, own_rows, size):
    chips = size // 2
    last = chips // 2
    right, left = [None] * HALVES, [None] * HALVES
    ordered = []
    for turn in range(last):
        chains = [(right, 1, 0), (left, -1, 1), (right, 1, 1), (left, -1, 0)]
        if turn == 0:
            chains = [chains[0], chains[3], chains[2], chains[1]]
        groups = [[chain] for chain in chains] if turn < last - 1 else [chains[:2]]
        for group in groups:
            sides = []
            for chain, by, h in group:
                longer = (by == 1) == (h == 0)
                steps = last - turn - (not longer)
                index = min(2 * steps, chips - 1) if by == 1 else 2 * steps - 1
                sides.append((mine[h], theirs[h], index, chain[h]))
            sums = add_blocks(sides, own_rows, ordered)
            ordered = [sums[0]]
            for (chain, by, h), value in zip(group, sums):
                chain[h] = lax.ppermute(value, AXIS, ring(size, by))
    return list(zip(mine, theirs, right, left))


def finish_rows(halves, activations, gain, own_rows):
    width = activations.shape[1] // HALVES

    def kernel(*refs):
        refs, (act, gain_ref, block_out, normed, stream) = refs[:-5], refs[-5:]
        square = jnp.zeros((own_rows, 1), jnp.float32)
        for h in range(HALVES):
            mine, theirs, right, left = refs[4 * h : 4 * h + 4]
            at = slice(h * width, (h + 1) * width)
            total = act[:, at].astype(jnp.float32)
            for ref in (mine, theirs):
                total = total + ref[:own_rows, :].astype(jnp.float32)
            for ref in (right, left):
                total = total + ref[...].astype(jnp.float32)
            stream[:, at] = total
            block_out[:, at] = total.astype(jnp.bfloat16)
            square = square + jnp.sum(total * total, axis=1, keepdims=True)
        scale = lax.rsqrt(square * (1.0 / act.shape[1]) + 1e-05)
        normed[...] = (stream[...] * scale * gain_ref[...].astype(jnp.float32)).astype(
            jnp.bfloat16
        )

    out = jax.ShapeDtypeStruct(activations.shape, jnp.bfloat16)
    return call(
        kernel,
        (out, out),
        [array for half in halves for array in half] + [activations, gain],
        "finish_rows",
        scratch_shapes=[pltpu.VMEM(activations.shape, jnp.float32)],
    )


def body(
    activations,
    gate_weight,
    up_weight,
    down_weight,
    norm_gain_vector,
    shrink_factors,
    expand_factors,
    adapter_ranks,
    adapter_storage_slot,
    segment_start,
    segment_adapter,
):
    size = lax.axis_size(AXIS)
    own_rows, model_width = activations.shape
    assert size & (size - 1) == 0 and own_rows & (own_rows - 1) == 0
    tables = (segment_start, segment_adapter, adapter_ranks, adapter_storage_slot)
    scale, to_place, from_place, hot, factor = row_masks(
        tables, shrink_factors, own_rows, size
    )

    parts, loads = gather_rows(activations, size, (gate_weight, up_weight), [scale])
    rows, coeff = shrink_rows(parts, factor, scale, to_place, shrink_factors.shape[2])

    bits = [1 << b for b in range(size.bit_length() - 1)]
    mixed = None
    for step, bit in enumerate(bits):
        received = lax.ppermute(coeff, AXIS, flip(size, bit))
        part = step - (len(bits) - LOADS - 1)
        if part == LOADS:
            cuts = depth_cuts(model_width)
            mixed = stream_rows(
                rows, (gate_weight, up_weight), mixed, cuts[part], cuts[part + 1], [coeff]
            )
        elif part >= 0:
            mixed = mixed_rows(rows, loads[part], part, mixed, [coeff])
        if bit < bits[-1]:
            coeff = add_coefficients(coeff, received, [] if mixed is None else [mixed])
    hidden = hidden_rows(mixed, coeff, received, expand_factors, from_place, hot)

    half = size * own_rows // 2
    width = model_width // HALVES
    mine, theirs = [None] * HALVES, [None] * HALVES
    for h in range(HALVES):
        term = jnp.dot(
            hidden,
            down_weight[:, h * width : (h + 1) * width],
            preferred_element_type=jnp.float32,
        ).astype(jnp.bfloat16)
        mine[h] = term
        theirs[h] = lax.ppermute(term[half:], AXIS, flip(size, 1))
    halves = scatter_rows(mine, theirs, own_rows, size)
    return finish_rows(halves, activations, norm_gain_vector[None], own_rows)


def solution(mesh):
    return jax.shard_map(
        body,
        mesh=mesh,
        in_specs=(
            P(("groups", "mp"), None),
            P(None, "mp"),
            P(None, "mp"),
            P("mp", None),
            P(),
            P("mp", None, None),
            P(None, None, "mp"),
            P(),
            P(),
            P("groups"),
            P("groups"),
        ),
        out_specs=(P(("groups", "mp"), None), P(("groups", "mp"), None)),
        check_vma=False,
    )
```

```python
import functools

import jax
import jax.numpy as jnp
from jax import lax
from jax.experimental import pallas as pl
from jax.experimental.pallas import tpu as pltpu
from jax.sharding import PartitionSpec as P

adapter_alpha = 32.0
AXIS = "mp"
HALVES = 2
DEPTH_BLOCK = 256
LOADS = 2
VMEM_LIMIT = 12 * 1024 * 1024
LOAD_LIMITS = [mb * 1024 * 1024 for mb in (42, 36)]
STREAM_LIMIT = 34 * 1024 * 1024
STREAM_COST = 4


def chip_at(place, chips):
    if chips == 8:
        return jnp.where(place < 4, 2 * place, 2 * (7 - place) + 1)
    return place


def place_of(chip, chips):
    if chips == 8:
        return jnp.where((chip & 1) == 0, chip >> 1, 7 - (chip >> 1))
    return chip


def ring(size, by):
    chips = size // 2
    order = [0, 2, 4, 6, 7, 5, 3, 1] if chips == 8 else list(range(chips))
    pairs = []
    for place, chip in enumerate(order):
        to = order[(place + by) % chips]
        pairs += [(2 * chip + core, 2 * to + core) for core in range(2)]
    return pairs


def flip(size, bit):
    return [(i, i ^ bit) for i in range(size)]


def row_positions(me, row, own_rows, size):
    chips = size // 2
    block = row // own_rows
    index = block & (chips - 1)
    step = (index + 1) >> 1
    delta = jnp.where((index & 1) == 1, step, -step)
    place = (place_of(me >> 1, chips) - delta + chips) & (chips - 1)
    core = (me & 1) ^ (block // chips)
    return (2 * chip_at(place, chips) + core) * own_rows + (row & (own_rows - 1))


def pick(index, table):
    hot = index == lax.broadcasted_iota(jnp.int32, (1, table.shape[1]), 1)
    return jnp.sum(jnp.where(hot, table, 0), axis=1, keepdims=True)


def row_adapters(position, start, adapters):
    segment = jnp.sum((start <= position).astype(jnp.int32), axis=1, keepdims=True) - 1
    return pick(segment, adapters)


def whole(space=pltpu.VMEM):
    return pl.BlockSpec(memory_space=space)


def call(kernel, out_shape, operands, name, ordered=(), limit=VMEM_LIMIT, **options):
    count = len(operands)

    def run(*refs):
        kernel(*refs[:count], *refs[count + len(ordered) :])

    return pl.pallas_call(
        run,
        out_shape=out_shape,
        in_specs=[
            whole(pltpu.SMEM if operand.ndim == 1 else pltpu.VMEM) for operand in operands
        ]
        + [whole(pl.ANY)] * len(ordered),
        out_specs=jax.tree.map(lambda _: whole(), out_shape),
        compiler_params=pltpu.CompilerParams(vmem_limit_bytes=limit),
        name=name,
        **options,
    )(*operands, *ordered)


def column_half(array, h):
    rows, columns = array.shape
    width = columns // HALVES

    def kernel(ref, out):
        out[...] = ref[:, h * width : (h + 1) * width]

    return call(
        kernel, jax.ShapeDtypeStruct((rows, width), array.dtype), [array], "column_half"
    )


def pass_on(array, ordered):
    def kernel(ref, out):
        out[...] = ref[...]

    return call(
        kernel, jax.ShapeDtypeStruct(array.shape, array.dtype), [array], "pass_on", ordered
    )


def join(pieces, columns, ordered=()):
    rows, width = pieces[0].shape
    across = columns // width

    def kernel(*refs):
        out = refs[-1]
        for i, ref in enumerate(refs[:-1]):
            top, left = i // across * rows, i % across * width
            out[top : top + rows, left : left + width] = ref[...]

    shape = (rows * len(pieces) // across, columns)
    return call(
        kernel, jax.ShapeDtypeStruct(shape, pieces[0].dtype), pieces, "join_pieces", ordered
    )


def gather_rows(own, size, weights, ordered):
    chips = size // 2
    last = chips // 2
    columns = own.shape[1]
    right = left = own
    pieces, loads = [], []
    mine, theirs = [own], []
    for step in range(1, last):
        before = right
        right = lax.ppermute(right, AXIS, ring(size, 1))
        left = lax.ppermute(left, AXIS, ring(size, -1))
        if step == 1:
            theirs.append(lax.ppermute(own, AXIS, flip(size, 1)))
        pieces += [right, left]
        if step <= LOADS:
            loads.append(load_rows(weights, step - 1, [before] if step > 1 else []))
            right = pass_on(right, loads[-1])
    part = join(pieces, columns, ordered)
    mine.append(part)
    theirs.append(lax.ppermute(part, AXIS, flip(size, 1)))
    part = join(
        [
            lax.ppermute(column_half(right, 0), AXIS, ring(size, 1)),
            lax.ppermute(column_half(left, 1), AXIS, ring(size, -1)),
        ],
        columns,
    )
    mine.append(part)
    theirs.append(lax.ppermute(part, AXIS, flip(size, 1)))
    return mine + theirs, loads


def row_masks(tables, shrink_factors, own_rows, size):
    batch_rows = own_rows * size
    slots, model_width, rank_limit = shrink_factors.shape
    factor = jnp.swapaxes(shrink_factors, 1, 2).reshape(slots * rank_limit, model_width)
    adapters = tables[2].shape[0]

    def kernel(*refs):
        start, segment_adapter, ranks, slot_of = (ref[...] for ref in refs[:4])
        factor_in, scale, to_place, from_place, hot, factor_out = refs[4:]
        factor_out[...] = factor_in[...]
        me = lax.axis_index(AXIS)
        row = lax.broadcasted_iota(jnp.int32, (batch_rows, 1), 0)
        column = lax.broadcasted_iota(jnp.int32, (1, batch_rows), 1)
        position = row_positions(me, row, own_rows, size)
        adapter = row_adapters(position, start, segment_adapter)
        rank = pick(adapter, ranks)
        slot = pick(adapter, slot_of) - me * slots
        at = lax.broadcasted_iota(jnp.int32, (1, slots * rank_limit), 1)
        keep = (at // rank_limit == slot) & (at % rank_limit < rank)
        scale[...] = jnp.where(keep, adapter_alpha / rank.astype(jnp.float32), 0.0)
        to_place[...] = (row_positions(me, column, own_rows, size) == row).astype(jnp.bfloat16)
        from_place[...] = (position == column).astype(jnp.bfloat16)
        depth = lax.broadcasted_iota(jnp.int32, (1, adapters * rank_limit), 1)
        hot[...] = (depth // rank_limit == adapter).astype(jnp.bfloat16)

    shapes = (
        jax.ShapeDtypeStruct((batch_rows, slots * rank_limit), jnp.float32),
        jax.ShapeDtypeStruct((batch_rows, batch_rows), jnp.bfloat16),
        jax.ShapeDtypeStruct((batch_rows, batch_rows), jnp.bfloat16),
        jax.ShapeDtypeStruct((batch_rows, adapters * rank_limit), jnp.bfloat16),
        jax.ShapeDtypeStruct(factor.shape, factor.dtype),
    )
    return call(kernel, shapes, [*(table[None] for table in tables), factor], "row_masks")


def shrink_rows(parts, factor, scale, to_place, rank_limit):
    model_width = factor.shape[1]
    slots = factor.shape[0] // rank_limit
    batch_rows = to_place.shape[0]
    width = model_width // 2

    def kernel(*refs):
        factor_ref, scale_ref, place_ref, rows_out, coeff_out, total = refs[len(parts) :]

        def columns(k, _):
            at = pl.ds(pl.multiple_of(k * width, width), width)
            top = 0
            for part in refs[: len(parts)]:
                rows_out[top : top + part.shape[0], at] = part[:, at]
                top += part.shape[0]
            product = lax.dot_general(
                rows_out[:, at],
                factor_ref[:, at],
                (((1,), (1,)), ((), ())),
                preferred_element_type=jnp.float32,
            )
            total[...] = jnp.where(k == 0, product, total[...] + product)
            return 0

        lax.fori_loop(0, model_width // width, columns, 0)
        scaled = total[...] * scale_ref[...]
        coeff = scaled[:, :rank_limit]
        for s in range(1, slots):
            coeff = coeff + scaled[:, s * rank_limit : (s + 1) * rank_limit]
        coeff_out[...] = jnp.dot(
            place_ref[...], coeff.astype(jnp.bfloat16), preferred_element_type=jnp.float32
        ).astype(jnp.bfloat16)

    return call(
        kernel,
        (
            jax.ShapeDtypeStruct((batch_rows, model_width), jnp.bfloat16),
            jax.ShapeDtypeStruct((batch_rows, rank_limit), jnp.bfloat16),
        ),
        [*parts, factor, scale, to_place],
        "shrink_rows",
        scratch_shapes=[pltpu.VMEM((batch_rows, slots * rank_limit), jnp.float32)],
        cost_estimate=pl.CostEstimate(
            flops=2 * batch_rows * model_width * slots * rank_limit,
            bytes_accessed=4 * batch_rows * model_width,
            transcendentals=0,
        ),
    )


def add_coefficients(a, b, ordered):
    def kernel(a_ref, b_ref, out):
        out[...] = a_ref[...] + b_ref[...]

    return call(
        kernel, jax.ShapeDtypeStruct(a.shape, a.dtype), [a, b], "add_coefficients", ordered
    )


def lane_tiles(width):
    return -(-width // 128) * 128


def depth_cuts(depth):
    part = -(-13 * depth // 32 // DEPTH_BLOCK) * DEPTH_BLOCK
    return [part * p for p in range(LOADS + 1)] + [depth]


def load_rows(weights, part, ordered):
    depth = weights[0].shape[0]
    first, last = depth_cuts(depth)[part : part + 2]
    widths = [weight.shape[1] for weight in weights]
    if all(width % 128 == 0 for width in widths):
        places = [(0, sum(widths[:w])) for w in range(len(weights))]
        shapes = [(last - first, sum(widths))]
    else:
        places = [(w, 0) for w in range(len(weights))]
        shapes = [(last - first, width) for width in widths]

    def kernel(*refs):
        sources = refs[: len(weights)]
        outs = refs[len(weights) + len(ordered) : -1]
        arrived = refs[-1]
        copies = []
        for i, top in enumerate(range(0, last - first, DEPTH_BLOCK)):
            for w, (out, left) in enumerate(places):
                copy = pltpu.make_async_copy(
                    sources[w].at[first + top : first + top + DEPTH_BLOCK, :],
                    outs[out].at[top : top + DEPTH_BLOCK, left : left + widths[w]],
                    arrived.at[i, w],
                )
                copy.start()
                copies.append(copy)
        for copy in copies:
            copy.wait()

    return pl.pallas_call(
        kernel,
        out_shape=[jax.ShapeDtypeStruct(shape, weights[0].dtype) for shape in shapes],
        in_specs=[whole(pltpu.HBM)] * len(weights) + [whole(pl.ANY)] * len(ordered),
        out_specs=[whole()] * len(shapes),
        scratch_shapes=[
            pltpu.SemaphoreType.DMA(((last - first) // DEPTH_BLOCK, len(weights)))
        ],
        compiler_params=pltpu.CompilerParams(vmem_limit_bytes=LOAD_LIMITS[part]),
        cost_estimate=pl.CostEstimate(
            flops=0, bytes_accessed=4 * (last - first) * sum(widths), transcendentals=0
        ),
        name="load_rows",
    )(*weights, *ordered)


def mixed_rows(rows, loaded, part, before, ordered):
    batch_rows, depth = rows.shape
    first, last = depth_cuts(depth)[part : part + 2]
    widths = [block.shape[1] for block in loaded]
    lefts = [sum(lane_tiles(width) for width in widths[:w]) for w in range(len(widths))]
    width = sum(lane_tiles(width) for width in widths)

    def kernel(rows_ref, *refs):
        out = refs[-1]
        for block, left, wide in zip(refs, lefts, widths):
            columns = slice(left, left + wide)
            product = jnp.dot(
                rows_ref[:, first:last], block[...], preferred_element_type=jnp.float32
            )
            if before is not None:
                product = refs[len(widths)][:, columns] + product
            out[:, columns] = product

    return call(
        kernel,
        jax.ShapeDtypeStruct((batch_rows, width), jnp.float32),
        [rows, *loaded] + ([] if before is None else [before]),
        "mixed_rows",
        ordered,
        cost_estimate=pl.CostEstimate(
            flops=2 * batch_rows * (last - first) * width,
            bytes_accessed=2 * (last - first) * width,
            transcendentals=0,
        ),
    )


def stream_rows(rows, weights, before, first, last, ordered):
    batch_rows = rows.shape[0]
    widths = [weight.shape[1] for weight in weights]
    lefts = [sum(lane_tiles(width) for width in widths[:w]) for w in range(len(weights))]
    width = sum(lane_tiles(width) for width in widths)
    if width == sum(widths):
        buffer_of, offsets = [0] * len(weights), lefts
        products = [(0, width)]
    else:
        buffer_of, offsets = list(range(len(weights))), [0] * len(weights)
        products = list(zip(lefts, widths))
    blocks = []
    at = first
    while at < last:
        depth = min(4 * DEPTH_BLOCK if blocks else 2 * DEPTH_BLOCK, last - at)
        blocks.append((at, depth))
        at += depth

    def kernel(rows_ref, *refs):
        sources = refs[: len(weights)]
        arrived = refs[-1]
        buffers = refs[-1 - len(products) : -1]
        out = refs[-2 - len(products)]
        copies = []
        for b, (at, depth) in enumerate(blocks):
            copies.append([])
            half = depth // 2
            for p in range(2):
                for w, source in enumerate(sources):
                    top = at - first + p * half
                    copy = pltpu.make_async_copy(
                        source.at[at + p * half : at + (p + 1) * half, :],
                        buffers[buffer_of[w]].at[
                            top : top + half, offsets[w] : offsets[w] + widths[w]
                        ],
                        arrived.at[b, 2 * w + p],
                    )
                    copy.start()
                    copies[-1].append(copy)
        for (at, depth), group in zip(blocks, copies):
            for copy in group:
                copy.wait()
            for (left, wide), buffer in zip(products, buffers):
                columns = slice(left, left + wide)
                product = jnp.dot(
                    rows_ref[:, at : at + depth],
                    buffer[at - first : at - first + depth, :],
                    preferred_element_type=jnp.float32,
                )
                if at > first:
                    product = out[:, columns] + product
                elif before is not None:
                    product = refs[len(weights)][:, columns] + product
                out[:, columns] = product

    return pl.pallas_call(
        kernel,
        out_shape=jax.ShapeDtypeStruct((batch_rows, width), jnp.float32),
        in_specs=[whole()]
        + [whole(pltpu.HBM)] * len(weights)
        + [whole()] * (before is not None)
        + [whole(pl.ANY)] * len(ordered),
        out_specs=whole(),
        scratch_shapes=[pltpu.VMEM((last - first, wide), rows.dtype) for _, wide in products]
        + [pltpu.SemaphoreType.DMA((len(blocks), 2 * len(weights)))],
        compiler_params=pltpu.CompilerParams(vmem_limit_bytes=STREAM_LIMIT),
        cost_estimate=pl.CostEstimate(
            flops=2 * batch_rows * (last - first) * width,
            bytes_accessed=STREAM_COST * (last - first) * width,
            transcendentals=0,
        ),
        name="stream_rows",
    )(rows, *weights, *([] if before is None else [before]), *ordered)


def hidden_kernel(coeff, recv, from_place, hot, expand, mixed, out, spread):
    rank_limit = coeff.shape[1]
    own = jnp.dot(
        from_place[...], coeff[...] + recv[...], preferred_element_type=jnp.float32
    ).astype(jnp.bfloat16)
    pair = jnp.concatenate([own, own], axis=1)
    for p in range(spread.shape[1] // (2 * rank_limit)):
        at = slice(p * 2 * rank_limit, (p + 1) * 2 * rank_limit)
        spread[:, at] = hot[:, at] * pair
    lora = jnp.dot(spread[...], expand[...], preferred_element_type=jnp.float32)
    width = out.shape[1]
    value = mixed[:, :width]
    total = mixed[:, lane_tiles(width) : lane_tiles(width) + width] + lora
    out[...] = (value / (1.0 + jnp.exp(-value)) * total).astype(jnp.bfloat16)


def hidden_rows(mixed, coeff, recv, expand_factors, from_place, hot):
    adapters, rank_limit, width = expand_factors.shape
    batch_rows = mixed.shape[0]
    expand = expand_factors.reshape(adapters * rank_limit, width)
    return call(
        hidden_kernel,
        jax.ShapeDtypeStruct((batch_rows, width), jnp.bfloat16),
        [coeff, recv, from_place, hot, expand, mixed],
        "hidden_rows",
        scratch_shapes=[pltpu.VMEM((batch_rows, adapters * rank_limit), jnp.bfloat16)],
        cost_estimate=pl.CostEstimate(
            flops=2 * batch_rows * adapters * rank_limit * width,
            bytes_accessed=2 * adapters * rank_limit * width,
            transcendentals=batch_rows * width,
        ),
    )


def add_blocks(sides, own_rows, ordered):
    operands, shapes = [], []
    for mine, theirs, _, arrived in sides:
        operands += [mine, theirs] + ([] if arrived is None else [arrived])
        shapes.append(jax.ShapeDtypeStruct((own_rows, mine.shape[1]), jnp.bfloat16))

    def kernel(*refs):
        refs = list(refs)
        outs = refs[-len(sides) :]
        for (_, _, index, arrived), out in zip(sides, outs):
            at = slice(index * own_rows, (index + 1) * own_rows)
            total = refs.pop(0)[at, :].astype(jnp.float32)
            total = total + refs.pop(0)[at, :].astype(jnp.float32)
            if arrived is not None:
                total = total + refs.pop(0)[...].astype(jnp.float32)
            out[...] = total.astype(jnp.bfloat16)

    return call(kernel, tuple(shapes), operands, "add_blocks", ordered)


def scatter_rows(mine, theirs, own_rows, size):
    chips = size // 2
    last = chips // 2
    right, left = [None] * HALVES, [None] * HALVES
    ordered = []
    for turn in range(last):
        chains = [(right, 1, 0), (left, -1, 1), (right, 1, 1), (left, -1, 0)]
        groups = [[chain] for chain in chains]
        if turn < 2:
            groups = [[chains[0], chains[3]], [chains[1]], [chains[2]]]
        if turn == last - 1:
            groups = [chains[:2]]
        for group in groups:
            sides = []
            for chain, by, h in group:
                longer = (by == 1) == (h == 0)
                steps = last - turn - (not longer)
                index = min(2 * steps, chips - 1) if by == 1 else 2 * steps - 1
                sides.append((mine[h], theirs[h], index, chain[h]))
            sums = add_blocks(sides, own_rows, ordered)
            ordered = [sums[0]]
            for (chain, by, h), value in zip(group, sums):
                chain[h] = lax.ppermute(value, AXIS, ring(size, by))
    return list(zip(mine, theirs, right, left))


def finish_rows(halves, activations, gain, own_rows):
    width = activations.shape[1] // HALVES

    def kernel(*refs):
        refs, (act, gain_ref, block_out, normed, stream) = refs[:-5], refs[-5:]
        square = jnp.zeros((own_rows, 1), jnp.float32)
        for h in range(HALVES):
            mine, theirs, right, left = refs[4 * h : 4 * h + 4]
            at = slice(h * width, (h + 1) * width)
            total = act[:, at].astype(jnp.float32)
            for ref in (mine, theirs):
                total = total + ref[:own_rows, :].astype(jnp.float32)
            for ref in (right, left):
                total = total + ref[...].astype(jnp.float32)
            stream[:, at] = total
            block_out[:, at] = total.astype(jnp.bfloat16)
            square = square + jnp.sum(total * total, axis=1, keepdims=True)
        scale = lax.rsqrt(square * (1.0 / act.shape[1]) + 1e-05)
        normed[...] = (stream[...] * scale * gain_ref[...].astype(jnp.float32)).astype(
            jnp.bfloat16
        )

    out = jax.ShapeDtypeStruct(activations.shape, jnp.bfloat16)
    return call(
        kernel,
        (out, out),
        [array for half in halves for array in half] + [activations, gain],
        "finish_rows",
        scratch_shapes=[pltpu.VMEM(activations.shape, jnp.float32)],
    )


def body(
    activations,
    gate_weight,
    up_weight,
    down_weight,
    norm_gain_vector,
    shrink_factors,
    expand_factors,
    adapter_ranks,
    adapter_storage_slot,
    segment_start,
    segment_adapter,
):
    size = lax.axis_size(AXIS)
    own_rows, model_width = activations.shape
    assert size & (size - 1) == 0 and own_rows & (own_rows - 1) == 0
    tables = (segment_start, segment_adapter, adapter_ranks, adapter_storage_slot)
    scale, to_place, from_place, hot, factor = row_masks(
        tables, shrink_factors, own_rows, size
    )

    parts, loads = gather_rows(activations, size, (gate_weight, up_weight), [scale])
    rows, coeff = shrink_rows(parts, factor, scale, to_place, shrink_factors.shape[2])

    bits = [1 << b for b in range(size.bit_length() - 1)]
    mixed = None
    for step, bit in enumerate(bits):
        received = lax.ppermute(coeff, AXIS, flip(size, bit))
        part = step - (len(bits) - LOADS - 1)
        if part == LOADS:
            cuts = depth_cuts(model_width)
            mixed = stream_rows(
                rows, (gate_weight, up_weight), mixed, cuts[part], cuts[part + 1], [coeff]
            )
        elif part >= 0:
            mixed = mixed_rows(rows, loads[part], part, mixed, [coeff])
        if bit < bits[-1]:
            coeff = add_coefficients(coeff, received, [] if mixed is None else [mixed])
    hidden = hidden_rows(mixed, coeff, received, expand_factors, from_place, hot)

    half = size * own_rows // 2
    width = model_width // HALVES
    mine, theirs = [None] * HALVES, [None] * HALVES
    for h in range(HALVES):
        term = jnp.dot(
            hidden,
            down_weight[:, h * width : (h + 1) * width],
            preferred_element_type=jnp.float32,
        ).astype(jnp.bfloat16)
        mine[h] = term
        theirs[h] = lax.ppermute(term[half:], AXIS, flip(size, 1))
    halves = scatter_rows(mine, theirs, own_rows, size)
    return finish_rows(halves, activations, norm_gain_vector[None], own_rows)


def solution(mesh):
    return jax.shard_map(
        body,
        mesh=mesh,
        in_specs=(
            P(("groups", "mp"), None),
            P(None, "mp"),
            P(None, "mp"),
            P("mp", None),
            P(),
            P("mp", None, None),
            P(None, None, "mp"),
            P(),
            P(),
            P("groups"),
            P("groups"),
        ),
        out_specs=(P(("groups", "mp"), None), P(("groups", "mp"), None)),
        check_vma=False,
    )
```

```python
import functools

import jax
import jax.numpy as jnp
from jax import lax
from jax.experimental import pallas as pl
from jax.experimental.pallas import tpu as pltpu
from jax.sharding import PartitionSpec as P

adapter_alpha = 32.0
AXIS = "mp"
HALVES = 2
DEPTH_BLOCK = 256
LOADS = 2
VMEM_LIMIT = 12 * 1024 * 1024
LOAD_LIMITS = [mb * 1024 * 1024 for mb in (42, 36)]
STREAM_LIMIT = 34 * 1024 * 1024
STREAM_COST = 4


def chip_at(place, chips):
    if chips == 8:
        return jnp.where(place < 4, 2 * place, 2 * (7 - place) + 1)
    return place


def place_of(chip, chips):
    if chips == 8:
        return jnp.where((chip & 1) == 0, chip >> 1, 7 - (chip >> 1))
    return chip


def ring(size, by):
    chips = size // 2
    order = [0, 2, 4, 6, 7, 5, 3, 1] if chips == 8 else list(range(chips))
    pairs = []
    for place, chip in enumerate(order):
        to = order[(place + by) % chips]
        pairs += [(2 * chip + core, 2 * to + core) for core in range(2)]
    return pairs


def flip(size, bit):
    return [(i, i ^ bit) for i in range(size)]


def row_positions(me, row, own_rows, size):
    chips = size // 2
    block = row // own_rows
    index = block & (chips - 1)
    step = (index + 1) >> 1
    delta = jnp.where((index & 1) == 1, step, -step)
    place = (place_of(me >> 1, chips) - delta + chips) & (chips - 1)
    core = (me & 1) ^ (block // chips)
    return (2 * chip_at(place, chips) + core) * own_rows + (row & (own_rows - 1))


def pick(index, table):
    hot = index == lax.broadcasted_iota(jnp.int32, (1, table.shape[1]), 1)
    return jnp.sum(jnp.where(hot, table, 0), axis=1, keepdims=True)


def row_adapters(position, start, adapters):
    segment = jnp.sum((start <= position).astype(jnp.int32), axis=1, keepdims=True) - 1
    return pick(segment, adapters)


def whole(space=pltpu.VMEM):
    return pl.BlockSpec(memory_space=space)


def call(kernel, out_shape, operands, name, ordered=(), limit=VMEM_LIMIT, **options):
    count = len(operands)

    def run(*refs):
        kernel(*refs[:count], *refs[count + len(ordered) :])

    return pl.pallas_call(
        run,
        out_shape=out_shape,
        in_specs=[
            whole(pltpu.SMEM if operand.ndim == 1 else pltpu.VMEM) for operand in operands
        ]
        + [whole(pl.ANY)] * len(ordered),
        out_specs=jax.tree.map(lambda _: whole(), out_shape),
        compiler_params=pltpu.CompilerParams(vmem_limit_bytes=limit),
        name=name,
        **options,
    )(*operands, *ordered)


def column_half(array, h):
    rows, columns = array.shape
    width = columns // HALVES

    def kernel(ref, out):
        out[...] = ref[:, h * width : (h + 1) * width]

    return call(
        kernel, jax.ShapeDtypeStruct((rows, width), array.dtype), [array], "column_half"
    )


def pass_on(array, ordered):
    def kernel(ref, out):
        out[...] = ref[...]

    return call(
        kernel, jax.ShapeDtypeStruct(array.shape, array.dtype), [array], "pass_on", ordered
    )


def join(pieces, columns, ordered=()):
    rows, width = pieces[0].shape
    across = columns // width

    def kernel(*refs):
        out = refs[-1]
        for i, ref in enumerate(refs[:-1]):
            top, left = i // across * rows, i % across * width
            out[top : top + rows, left : left + width] = ref[...]

    shape = (rows * len(pieces) // across, columns)
    return call(
        kernel, jax.ShapeDtypeStruct(shape, pieces[0].dtype), pieces, "join_pieces", ordered
    )


def gather_rows(own, size, weights, ordered):
    chips = size // 2
    last = chips // 2
    columns = own.shape[1]
    right = left = own
    pieces, loads = [], []
    mine, theirs = [own], []
    for step in range(1, last):
        before = right
        right = lax.ppermute(right, AXIS, ring(size, 1))
        left = lax.ppermute(left, AXIS, ring(size, -1))
        if step == 1:
            theirs.append(lax.ppermute(own, AXIS, flip(size, 1)))
        pieces += [right, left]
        if step <= LOADS:
            loads.append(load_rows(weights, step - 1, [before] if step > 1 else []))
            right = pass_on(right, loads[-1])
    part = join(pieces, columns, ordered)
    mine.append(part)
    theirs.append(lax.ppermute(part, AXIS, flip(size, 1)))
    part = join(
        [
            lax.ppermute(column_half(right, 0), AXIS, ring(size, 1)),
            lax.ppermute(column_half(left, 1), AXIS, ring(size, -1)),
        ],
        columns,
    )
    mine.append(part)
    theirs.append(lax.ppermute(part, AXIS, flip(size, 1)))
    return mine + theirs, loads


def row_masks(tables, shrink_factors, own_rows, size):
    batch_rows = own_rows * size
    slots, model_width, rank_limit = shrink_factors.shape
    factor = jnp.swapaxes(shrink_factors, 1, 2).reshape(slots * rank_limit, model_width)
    adapters = tables[2].shape[0]

    def kernel(*refs):
        start, segment_adapter, ranks, slot_of = (ref[...] for ref in refs[:4])
        factor_in, scale, to_place, from_place, hot, factor_out = refs[4:]
        factor_out[...] = factor_in[...]
        me = lax.axis_index(AXIS)
        row = lax.broadcasted_iota(jnp.int32, (batch_rows, 1), 0)
        column = lax.broadcasted_iota(jnp.int32, (1, batch_rows), 1)
        position = row_positions(me, row, own_rows, size)
        adapter = row_adapters(position, start, segment_adapter)
        rank = pick(adapter, ranks)
        slot = pick(adapter, slot_of) - me * slots
        at = lax.broadcasted_iota(jnp.int32, (1, slots * rank_limit), 1)
        keep = (at // rank_limit == slot) & (at % rank_limit < rank)
        scale[...] = jnp.where(keep, adapter_alpha / rank.astype(jnp.float32), 0.0)
        to_place[...] = (row_positions(me, column, own_rows, size) == row).astype(jnp.bfloat16)
        from_place[...] = (position == column).astype(jnp.bfloat16)
        depth = lax.broadcasted_iota(jnp.int32, (1, adapters * rank_limit), 1)
        hot[...] = (depth // rank_limit == adapter).astype(jnp.bfloat16)

    shapes = (
        jax.ShapeDtypeStruct((batch_rows, slots * rank_limit), jnp.float32),
        jax.ShapeDtypeStruct((batch_rows, batch_rows), jnp.bfloat16),
        jax.ShapeDtypeStruct((batch_rows, batch_rows), jnp.bfloat16),
        jax.ShapeDtypeStruct((batch_rows, adapters * rank_limit), jnp.bfloat16),
        jax.ShapeDtypeStruct(factor.shape, factor.dtype),
    )
    return call(kernel, shapes, [*(table[None] for table in tables), factor], "row_masks")


def shrink_rows(parts, factor, scale, to_place, rank_limit):
    model_width = factor.shape[1]
    slots = factor.shape[0] // rank_limit
    batch_rows = to_place.shape[0]
    width = model_width // 2

    def kernel(*refs):
        factor_ref, scale_ref, place_ref, rows_out, coeff_out, total = refs[len(parts) :]

        def columns(k, _):
            at = pl.ds(pl.multiple_of(k * width, width), width)
            top = 0
            for part in refs[: len(parts)]:
                rows_out[top : top + part.shape[0], at] = part[:, at]
                top += part.shape[0]
            product = lax.dot_general(
                rows_out[:, at],
                factor_ref[:, at],
                (((1,), (1,)), ((), ())),
                preferred_element_type=jnp.float32,
            )
            total[...] = jnp.where(k == 0, product, total[...] + product)
            return 0

        lax.fori_loop(0, model_width // width, columns, 0)
        scaled = total[...] * scale_ref[...]
        coeff = scaled[:, :rank_limit]
        for s in range(1, slots):
            coeff = coeff + scaled[:, s * rank_limit : (s + 1) * rank_limit]
        coeff_out[...] = jnp.dot(
            place_ref[...], coeff.astype(jnp.bfloat16), preferred_element_type=jnp.float32
        ).astype(jnp.bfloat16)

    return call(
        kernel,
        (
            jax.ShapeDtypeStruct((batch_rows, model_width), jnp.bfloat16),
            jax.ShapeDtypeStruct((batch_rows, rank_limit), jnp.bfloat16),
        ),
        [*parts, factor, scale, to_place],
        "shrink_rows",
        scratch_shapes=[pltpu.VMEM((batch_rows, slots * rank_limit), jnp.float32)],
        cost_estimate=pl.CostEstimate(
            flops=2 * batch_rows * model_width * slots * rank_limit,
            bytes_accessed=4 * batch_rows * model_width,
            transcendentals=0,
        ),
    )


def add_coefficients(a, b, ordered):
    def kernel(a_ref, b_ref, out):
        out[...] = a_ref[...] + b_ref[...]

    return call(
        kernel, jax.ShapeDtypeStruct(a.shape, a.dtype), [a, b], "add_coefficients", ordered
    )


def lane_tiles(width):
    return -(-width // 128) * 128


def depth_cuts(depth):
    part = -(-13 * depth // 32 // DEPTH_BLOCK) * DEPTH_BLOCK
    return [part * p for p in range(LOADS + 1)] + [depth]


def load_rows(weights, part, ordered):
    depth = weights[0].shape[0]
    first, last = depth_cuts(depth)[part : part + 2]
    widths = [weight.shape[1] for weight in weights]
    if all(width % 128 == 0 for width in widths):
        places = [(0, sum(widths[:w])) for w in range(len(weights))]
        shapes = [(last - first, sum(widths))]
    else:
        places = [(w, 0) for w in range(len(weights))]
        shapes = [(last - first, width) for width in widths]

    def kernel(*refs):
        sources = refs[: len(weights)]
        outs = refs[len(weights) + len(ordered) : -1]
        arrived = refs[-1]
        copies = []
        for i, top in enumerate(range(0, last - first, DEPTH_BLOCK)):
            for w, (out, left) in enumerate(places):
                copy = pltpu.make_async_copy(
                    sources[w].at[first + top : first + top + DEPTH_BLOCK, :],
                    outs[out].at[top : top + DEPTH_BLOCK, left : left + widths[w]],
                    arrived.at[i, w],
                )
                copy.start()
                copies.append(copy)
        for copy in copies:
            copy.wait()

    return pl.pallas_call(
        kernel,
        out_shape=[jax.ShapeDtypeStruct(shape, weights[0].dtype) for shape in shapes],
        in_specs=[whole(pltpu.HBM)] * len(weights) + [whole(pl.ANY)] * len(ordered),
        out_specs=[whole()] * len(shapes),
        scratch_shapes=[
            pltpu.SemaphoreType.DMA(((last - first) // DEPTH_BLOCK, len(weights)))
        ],
        compiler_params=pltpu.CompilerParams(vmem_limit_bytes=LOAD_LIMITS[part]),
        cost_estimate=pl.CostEstimate(
            flops=0, bytes_accessed=4 * (last - first) * sum(widths), transcendentals=0
        ),
        name="load_rows",
    )(*weights, *ordered)


def mixed_rows(rows, loaded, part, before, ordered):
    batch_rows, depth = rows.shape
    first, last = depth_cuts(depth)[part : part + 2]
    widths = [block.shape[1] for block in loaded]
    lefts = [sum(lane_tiles(width) for width in widths[:w]) for w in range(len(widths))]
    width = sum(lane_tiles(width) for width in widths)

    def kernel(rows_ref, *refs):
        out = refs[-1]
        for block, left, wide in zip(refs, lefts, widths):
            columns = slice(left, left + wide)
            product = jnp.dot(
                rows_ref[:, first:last], block[...], preferred_element_type=jnp.float32
            )
            if before is not None:
                product = refs[len(widths)][:, columns] + product
            out[:, columns] = product

    return call(
        kernel,
        jax.ShapeDtypeStruct((batch_rows, width), jnp.float32),
        [rows, *loaded] + ([] if before is None else [before]),
        "mixed_rows",
        ordered,
        cost_estimate=pl.CostEstimate(
            flops=2 * batch_rows * (last - first) * width,
            bytes_accessed=2 * (last - first) * width,
            transcendentals=0,
        ),
    )


def stream_rows(rows, weights, before, first, last, ordered):
    batch_rows = rows.shape[0]
    widths = [weight.shape[1] for weight in weights]
    lefts = [sum(lane_tiles(width) for width in widths[:w]) for w in range(len(weights))]
    width = sum(lane_tiles(width) for width in widths)
    if width == sum(widths):
        buffer_of, offsets = [0] * len(weights), lefts
        products = [(0, width)]
    else:
        buffer_of, offsets = list(range(len(weights))), [0] * len(weights)
        products = list(zip(lefts, widths))
    blocks = []
    at = first
    while at < last:
        depth = min(4 * DEPTH_BLOCK if blocks else 2 * DEPTH_BLOCK, last - at)
        blocks.append((at, depth))
        at += depth

    def kernel(rows_ref, *refs):
        sources = refs[: len(weights)]
        arrived = refs[-1]
        buffers = refs[-1 - len(products) : -1]
        out = refs[-2 - len(products)]
        copies = []
        for b, (at, depth) in enumerate(blocks):
            copies.append([])
            half = depth // 2
            for p in range(2):
                for w, source in enumerate(sources):
                    top = at - first + p * half
                    copy = pltpu.make_async_copy(
                        source.at[at + p * half : at + (p + 1) * half, :],
                        buffers[buffer_of[w]].at[
                            top : top + half, offsets[w] : offsets[w] + widths[w]
                        ],
                        arrived.at[b, 2 * w + p],
                    )
                    copy.start()
                    copies[-1].append(copy)
        for (at, depth), group in zip(blocks, copies):
            for copy in group:
                copy.wait()
            for (left, wide), buffer in zip(products, buffers):
                columns = slice(left, left + wide)
                product = jnp.dot(
                    rows_ref[:, at : at + depth],
                    buffer[at - first : at - first + depth, :],
                    preferred_element_type=jnp.float32,
                )
                if at > first:
                    product = out[:, columns] + product
                elif before is not None:
                    product = refs[len(weights)][:, columns] + product
                out[:, columns] = product

    return pl.pallas_call(
        kernel,
        out_shape=jax.ShapeDtypeStruct((batch_rows, width), jnp.float32),
        in_specs=[whole()]
        + [whole(pltpu.HBM)] * len(weights)
        + [whole()] * (before is not None)
        + [whole(pl.ANY)] * len(ordered),
        out_specs=whole(),
        scratch_shapes=[pltpu.VMEM((last - first, wide), rows.dtype) for _, wide in products]
        + [pltpu.SemaphoreType.DMA((len(blocks), 2 * len(weights)))],
        compiler_params=pltpu.CompilerParams(vmem_limit_bytes=STREAM_LIMIT),
        cost_estimate=pl.CostEstimate(
            flops=2 * batch_rows * (last - first) * width,
            bytes_accessed=STREAM_COST * (last - first) * width,
            transcendentals=0,
        ),
        name="stream_rows",
    )(rows, *weights, *([] if before is None else [before]), *ordered)


def hidden_kernel(coeff, recv, from_place, hot, expand, mixed, out, spread):
    rank_limit = coeff.shape[1]
    own = jnp.dot(
        from_place[...], coeff[...] + recv[...], preferred_element_type=jnp.float32
    ).astype(jnp.bfloat16)
    pair = jnp.concatenate([own, own], axis=1)
    for p in range(spread.shape[1] // (2 * rank_limit)):
        at = slice(p * 2 * rank_limit, (p + 1) * 2 * rank_limit)
        spread[:, at] = hot[:, at] * pair
    lora = jnp.dot(spread[...], expand[...], preferred_element_type=jnp.float32)
    width = out.shape[1]
    value = mixed[:, :width]
    total = mixed[:, lane_tiles(width) : lane_tiles(width) + width] + lora
    out[...] = (value / (1.0 + jnp.exp(-value)) * total).astype(jnp.bfloat16)


def hidden_rows(mixed, coeff, recv, expand_factors, from_place, hot):
    adapters, rank_limit, width = expand_factors.shape
    batch_rows = mixed.shape[0]
    expand = expand_factors.reshape(adapters * rank_limit, width)
    return call(
        hidden_kernel,
        jax.ShapeDtypeStruct((batch_rows, width), jnp.bfloat16),
        [coeff, recv, from_place, hot, expand, mixed],
        "hidden_rows",
        scratch_shapes=[pltpu.VMEM((batch_rows, adapters * rank_limit), jnp.bfloat16)],
        cost_estimate=pl.CostEstimate(
            flops=2 * batch_rows * adapters * rank_limit * width,
            bytes_accessed=2 * adapters * rank_limit * width,
            transcendentals=batch_rows * width,
        ),
    )


def add_blocks(sides, own_rows, ordered):
    operands, shapes = [], []
    for mine, theirs, _, arrived in sides:
        operands += [mine, theirs] + ([] if arrived is None else [arrived])
        shapes.append(jax.ShapeDtypeStruct((own_rows, mine.shape[1]), jnp.bfloat16))

    def kernel(*refs):
        refs = list(refs)
        outs = refs[-len(sides) :]
        for (_, _, index, arrived), out in zip(sides, outs):
            at = slice(index * own_rows, (index + 1) * own_rows)
            total = refs.pop(0)[at, :].astype(jnp.float32)
            total = total + refs.pop(0)[at, :].astype(jnp.float32)
            if arrived is not None:
                total = total + refs.pop(0)[...].astype(jnp.float32)
            out[...] = total.astype(jnp.bfloat16)

    return call(kernel, tuple(shapes), operands, "add_blocks", ordered)


def scatter_rows(mine, theirs, own_rows, size):
    chips = size // 2
    last = chips // 2
    right, left = [None] * HALVES, [None] * HALVES
    ordered = []
    for turn in range(last):
        chains = [(right, 1, 0), (left, -1, 1), (right, 1, 1), (left, -1, 0)]
        if turn == 0:
            chains = [chains[0], chains[3], chains[2], chains[1]]
        groups = [[chain] for chain in chains] if turn < last - 1 else [chains[:2]]
        for group in groups:
            sides = []
            for chain, by, h in group:
                longer = (by == 1) == (h == 0)
                steps = last - turn - (not longer)
                index = min(2 * steps, chips - 1) if by == 1 else 2 * steps - 1
                sides.append((mine[h], theirs[h], index, chain[h]))
            sums = add_blocks(sides, own_rows, ordered)
            ordered = [sums[0]]
            for (chain, by, h), value in zip(group, sums):
                chain[h] = lax.ppermute(value, AXIS, ring(size, by))
    return list(zip(mine, theirs, right, left))


def finish_rows(halves, activations, gain, own_rows):
    width = activations.shape[1] // HALVES

    def kernel(*refs):
        refs, (act, gain_ref, block_out, normed, stream) = refs[:-5], refs[-5:]
        square = jnp.zeros((own_rows, 1), jnp.float32)
        for h in range(HALVES):
            mine, theirs, right, left = refs[4 * h : 4 * h + 4]
            at = slice(h * width, (h + 1) * width)
            total = act[:, at].astype(jnp.float32)
            for ref in (mine, theirs):
                total = total + ref[:own_rows, :].astype(jnp.float32)
            for ref in (right, left):
                total = total + ref[...].astype(jnp.float32)
            stream[:, at] = total
            block_out[:, at] = total.astype(jnp.bfloat16)
            square = square + jnp.sum(total * total, axis=1, keepdims=True)
        scale = lax.rsqrt(square * (1.0 / act.shape[1]) + 1e-05)
        normed[...] = (stream[...] * scale * gain_ref[...].astype(jnp.float32)).astype(
            jnp.bfloat16
        )

    out = jax.ShapeDtypeStruct(activations.shape, jnp.bfloat16)
    return call(
        kernel,
        (out, out),
        [array for half in halves for array in half] + [activations, gain],
        "finish_rows",
        scratch_shapes=[pltpu.VMEM(activations.shape, jnp.float32)],
    )


def body(
    activations,
    gate_weight,
    up_weight,
    down_weight,
    norm_gain_vector,
    shrink_factors,
    expand_factors,
    adapter_ranks,
    adapter_storage_slot,
    segment_start,
    segment_adapter,
):
    size = lax.axis_size(AXIS)
    own_rows, model_width = activations.shape
    assert size & (size - 1) == 0 and own_rows & (own_rows - 1) == 0
    tables = (segment_start, segment_adapter, adapter_ranks, adapter_storage_slot)
    scale, to_place, from_place, hot, factor = row_masks(
        tables, shrink_factors, own_rows, size
    )

    parts, loads = gather_rows(activations, size, (gate_weight, up_weight), [scale])
    rows, coeff = shrink_rows(parts, factor, scale, to_place, shrink_factors.shape[2])

    bits = [1 << b for b in range(size.bit_length() - 1)]
    mixed = None
    for step, bit in enumerate(bits):
        received = lax.ppermute(coeff, AXIS, flip(size, bit))
        part = step - (len(bits) - LOADS - 1)
        if part == LOADS:
            cuts = depth_cuts(model_width)
            mixed = stream_rows(
                rows, (gate_weight, up_weight), mixed, cuts[part], cuts[part + 1], [coeff]
            )
        elif part >= 0:
            mixed = mixed_rows(rows, loads[part], part, mixed, [coeff])
        if bit < bits[-1]:
            coeff = add_coefficients(coeff, received, [] if mixed is None else [mixed])
    hidden = hidden_rows(mixed, coeff, received, expand_factors, from_place, hot)

    half = size * own_rows // 2
    width = model_width // HALVES
    mine, theirs = [None] * HALVES, [None] * HALVES
    for h in range(HALVES):
        term = jnp.dot(
            hidden,
            down_weight[:, h * width : (h + 1) * width],
            preferred_element_type=jnp.float32,
        ).astype(jnp.bfloat16)
        mine[h] = term
        theirs[h] = lax.ppermute(term[half:], AXIS, flip(size, 1))
    halves = scatter_rows(mine, theirs, own_rows, size)
    return finish_rows(halves, activations, norm_gain_vector[None], own_rows)


def solution(mesh):
    return jax.shard_map(
        body,
        mesh=mesh,
        in_specs=(
            P(("groups", "mp"), None),
            P(None, "mp"),
            P(None, "mp"),
            P("mp", None),
            P(),
            P("mp", None, None),
            P(None, None, "mp"),
            P(),
            P(),
            P("groups"),
            P("groups"),
        ),
        out_specs=(P(("groups", "mp"), None), P(("groups", "mp"), None)),
        check_vma=False,
    )
```
